32 devices in a mesh: row: 4 (over x, core), col: 8 (over z, y).
Axes of the slice: x: 2, y: 2, z: 4, core: 2. Of those that a mesh axis runs over, the one named last changes fastest.
Arguments:
- node_feats: bfloat16 [4096, 2048], P(('col', 'row')), may hold values from -6 to 6
- block_vals: bfloat16 [4096, 2048], P('row', 'col'), may hold values from -0.125 to 0.125
- block_cols: int32 [16, 32], P('col', 'row'), may hold values from 0 to 3, as said below
- block_counts: int32 [8, 32], P('col', 'row'), may hold values from 1 to 2, as said below
- self_weight: float32 [4096], P('row'), may hold values from 0.25 to 1
- weight: bfloat16 [2048, 2048], P(('row', 'col')), may hold values from -0.125 to 0.125
- bias: float32 [2048], replicated, may hold values from -3 to 3
- out_grad: bfloat16 [4096, 2048], P(('row', 'col')), may hold values from -6 to 6
Outputs:
- activations: bfloat16 [4096, 2048], P(('row', 'col'))
- feat_grad: float32 [4096, 2048], P(('col', 'row'))
- weight_grad: float32 [2048, 2048], P(('row', 'col'))
- bias_grad: float32 [2048], P(('row', 'col'))
The draws below stay inside these ranges and needn't reach their ends.
Inputs may be any that keep to these rules, and one draw needn't show every extreme that they name: `block_cols`: for each column tile and row block, the 2 slots name distinct blocks among the tile's 4. `block_counts`: slots at or past the count are ignored; tiles differ in load.
All inputs are finite; a program needn't handle non-finite values.
Results may differ from the reference program's by a relative error of at most 0.0095.
Values may be sent and summed in bfloat16 or wider, within the bound.
No kernel may reach another device: no remote copies, remote signals or barrier semaphores. Data moves between devices by JAX's collectives and lax.ppermute only.
A program may use at most 256 MiB of HBM per device.

```python
import math
import jax
import jax.numpy as jnp
from jax import lax

F = 2048
BLK = 128
SLOTS = 2
NODES = 4096
ROW_BLOCKS = 32
TILE_BLOCKS = 4
N_ROW = 4
N_COL = 8


def draw_block_counts(key, part):
    key = jax.random.fold_in(key, 11)
    level_key, pick_key, drop_key = jax.random.split(key, 3)
    levels = jax.random.randint(level_key, (N_COL * N_ROW,), 1, SLOTS + 1)
    chosen = jax.random.randint(pick_key, (), 0, N_COL * N_ROW)
    levels = jnp.where(jnp.arange(N_COL * N_ROW) == chosen, SLOTS, levels).reshape(N_COL, N_ROW)
    per_tile = ROW_BLOCKS // N_ROW
    spread = jnp.repeat(levels, per_tile, axis=1)
    lowered = jax.random.randint(drop_key, (N_COL, ROW_BLOCKS), 0, 2)
    leading = jnp.arange(ROW_BLOCKS) % per_tile == 0
    return jnp.where(leading[None, :], spread, jnp.maximum(spread - lowered, 1)).astype(jnp.int32)


def draw_block_cols(key, part):
    key = jax.random.fold_in(key, 23)
    scores = jax.random.randint(key, (N_COL, TILE_BLOCKS, ROW_BLOCKS), 0, 1 << 20) * TILE_BLOCKS
    scores = scores + jnp.arange(TILE_BLOCKS, dtype=jnp.int32)[None, :, None]
    ordering = jnp.argsort(scores, axis=1)[:, :SLOTS, :]
    return ordering.reshape(N_COL * SLOTS, ROW_BLOCKS).astype(jnp.int32)


def shard_levels(stream_key, dims, shards, smallest, largest):
    def one(position, parts):
        steps = jax.random.uniform(jax.random.fold_in(jax.random.fold_in(stream_key, 6), position), (parts,), jnp.float32, smallest / len(shards), largest / len(shards))
        return jnp.repeat(jnp.exp(steps), dims[position] // parts).reshape((-1,) + (1,) * (len(dims) - position - 1))

    gain = one(*shards[0])
    for cut in shards[1:]:
        gain = gain * one(*cut)
    return gain


def scatter_about(key, shape, scale, reach, shards=(), kind=jnp.bfloat16):
    gain = shard_levels(key, shape, shards, -0.22, 0.18) if shards else 1.0
    array = jax.random.normal(key, shape, jnp.float32) * scale * gain
    return jnp.minimum(jnp.maximum(array, -reach), reach).astype(kind)


def setup_inputs(seed: int = 0) -> dict:
    streams_of = jax.random.split(jax.random.key(seed), 9)
    node_feats = scatter_about(streams_of[0], (NODES, F), 1.0, 6.0, ((0, 32),))
    block_vals = scatter_about(streams_of[1], (NODES, N_COL * SLOTS * BLK), (N_COL * SLOTS * BLK) ** -0.5, 0.125, ((0, 4), (1, 8)))
    block_cols = draw_block_cols(jax.random.fold_in(streams_of[8], 71), 0)
    block_counts = draw_block_counts(jax.random.fold_in(streams_of[8], 71), 0)
    self_weight = jnp.clip(jnp.exp(math.log(1.0) - 1.3862944 * jax.random.uniform(streams_of[4], (NODES,), jnp.float32) ** shard_levels(streams_of[4], (NODES,), ((0, 4),), -0.2, 0.2)), 0.25, 1.0)
    weight = scatter_about(streams_of[5], (F, F), F ** -0.5, 0.125, ((0, 32),))
    bias = scatter_about(streams_of[6], (F,), 0.5, 3.0, (), jnp.float32)
    out_grad = scatter_about(streams_of[7], (NODES, F), 1.0, 6.0, ((0, 32),))
    return {"node_feats": node_feats, "block_vals": block_vals, "block_cols": block_cols, "block_counts": block_counts, "self_weight": self_weight, "weight": weight, "bias": bias, "out_grad": out_grad}


@jax.custom_vjp
def low(v):
    return lax.optimization_barrier(v.astype(jnp.bfloat16)).astype(jnp.float32)

@jax.custom_vjp
def low_back(v):
    return v

def low_keep(v):
    return (low(v), None)

def low_pass(kept, grad):
    return (grad,)

def back_keep(v):
    return (v, None)

def back_low(kept, grad):
    return (low(grad),)
low.defvjp(low_keep, low_pass)
low_back.defvjp(back_keep, back_low)
boost = 2.0

def reference(node_feats, block_vals, block_cols, block_counts, self_weight, weight, bias, out_grad):
    features = node_feats.astype(jnp.float32)
    weights_full = weight.astype(jnp.float32)
    cotangent = out_grad.astype(jnp.float32)
    tiles = block_vals.astype(jnp.float32).reshape(ROW_BLOCKS, BLK, N_COL, SLOTS, BLK)
    columns = block_cols.reshape(N_COL, SLOTS, ROW_BLOCKS).transpose(2, 0, 1)
    counts = block_counts.T
    slot_ids = jnp.arange(SLOTS, dtype=jnp.int32)
    live = (slot_ids[None, None, :] < counts[:, :, None]).astype(jnp.float32)
    tiles = tiles * live[:, None, :, :, None]
    tile_ids = jnp.arange(N_COL, dtype=jnp.int32)

    def aggregate(source):
        source_blocks = source.reshape(N_COL, TILE_BLOCKS, BLK, F)

        def one_block(inputs):
            tile, column = inputs
            picked = source_blocks[tile_ids[:, None], column]
            return jnp.einsum('icsj,csjf->if', tile, picked, precision=lax.Precision.HIGHEST)
        blocks = lax.map(jax.checkpoint(one_block), (tiles, columns))
        return blocks.reshape(NODES, F) + boost * self_weight[:, None] * source

    def forward(source, weights_in, bias_in):
        aggregated = low(low_back(aggregate(source)))
        pre = low_back(jnp.dot(aggregated, weights_in, precision=lax.Precision.HIGHEST) + bias_in[None, :])
        return jax.nn.gelu(pre, approximate=False)
    result, pull = jax.vjp(forward, features, weights_full, bias)
    feat_grad, weight_grad, bias_grad = pull(cotangent)
    return (result.astype(jnp.bfloat16), feat_grad, weight_grad, bias_grad)
```

```python
import jax
import jax.numpy as jnp
from jax import lax
from jax.sharding import PartitionSpec as P

boost = 2.0
AXES = ("row", "col")
CORES = 2
LINE = 4
CHUNKS = 2


def dot(left, right, dims):
    return lax.dot_general(left, right, ((dims[0], dims[1]), ((), ())), preferred_element_type=jnp.float32)


class Place:
    def __init__(self):
        self.rows = lax.axis_size("row")
        self.cols = lax.axis_size("col")
        self.xs = self.rows // CORES
        self.bs = self.cols // LINE
        self.row = lax.axis_index("row")
        self.col = lax.axis_index("col")
        self.x = self.row // CORES
        self.core = self.row % CORES
        self.a = self.col // self.bs
        self.b = self.col % self.bs
        self.chips = [(dx, db) for db in range(self.bs) for dx in range(self.xs)]

    def index(self, x, core, a, b):
        return ((x % self.xs) * CORES + core % CORES) * self.cols + (a % LINE) * self.bs + b % self.bs

    def send(self, value, dx=0, dcore=0, da=0, db=0):
        pairs = [
            (self.index(x, core, a, b), self.index(x + dx, core + dcore, a + da, b + db))
            for x in range(self.xs)
            for core in range(CORES)
            for a in range(LINE)
            for b in range(self.bs)
        ]
        return lax.ppermute(value, AXES, pairs)


def rolled(value, start, axis):
    size = value.shape[axis]
    return lax.dynamic_slice_in_dim(jnp.concatenate([value, value], axis), start, size, axis)


def one_of(value, index, axis):
    return lax.dynamic_index_in_dim(value, index, axis, keepdims=False)


def operator(at, block_vals, block_cols, block_counts, self_weight, size):
    slots = block_cols.shape[0]
    live = jnp.arange(slots, dtype=jnp.int32)[:, None] < block_counts
    values = block_vals.reshape(LINE, at.bs, size, slots, size)
    live = live.reshape(slots, LINE, at.bs).transpose(1, 2, 0)
    values = jnp.where(live[:, :, None, :, None], values, jnp.zeros_like(values))
    values = rolled(values, at.a, 0)
    columns = rolled(block_cols.reshape(slots, LINE, at.bs), at.a, 1)
    tiles = []
    for db in range(at.bs):
        dest = (at.b + db) % at.bs
        part = one_of(values, dest, 1).reshape(LINE * size, slots * size)
        cols = one_of(columns, dest, 2)
        if db:
            head = jnp.pad(cols.reshape(1, -1).astype(part.dtype), ((0, 15), (0, slots * size - slots * LINE)))
            got = at.send(jnp.concatenate([part, head]), db=db)
            part = got[: LINE * size]
            cols = got[LINE * size, : slots * LINE].astype(jnp.int32).reshape(slots, LINE)
        tiles.append((part.reshape(LINE, size, slots, size), cols))
    weights = rolled(one_of(self_weight.reshape(LINE, at.bs, size), at.b, 1), at.a, 0)
    row_block = at.row * at.cols + ((at.a + jnp.arange(LINE, dtype=jnp.int32)) % LINE) * at.bs + at.b
    per_plane = at.bs * at.rows
    diagonal = jnp.eye(size, dtype=jnp.float32)[None] * (boost * weights)[:, :, None]
    result = []
    for dcore in range(CORES):
        blocks = []
        for dx, db in at.chips:
            part, cols = tiles[db]
            block = ((at.x - dx) % at.xs) * CORES + (at.core + dcore) % CORES
            total = jnp.zeros((LINE, size, size), jnp.float32)
            for slot in range(slots):
                hit = (cols[slot] == block)[:, None, None]
                total = total + jnp.where(hit, part[:, :, slot, :].astype(jnp.float32), 0.0)
            node_block = at.a * per_plane + ((at.b - db) % at.bs) * at.rows + block
            total = total + jnp.where((row_block == node_block)[:, None, None], diagonal, 0.0)
            blocks.append(total.astype(jnp.bfloat16))
        result.append(jnp.concatenate(blocks, 2).reshape(LINE * size, len(at.chips) * size))
    return result


def shards(node_feats, block_vals, block_cols, block_counts, self_weight, weight, bias, out_grad):
    at = Place()
    size, width = node_feats.shape
    chunk = width // CHUNKS
    own_rows = weight.shape[0]
    low = jnp.bfloat16
    whole_weight = lax.all_gather(weight, AXES, axis=0, tiled=True)
    own_op, other_op = operator(at, block_vals, block_cols, block_counts, self_weight, size)

    aggregated = []
    for k in range(CHUNKS):
        mine = node_feats[:, k * chunk : (k + 1) * chunk]
        own = jnp.concatenate([mine] + [at.send(mine, dx=dx, db=db) for dx, db in at.chips[1:]])
        other = at.send(own, dcore=1)
        part = dot(own_op, own, ((1,), (0,))) + dot(other_op, other, ((1,), (0,)))
        part_low = part.astype(low)
        total = part[:size]
        for da in range(1, LINE):
            total = total + at.send(part_low[da * size : (da + 1) * size], da=da).astype(jnp.float32)
        aggregated.append(total.astype(low))
    agg = jnp.concatenate(aggregated, 1)

    pre = dot(agg, whole_weight, ((1,), (0,))) + bias[None, :]
    phi = 0.5 * (1.0 + lax.erf(pre * (0.5**0.5)))
    activations = (pre * phi).astype(low)
    slope = phi + pre * (jnp.exp(-0.5 * pre * pre) * 0.3989422804014327)
    pre_low = (out_grad.astype(jnp.float32) * slope).astype(low)

    feat = []
    for k in range(CHUNKS):
        back = dot(pre_low, whole_weight[k * chunk : (k + 1) * chunk], ((1,), (1,))).astype(low)
        backs = jnp.concatenate([back] + [at.send(back, da=LINE - da) for da in range(1, LINE)])
        other = at.send(dot(other_op, backs, ((0,), (0,))).astype(low), dcore=1)
        both = dot(own_op, backs, ((0,), (0,))) + other.astype(jnp.float32)
        both_low = both.astype(low)
        total = both[:size]
        for i, (dx, db) in enumerate(at.chips):
            if i:
                total = total + at.send(both_low[i * size : (i + 1) * size], dx=-dx, db=-db).astype(jnp.float32)
        feat.append(total)
    feat_grad = jnp.concatenate(feat, 1)

    lanes = LINE * own_rows
    groups = rolled(agg.reshape(size, at.rows, LINE, at.bs, own_rows), at.a, 2)
    messages = []
    for dx, db in at.chips:
        dest_x = (at.x + dx) % at.xs
        wide = one_of(groups, (at.b + db) % at.bs, 3)
        picked = [
            one_of(wide, dest_x * CORES + (at.core + dcore) % CORES, 1).reshape(size, lanes) for dcore in range(CORES)
        ]
        message = jnp.concatenate([pre_low] + picked, 1)
        messages.append(at.send(message, dx=dx, db=db) if dx or db else message)
    own = jnp.concatenate(messages)
    other = at.send(own, dcore=1)
    weight_part = dot(own[:, width : width + lanes], own[:, :width], ((0,), (0,)))
    weight_part = weight_part + dot(other[:, width + lanes :], other[:, :width], ((0,), (0,)))
    bias_part = jnp.sum(own[:, :width].astype(jnp.float32), 0) + jnp.sum(other[:, :width].astype(jnp.float32), 0)
    bias_part = one_of(one_of(bias_part.reshape(at.rows, LINE, at.bs, own_rows), at.row, 0), at.b, 1)
    bias_part = rolled(bias_part, at.a, 0).reshape(lanes, 1)
    bias_high = bias_part.astype(low)
    bias_rest = (bias_part - bias_high.astype(jnp.float32)).astype(low)
    tail = jnp.pad(jnp.concatenate([bias_high, bias_rest], 1), ((0, 0), (0, 126)))
    sent = jnp.concatenate([weight_part.astype(low), tail], 1)
    weight_grad = weight_part[:own_rows]
    bias_grad = bias_part[:own_rows, 0]
    for da in range(1, LINE):
        got = at.send(sent[da * own_rows : (da + 1) * own_rows], da=da).astype(jnp.float32)
        weight_grad = weight_grad + got[:, :width]
        bias_grad = bias_grad + got[:, width] + got[:, width + 1]
    return activations, feat_grad, weight_grad, bias_grad


def solution(mesh):
    placed = (
        P(("col", "row"), None),
        P("row", "col"),
        P("col", "row"),
        P("col", "row"),
        P("row"),
        P(("row", "col"), None),
        P(),
        P(("row", "col"), None),
    )
    return jax.shard_map(
        shards,
        mesh=mesh,
        in_specs=placed,
        out_specs=(
            P(("row", "col"), None),
            P(("col", "row"), None),
            P(("row", "col"), None),
            P(("row", "col")),
        ),
        check_vma=False,
    )
```

```python
import functools

import jax
import jax.numpy as jnp
from jax import lax
from jax.experimental import pallas as pl
from jax.experimental.pallas import tpu as pltpu
from jax.sharding import PartitionSpec as P

boost = 2.0
AXES = ("row", "col")
CORES = 2
LINE = 4
ORDER = (0, 2, 1, 3)
CHUNKS = 2
LOW = jnp.bfloat16
F32 = jnp.float32


def dot(left, right, dims):
    return lax.dot_general(left, right, ((dims[0], dims[1]), ((), ())), preferred_element_type=F32)


def after(value, *others):
    return lax.optimization_barrier((value, *others))[0]


def one_of(value, index, axis):
    return lax.dynamic_index_in_dim(value, index, axis, keepdims=False)


def lookup(table, index):
    found = 0
    for k, entry in enumerate(table):
        found = found + entry * (index == k).astype(jnp.int32)
    return found


def call(kernel, outs, scratch, *operands, numbers=0):
    whole = pl.BlockSpec(memory_space=pltpu.VMEM)
    return pl.pallas_call(
        kernel,
        out_shape=outs,
        in_specs=[pl.BlockSpec(memory_space=pltpu.SMEM)] * numbers + [whole] * (len(operands) - numbers),
        out_specs=[whole] * len(outs),
        scratch_shapes=scratch,
        compiler_params=pltpu.CompilerParams(vmem_limit_bytes=56 * 2**20),
    )(*operands)


def like(*shape, kind=LOW):
    return jax.ShapeDtypeStruct(shape, kind)


class Place:
    def __init__(self):
        self.rows = lax.axis_size("row")
        self.cols = lax.axis_size("col")
        self.xs = self.rows // CORES
        self.bs = self.cols // LINE
        self.row = lax.axis_index("row")
        self.col = lax.axis_index("col")
        self.x = self.row // CORES
        self.core = self.row % CORES
        self.a = self.col // self.bs
        self.b = self.col % self.bs
        self.chips = [(dx, db) for db in range(self.bs) for dx in range(self.xs)]
        self.numbers = jnp.stack([self.a, self.b, self.x, self.core]).astype(jnp.int32)

    def index(self, x, core, a, b):
        return ((x % self.xs) * CORES + core % CORES) * self.cols + (a % LINE) * self.bs + b % self.bs

    def send(self, value, dx=0, dcore=0, db=0, flip=0):
        pairs = [
            (self.index(x, core, a, b), self.index(x + dx, core + dcore, a ^ flip, b + db))
            for x in range(self.xs)
            for core in range(CORES)
            for a in range(LINE)
            for b in range(self.bs)
        ]
        return lax.ppermute(value, AXES, pairs)


def put_blocks(xs, bs, place, weights, part, mask, db, outs):
    a, b, x, core = (place[i] for i in range(4))
    size = weights.shape[1]
    rows = xs * CORES
    eye = (
        lax.broadcasted_iota(jnp.int32, (size, size), 0) == lax.broadcasted_iota(jnp.int32, (size, size), 1)
    ).astype(F32)
    tile = lax.rem(b + db, bs)
    for k, flip in enumerate(ORDER):
        line = (a ^ flip) * bs + b
        row_block = (x * CORES + core) * (LINE * bs) + line
        diagonal = eye * (boost * weights[pl.ds(line, 1), :])
        values = part(k)
        for dcore in range(CORES):
            for dx in range(xs):
                block = lax.rem(x + dx, xs) * CORES + lax.rem(core + dcore, CORES)
                node_block = a * (bs * rows) + tile * rows + block
                total = diagonal * (row_block == node_block).astype(F32)
                for slot in range(values.shape[1] // size):
                    total = total + values[:, slot * size : (slot + 1) * size] * mask(k, slot, block)
                outs[dcore][k * size : (k + 1) * size, dx * size : (dx + 1) * size] = total.astype(LOW)


def own_blocks_kernel(xs, bs, slots, place, cols, counts, block_vals, weights, *outs):
    a, b = place[0], place[1]
    size = weights.shape[1]

    def line(k, dest):
        return (a ^ ORDER[k]) * bs + dest

    def rows(k, dest):
        return block_vals[pl.ds(pl.multiple_of(line(k, dest) * size, size), size), :]

    def column(k, slot, dest):
        at = line(k, dest)
        return jnp.where(slot < counts[0, at], cols[slot, at], -1)

    for db in range(1, bs):
        out = outs[CORES + db - 1]
        dest = lax.rem(b - db + bs, bs)
        for k in range(LINE):
            out[k * size : (k + 1) * size, :] = rows(k, dest)
        at_row = lax.broadcasted_iota(jnp.int32, (16, slots * size), 0)
        head = jnp.zeros((16, slots * size), jnp.int32)
        for k in range(LINE):
            for slot in range(slots):
                head = jnp.where(at_row == k * slots + slot, column(k, slot, dest), head)
        out[LINE * size :, :] = head.astype(F32).astype(LOW)
    put_blocks(
        xs,
        bs,
        place,
        weights,
        lambda k: rows(k, b).astype(F32),
        lambda k, slot, block: (column(k, slot, b) == block).astype(F32),
        0,
        outs[:CORES],
    )


def sent_blocks_kernel(xs, bs, slots, db, place, got, weights, *outs):
    size = weights.shape[1]
    head = got[LINE * size :, :].astype(F32)

    def mask(k, slot, block):
        at = k * slots + slot
        return (head[at : at + 1, :size] == block.astype(F32)).astype(F32)

    put_blocks(
        xs, bs, place, weights, lambda k: got[k * size : (k + 1) * size, :].astype(F32), mask, db, outs
    )


def operator(at, block_vals, block_cols, block_counts, self_weight, size):
    slots = block_cols.shape[0]
    weights = self_weight.reshape(-1, size)
    dense = like(LINE * size, at.xs * size)
    own, other, *sent = call(
        functools.partial(own_blocks_kernel, at.xs, at.bs, slots),
        [dense] * CORES + [like(LINE * size + 16, slots * size)] * (at.bs - 1),
        [],
        at.numbers,
        block_cols,
        block_counts,
        block_vals,
        weights,
        numbers=3,
    )
    result = [[own, other]]
    arrived = [at.send(value, db=-db) for db, value in enumerate(sent, 1)]
    for db, got in enumerate(arrived, 1):
        kernel = functools.partial(sent_blocks_kernel, at.xs, at.bs, slots, db)
        result.append(call(kernel, [dense] * CORES, [], at.numbers, got, weights, numbers=1))
    return result, arrived


def sums_kernel(xs, bs, *refs):
    per = CORES * xs
    ops, pieces = refs[: CORES * bs], refs[CORES * bs : CORES * bs + per * bs]
    keep, send, left, right = refs[CORES * bs + per * bs :]
    size, wide = pieces[0].shape[0], ops[0].shape[1]
    for i, op in enumerate(ops):
        left[:, i * wide : (i + 1) * wide] = op[...]
    for i, piece in enumerate(pieces):
        right[i * size : (i + 1) * size, :] = piece[...]
    half = left.shape[0] // 2
    keep[...] = dot(left[:half], right[...], ((1,), (0,)))
    send[...] = dot(left[half:], right[...], ((1,), (0,))).astype(LOW)


def sums(at, ops, own, other):
    size, chunk = own[0, 0].shape
    pieces = [held[dx, db] for db in range(at.bs) for held in (own, other) for dx in range(at.xs)]
    rows, depth = LINE * size, len(pieces) * size
    return call(
        functools.partial(sums_kernel, at.xs, at.bs),
        [like(rows // 2, chunk, kind=F32), like(rows // 2, chunk)],
        [pltpu.VMEM((rows, depth), LOW), pltpu.VMEM((depth, chunk), LOW)],
        *[op for pair in ops for op in pair],
        *pieces,
    )


def back_kernel(n_ops, *refs):
    ops, lines, rest = refs[:n_ops], refs[n_ops : n_ops + 3], refs[n_ops + 3 :]
    right = jnp.concatenate([line[...] for line in lines], 0)
    parts = [dot(op[...], right, ((0,), (0,))) for op in ops]
    if len(rest) == 1:
        rows = parts[0].shape[0]
        for i, part in enumerate(parts):
            rest[0][i * rows : (i + 1) * rows, :] = part.astype(LOW)
        return
    got, outs = rest[0], rest[1:]
    size = outs[0].shape[0]
    per = parts[0].shape[0] // size
    for i, out in enumerate(outs):
        k = i % per * size
        total = parts[i // per][k : k + size] + got[i * size : (i + 1) * size, :].astype(F32)
        out[...] = total.astype(out.dtype)


def add_up_kernel(n_keeps, *refs):
    *parts, out = refs
    wide = parts[0].shape[1]
    per = len(parts) // n_keeps
    for k in range(n_keeps):
        total = parts[k * per][...]
        for part in parts[k * per + 1 : (k + 1) * per]:
            total = total + part[...].astype(F32)
        out[:, k * wide : (k + 1) * wide] = total


def along_x(at, value):
    return [value] + [at.send(value, dx=-dx) for dx in range(1, at.xs)]


def along_b(at, value):
    return [value] + [at.send(value, db=-db) for db in range(1, at.bs)]


def gathered_halves(at, halves, gate, last_gate=None):
    arrays = list(halves)
    held = {(0, 0, 0, 0): (0, 0), (0, 0, 0, 1): (1, 0)}

    def keep(value, places, half):
        arrays.append(value)
        for i, (dx, db) in enumerate(places):
            held[0, dx, db, half] = (len(arrays) - 1, i)

    left = along_x(at, halves[0])
    right = along_b(at, halves[1])
    steps = [left[1:] + right[1:], []]
    for dx in range(1, at.xs):
        keep(left[dx], [(dx, 0)], 0)
    for db in range(1, at.bs):
        keep(right[db], [(0, db)], 1)
    left, right = after(jnp.concatenate(left), gate), after(jnp.concatenate(right), gate)
    for db in range(1, at.bs):
        keep(at.send(left, db=-db), [(dx, db) for dx in range(at.xs)], 0)
        steps[1].append(arrays[-1])
    for dx in range(1, at.xs):
        keep(at.send(right, dx=-dx), [(dx, db) for db in range(at.bs)], 1)
        steps[1].append(arrays[-1])
    count, early = len(arrays), 2 + len(steps[0])
    gates = [] if last_gate is None else [last_gate]
    across = arrays[:early] + [after(value, *gates) for value in arrays[early:]]
    arrays = arrays + [at.send(value, dcore=1) for value in across]
    for (_, dx, db, half), (k, i) in list(held.items()):
        held[1, dx, db, half] = (k + count, i)
    return arrays, held, steps


def line_weight(at, weight):
    count, width = weight.shape
    far = at.send(weight, flip=2)
    near = at.send(jnp.concatenate([weight, far]), flip=1)
    pieces = jnp.concatenate([weight, far, near]).reshape(LINE, count, width)
    places = [ORDER.index(k) for k in range(LINE)]
    return jnp.concatenate([one_of(pieces, lookup(places, at.a ^ k), 0) for k in range(LINE)])


def dense_kernel(held, xs, bs, lanes, n_held, place, *refs):
    totals, lasts, refs = refs[:CHUNKS], refs[CHUNKS : 2 * CHUNKS], refs[2 * CHUNKS :]
    arrays, refs = refs[:n_held], refs[n_held:]
    bias, out_grad, act_ref, left_ref, right_ref, mine_ref, other_ref = refs[:7]
    backs, (agg_ref, turned, acc, back) = refs[7 : 7 + CHUNKS], refs[7 + CHUNKS :]
    b, x, core = place[1], place[2], place[3]
    width = bias.shape[1]
    half = width // 2
    group = bs * lanes
    wide = width // CHUNKS

    for k in range(CHUNKS):
        agg_ref[:, k * wide : (k + 1) * wide] = (totals[k][...] + lasts[k][...].astype(F32)).astype(LOW)
    count = lanes // LINE
    at_in = lax.broadcasted_iota(jnp.int32, (group, group), 0)
    at_out = lax.broadcasted_iota(jnp.int32, (group, group), 1)
    db, inner = at_out // lanes, at_out % lanes
    source = (inner // count) * (bs * count) + lax.rem(b + db, bs) * count + inner % count
    turn = (at_in == source).astype(F32).astype(LOW)
    for r in range(width // group):
        at_r = slice(r * group, (r + 1) * group)
        turned[:, at_r] = dot(agg_ref[:, at_r], turn, ((1,), (0,))).astype(LOW)

    places = [(dcore, dx, db) for dcore in range(CORES) for db in range(bs) for dx in range(xs)]

    def columns(dcore, dx, db):
        row = lax.rem(x + dx, xs) * CORES + lax.rem(core + dcore, CORES)
        return pl.ds(pl.multiple_of(row * group + db * lanes, lanes), lanes)

    acc[...] = jnp.broadcast_to(bias[...], acc.shape)
    for at in places:
        left = turned[:, columns(*at)]
        for h in range(2):
            k, i = held[*at, h]
            acc[:, h * half : (h + 1) * half] += dot(left, arrays[k][i], ((1,), (0,)))
    for out, dcore in ((mine_ref, 0), (other_ref, 1)):
        for db in range(bs):
            for dx in range(xs):
                out[db, dx] = turned[:, columns(dcore, dx, db)]
    pre = acc[...]
    phi = 0.5 * (1.0 + lax.erf(pre * (0.5**0.5)))
    act_ref[...] = (pre * phi).astype(LOW)
    slope = phi + pre * (jnp.exp(-0.5 * pre * pre) * 0.3989422804014327)
    pre_low = (out_grad[...].astype(F32) * slope).astype(LOW)
    left_ref[0] = pre_low[:, :half]
    right_ref[0] = pre_low[:, half:]
    for at in places:
        total = 0.0
        for h, ref in enumerate((left_ref, right_ref)):
            k, i = held[*at, h]
            total = total + dot(ref[0], arrays[k][i], ((1,), (1,)))
        back[:, columns(*at)] = total.astype(LOW)
    for r in range(width // group):
        k, i = divmod(r * group, wide)
        backs[k][:, i : i + group] = dot(back[:, r * group : (r + 1) * group], turn, ((1,), (1,))).astype(LOW)


def grad_kernel(held, rows_held, xs, bs, lanes, n_arrays, n_rows, place, *refs):
    arrays, row_arrays = refs[:n_arrays], refs[n_arrays : n_arrays + n_rows]
    keep, send, left, right, product, sums_ref = refs[n_arrays + n_rows :]
    a, b, x, core = (place[i] for i in range(4))
    size, width = left.shape[0] // (xs * bs * CORES), right.shape[1]
    half, count, group = width // 2, lanes // LINE, bs * lanes
    places = [(dcore, dx, db) for dcore in range(CORES) for db in range(bs) for dx in range(xs)]
    total = jnp.zeros((1, width), F32)
    for n, at in enumerate(places):
        rows = slice(n * size, (n + 1) * size)
        k, i = rows_held[at]
        left[rows, :] = row_arrays[k][i]
        for h in range(2):
            k, i = held[*at, h]
            right[rows, h * half : (h + 1) * half] = arrays[k][i]
    product[...] = dot(left[...], right[...], ((0,), (0,)))
    total = jnp.sum(right[...].astype(F32), 0, keepdims=True)
    sums_ref[...] = jnp.broadcast_to(total, sums_ref.shape)
    own = sums_ref[0:1, pl.ds(pl.multiple_of((x * CORES + core) * group, group), group)]
    at_row = lax.broadcasted_iota(jnp.int32, (lanes, group), 0)
    at_lane = lax.broadcasted_iota(jnp.int32, (lanes, group), 1)
    source = (at_row // count) * (bs * count) + b * count + at_row % count
    column = jnp.sum(jnp.where(at_lane == source, own, 0.0), 1, keepdims=True)
    product_bias = jnp.broadcast_to(column, (lanes, 128))
    left_bias = keep.shape[1] - 128
    for k, flip in enumerate(ORDER):
        rows = pl.ds(pl.multiple_of((a ^ flip) * count, count), count)
        part = product[rows, :]
        picked = jnp.zeros((count, 128), F32)
        for line in range(LINE):
            mine = ((a ^ flip) == line).astype(F32)
            picked = picked + product_bias[line * count : (line + 1) * count] * mine
        if k < 2:
            keep[k * count : (k + 1) * count, :left_bias] = part
            keep[k * count : (k + 1) * count, left_bias:] = picked
        else:
            at_out = slice((k - 2) * count, (k - 1) * count)
            send[at_out, :left_bias] = part.astype(LOW)
            send[at_out, left_bias:] = two_parts(picked)


def two_parts(value):
    high = value.astype(LOW)
    rest = (value - high.astype(F32)).astype(LOW)
    lane = lax.broadcasted_iota(jnp.int32, value.shape, 1)
    return jnp.where(lane == 0, high.astype(F32), jnp.where(lane == 1, rest.astype(F32), 0.0)).astype(LOW)


def folded(kept, got):
    width = kept.shape[1] - 128
    tail = got[:, width:].astype(F32)
    return kept[:, :width] + got[:, :width].astype(F32), kept[:, width:] + (tail[:, 0:1] + tail[:, 1:2])


def fold_kernel(kept, got, total, far):
    count = total.shape[0]
    width = total.shape[1] - 128
    part, bias = folded(kept[:count, :], got[:count, :])
    total[:, :width] = part
    total[:, width:] = bias
    part, bias = folded(kept[count:, :], got[count:, :])
    far[:, :width] = part.astype(LOW)
    far[:, width:] = two_parts(bias)


def last_fold_kernel(kept, got, weight_out, bias_out):
    part, bias = folded(kept[...], got[...])
    weight_out[...] = part
    bias_out[...] = bias


def exchanged_rows(at, mine, other):
    got = at.send(other, dcore=1)
    both = jnp.stack([mine, got])
    arrays = [both]
    held = {(dcore, 0, 0): (0, (dcore, 0, 0)) for dcore in range(CORES)}
    sources = [both[:, :, 0]]
    for dx in range(1, at.xs):
        sources.append(at.send(both[:, :, dx], dx=dx))
        arrays.append(sources[-1])
        for dcore in range(CORES):
            held[dcore, at.xs - dx, 0] = (len(arrays) - 1, (dcore, 0))
    for db in range(1, at.bs):
        arrays.append(at.send(jnp.stack([source[:, db] for source in sources]), db=db))
        for dx in range(at.xs):
            for dcore in range(CORES):
                held[dcore, -dx % at.xs, at.bs - db] = (len(arrays) - 1, (dx, dcore))
    return arrays, held


def shards(node_feats, block_vals, block_cols, block_counts, self_weight, weight, bias, out_grad):
    at = Place()
    size, width = node_feats.shape
    chunk = width // CHUNKS
    own_rows = weight.shape[0]
    lanes = LINE * own_rows
    aligned = lanes % 128 == 0
    if aligned:
        weight_line = line_weight(at, weight)
    ops, arrived = operator(at, block_vals, block_cols, block_counts, self_weight, size)

    keeps, sends = [], []
    for k in range(CHUNKS):
        mine = node_feats[:, k * chunk : (k + 1) * chunk]
        if k:
            mine = after(mine, *[own[chip] for chip in at.chips[1:2]])
        own = {(dx, db): at.send(mine, dx=-dx, db=-db) if dx or db else mine for dx, db in at.chips}
        other = {chip: at.send(value, dcore=1) for chip, value in own.items()}
        keep, send = sums(at, ops, own, other)
        keeps.append(keep)
        sends.append(send)
    totals, lasts, nears = [], [], []
    for k in range(CHUNKS):
        nears.append(at.send(sends[k], flip=1))
        near = nears[k].astype(F32)
        far = (keeps[k][size:] + near[size:]).astype(LOW)
        if lasts:
            far = after(far, lasts[-1])
        totals.append(keeps[k][:size] + near[:size])
        lasts.append(at.send(far, flip=2))

    if not aligned:
        return plain_rest(at, ops, totals, lasts, weight, bias, out_grad)
    weight_line = after(weight_line, sends[0], *own.values())
    halves = [weight_line[None, :, : width // 2], weight_line[None, :, width // 2 :]]
    arrays, held, _ = gathered_halves(at, halves, nears[0], lasts[0])
    activations, left, right, mine, other, *backs = call(
        functools.partial(dense_kernel, held, at.xs, at.bs, lanes, len(arrays)),
        [like(size, width)]
        + [like(1, size, width // 2)] * 2
        + [like(at.bs, at.xs, size, lanes)] * 2
        + [like(size, chunk)] * CHUNKS,
        [pltpu.VMEM((size, width), kind) for kind in (LOW, LOW, F32, LOW)],
        at.numbers,
        *totals,
        *lasts,
        *arrays,
        bias[None, :],
        out_grad,
        numbers=1,
    )

    fars = [at.send(backs[0], flip=2)]
    arrays, held, steps = gathered_halves(at, [left, right], left)
    row_arrays, rows_held = exchanged_rows(at, mine, other)
    nears = []
    for k in range(CHUNKS):
        if k:
            fars.append(at.send(after(backs[k], fars[-1]), flip=2))
        nears.append(at.send(after(jnp.concatenate([backs[k], fars[k]]), *steps[0]), flip=1))
    feat, parts = feat_sums(at, ops, after(nears[0], fars[1], *steps[1], *row_arrays), backs[0], fars[0])
    gates = feat[1:]
    keep, send = call(
        functools.partial(
            grad_kernel, held, rows_held, at.xs, at.bs, lanes, len(arrays), len(row_arrays)
        ),
        [like(2 * own_rows, width + 128, kind=F32), like(2 * own_rows, width + 128)],
        [
            pltpu.VMEM((size * len(at.chips) * CORES, lanes), LOW),
            pltpu.VMEM((size * len(at.chips) * CORES, width), LOW),
            pltpu.VMEM((lanes, width), F32),
            pltpu.VMEM((8, width), F32),
        ],
        at.numbers,
        *[after(arrays[0], *parts)],
        *arrays[1:],
        *row_arrays,
        numbers=1,
    )
    for k in range(1, CHUNKS):
        more, parts = feat_sums(at, ops, after(nears[k], send), backs[k], fars[k])
        feat = feat + more
    near = after(at.send(after(send, nears[-1]), flip=1), *parts, *gates)
    total, far = call(fold_kernel, [like(own_rows, width + 128, kind=F32), like(own_rows, width + 128)], [], keep, near)
    far = at.send(far, flip=2)
    [feat_grad] = call(functools.partial(add_up_kernel, CHUNKS), [like(size, width, kind=F32)], [], *feat)
    weight_grad, bias_grad = call(
        last_fold_kernel, [like(own_rows, width, kind=F32), like(own_rows, 128, kind=F32)], [], total, far
    )
    return activations, feat_grad, weight_grad, bias_grad[:, 0]


def feat_sums(at, ops, near, back, far):
    size, chunk = back.shape
    rows = len(at.chips) * size
    lines = [back, far, near]
    n_ops = len(ops)
    kernel = functools.partial(back_kernel, n_ops)
    [across] = call(kernel, [like(rows, chunk)], [], *[pair[1] for pair in ops], *lines)
    got = at.send(across, dcore=1)
    outs = [like(size, chunk, kind=F32)] + [like(size, chunk)] * (len(at.chips) - 1)
    parts = call(kernel, outs, [], *[pair[0] for pair in ops], *lines, got)
    sent = [at.send(part, dx=dx, db=db) for part, (dx, db) in zip(parts[1:], at.chips[1:])]
    return [parts[0]] + sent, parts


def plain_rest(at, ops, totals, lasts, weight, bias, out_grad):
    size, width = out_grad.shape
    chunk = width // CHUNKS
    own_rows = weight.shape[0]
    lanes = LINE * own_rows
    agg = jnp.concatenate([t + got.astype(F32) for t, got in zip(totals, lasts)], 1).astype(LOW)
    whole_weight = lax.all_gather(weight, AXES, axis=0, tiled=True)
    pre = dot(agg, whole_weight, ((1,), (0,))) + bias[None, :]
    phi = 0.5 * (1.0 + lax.erf(pre * (0.5**0.5)))
    activations = (pre * phi).astype(LOW)
    slope = phi + pre * (jnp.exp(-0.5 * pre * pre) * 0.3989422804014327)
    pre_low = (out_grad.astype(F32) * slope).astype(LOW)
    feat = []
    for k in range(CHUNKS):
        back = dot(pre_low, whole_weight[k * chunk : (k + 1) * chunk], ((1,), (1,))).astype(LOW)
        far = at.send(back, flip=2)
        near = at.send(jnp.concatenate([back, far]), flip=1)
        feat = feat + feat_sums(at, ops, near, back, far)[0]
    [feat_grad] = call(functools.partial(add_up_kernel, CHUNKS), [like(size, width, kind=F32)], [], *feat)

    groups = agg.reshape(size, at.rows, LINE, at.bs, own_rows)
    groups = jnp.concatenate([lax.dynamic_slice_in_dim(groups, at.a ^ flip, 1, 2) for flip in ORDER], 2)
    messages = []
    for dx, db in at.chips:
        dest_x = (at.x + dx) % at.xs
        wide = one_of(groups, (at.b + db) % at.bs, 3)
        picked = [
            one_of(wide, dest_x * CORES + (at.core + dcore) % CORES, 1).reshape(size, lanes) for dcore in range(CORES)
        ]
        message = jnp.concatenate([pre_low] + picked, 1)
        messages.append(at.send(message, dx=dx, db=db) if dx or db else message)
    own = jnp.concatenate(messages)
    other = at.send(own, dcore=1)
    weight_part = dot(own[:, width : width + lanes], own[:, :width], ((0,), (0,)))
    weight_part = weight_part + dot(other[:, width + lanes :], other[:, :width], ((0,), (0,)))
    bias_part = jnp.sum(own[:, :width].astype(F32), 0) + jnp.sum(other[:, :width].astype(F32), 0)
    bias_part = one_of(one_of(bias_part.reshape(at.rows, LINE, at.bs, own_rows), at.row, 0), at.b, 1)
    bias_part = jnp.concatenate([one_of(bias_part, at.a ^ flip, 0) for flip in ORDER])
    near = at.send(weight_part[2 * own_rows :].astype(LOW), flip=1).astype(F32)
    kept = weight_part[: 2 * own_rows] + near
    far = at.send(kept[own_rows:].astype(LOW), flip=2).astype(F32)
    near_bias = at.send(bias_part[2 * own_rows :], flip=1)
    kept_bias = bias_part[: 2 * own_rows] + near_bias
    bias_grad = kept_bias[:own_rows] + at.send(kept_bias[own_rows:], flip=2)
    return activations, feat_grad, kept[:own_rows] + far, bias_grad


def solution(mesh):
    placed = (
        P(("col", "row"), None),
        P("row", "col"),
        P("col", "row"),
        P("col", "row"),
        P("row"),
        P(("row", "col"), None),
        P(),
        P(("row", "col"), None),
    )
    return jax.shard_map(
        shards,
        mesh=mesh,
        in_specs=placed,
        out_specs=(
            P(("row", "col"), None),
            P(("col", "row"), None),
            P(("row", "col"), None),
            P(("row", "col")),
        ),
        check_vma=False,
    )
```

```python
import functools
import math

import jax
import jax.numpy as jnp
from jax import lax
from jax.experimental import pallas as pl
from jax.experimental.pallas import tpu as pltpu
from jax.sharding import PartitionSpec as P

boost = 2.0
AXES = ("row", "col")
CORES = 2
LINE = 4
ORDER = (0, 2, 1, 3)
CUTS = (0, 9, 16)
CHUNKS = len(CUTS) - 1
LOW = jnp.bfloat16
F32 = jnp.float32


def dot(left, right, dims):
    return lax.dot_general(left, right, ((dims[0], dims[1]), ((), ())), preferred_element_type=F32)


def after(value, *others):
    return lax.optimization_barrier((value, *others))[0]


def one_of(value, index, axis):
    return lax.dynamic_index_in_dim(value, index, axis, keepdims=False)


def lookup(table, index):
    found = 0
    for k, entry in enumerate(table):
        found = found + entry * (index == k).astype(jnp.int32)
    return found


def call(kernel, outs, scratch, *operands, numbers=0, outside=0, alone=False):
    whole = pl.BlockSpec(memory_space=pltpu.VMEM)
    specs = [pl.BlockSpec(memory_space=pltpu.SMEM)] * numbers + [pl.BlockSpec(memory_space=pltpu.HBM)] * outside
    specs += [whole] * (len(operands) - len(specs))
    arrays = [v for v in [*operands[numbers:], *outs, *scratch] if hasattr(v.dtype, "itemsize")]
    need = sum(math.prod(v.shape) * v.dtype.itemsize for v in arrays)
    need = 60 * 2**20 if alone else min(need + 6 * 2**20, 60 * 2**20)
    return pl.pallas_call(
        kernel,
        out_shape=outs,
        in_specs=specs,
        out_specs=[whole] * len(outs),
        scratch_shapes=scratch,
        compiler_params=pltpu.CompilerParams(vmem_limit_bytes=need),
        cost_estimate=pl.CostEstimate(flops=1, bytes_accessed=1, transcendentals=0),
    )(*operands)


def like(*shape, kind=LOW):
    return jax.ShapeDtypeStruct(shape, kind)


def bounds(width):
    return [(low * width // CUTS[-1], high * width // CUTS[-1]) for low, high in zip(CUTS, CUTS[1:])]


def join_kernel(pieces, *refs):
    out, row = refs[-1], 0
    for k, start, rows in pieces:
        out[row : row + rows, :] = refs[k][start : start + rows, :]
        row += rows


def join(*pieces):
    pieces = [piece if isinstance(piece, tuple) else (piece, 0, piece.shape[0]) for piece in pieces]
    arrays = list({id(piece[0]): piece[0] for piece in pieces}.values())
    order = {id(array): k for k, array in enumerate(arrays)}
    rows = sum(piece[2] for piece in pieces)
    places = [(order[id(array)], start, count) for array, start, count in pieces]
    return call(functools.partial(join_kernel, places), [like(rows, arrays[0].shape[1])], [], *arrays)[0]


def bounds(width):
    return [(low * width // CUTS[-1], high * width // CUTS[-1]) for low, high in zip(CUTS, CUTS[1:])]


def like(*shape, kind=LOW):
    return jax.ShapeDtypeStruct(shape, kind)


class Place:
    def __init__(self):
        self.rows = lax.axis_size("row")
        self.cols = lax.axis_size("col")
        self.xs = self.rows // CORES
        self.bs = self.cols // LINE
        self.row = lax.axis_index("row")
        self.col = lax.axis_index("col")
        self.x = self.row // CORES
        self.core = self.row % CORES
        self.a = self.col // self.bs
        self.b = self.col % self.bs
        self.chips = [(dx, db) for db in range(self.bs) for dx in range(self.xs)]
        self.numbers = jnp.stack([self.a, self.b, self.x, self.core]).astype(jnp.int32)

    def index(self, x, core, a, b):
        return ((x % self.xs) * CORES + core % CORES) * self.cols + (a % LINE) * self.bs + b % self.bs

    def send(self, value, dx=0, dcore=0, db=0, flip=0):
        pairs = [
            (self.index(x, core, a, b), self.index(x + dx, core + dcore, a ^ flip, b + db))
            for x in range(self.xs)
            for core in range(CORES)
            for a in range(LINE)
            for b in range(self.bs)
        ]
        return lax.ppermute(value, AXES, pairs)


def put_blocks(xs, bs, place, weights, part, mask, db, outs):
    a, b, x, core = (place[i] for i in range(4))
    size = weights.shape[1]
    rows = xs * CORES
    eye = (
        lax.broadcasted_iota(jnp.int32, (size, size), 0) == lax.broadcasted_iota(jnp.int32, (size, size), 1)
    ).astype(F32)
    tile = lax.rem(b + db, bs)
    for k, flip in enumerate(ORDER):
        line = (a ^ flip) * bs + b
        row_block = (x * CORES + core) * (LINE * bs) + line
        diagonal = eye * (boost * weights[pl.ds(line, 1), :])
        values = part(k)
        for dcore in range(CORES):
            for dx in range(xs):
                block = lax.rem(x + dx, xs) * CORES + lax.rem(core + dcore, CORES)
                node_block = a * (bs * rows) + tile * rows + block
                total = diagonal * (row_block == node_block).astype(F32)
                for slot in range(values.shape[1] // size):
                    total = total + values[:, slot * size : (slot + 1) * size] * mask(k, slot, block)
                outs[dcore][k * size : (k + 1) * size, dx * size : (dx + 1) * size] = total.astype(LOW)


def own_blocks_kernel(xs, bs, slots, place, *refs):
    held, outs, scratch, sems = refs[:4], refs[4:-5], refs[-5:-1], refs[-1]
    copies = [pltpu.make_async_copy(held[i], scratch[i], sems.at[i]) for i in range(4)]
    for copy in copies:
        copy.start()
    for copy in copies:
        copy.wait()
    cols, counts, block_vals, weights = scratch
    a, b = place[0], place[1]
    size = weights.shape[1]

    def line(k, dest):
        return (a ^ ORDER[k]) * bs + dest

    def rows(k, dest):
        return block_vals[pl.ds(pl.multiple_of(line(k, dest) * size, size), size), :]

    def column(k, slot, dest):
        at = line(k, dest)
        return jnp.where(slot < counts[0, at], cols[slot, at], -1)

    for db in range(1, bs):
        out = outs[CORES + db - 1]
        dest = lax.rem(b - db + bs, bs)
        for k in range(LINE):
            out[k * size : (k + 1) * size, :] = rows(k, dest)
        at_row = lax.broadcasted_iota(jnp.int32, (16, slots * size), 0)
        head = jnp.zeros((16, slots * size), jnp.int32)
        for k in range(LINE):
            for slot in range(slots):
                head = jnp.where(at_row == k * slots + slot, column(k, slot, dest), head)
        out[LINE * size :, :] = head.astype(F32).astype(LOW)
    put_blocks(
        xs,
        bs,
        place,
        weights,
        lambda k: rows(k, b).astype(F32),
        lambda k, slot, block: (column(k, slot, b) == block).astype(F32),
        0,
        outs[:CORES],
    )


def sent_blocks_kernel(xs, bs, slots, db, place, got, weights, *outs):
    size = weights.shape[1]
    head = got[LINE * size :, :].astype(F32)

    def mask(k, slot, block):
        at = k * slots + slot
        return (head[at : at + 1, :size] == block.astype(F32)).astype(F32)

    put_blocks(
        xs, bs, place, weights, lambda k: got[k * size : (k + 1) * size, :].astype(F32), mask, db, outs
    )


def operator(at, block_vals, block_cols, block_counts, self_weight, size):
    slots = block_cols.shape[0]
    weights = self_weight.reshape(-1, size)
    dense = like(LINE * size, at.xs * size)
    own, other, *sent = call(
        functools.partial(own_blocks_kernel, at.xs, at.bs, slots),
        [dense] * CORES + [like(LINE * size + 16, slots * size)] * (at.bs - 1),
        [
            pltpu.SMEM(block_cols.shape, jnp.int32),
            pltpu.SMEM(block_counts.shape, jnp.int32),
            pltpu.VMEM(block_vals.shape, block_vals.dtype),
            pltpu.VMEM(weights.shape, weights.dtype),
            pltpu.SemaphoreType.DMA((4,)),
        ],
        at.numbers,
        block_cols,
        block_counts,
        block_vals,
        weights,
        numbers=1,
        outside=4,
        alone=True,
    )
    result = [[own, other]]
    arrived = [at.send(value, db=-db) for db, value in enumerate(sent, 1)]
    for db, got in enumerate(arrived, 1):
        kernel = functools.partial(sent_blocks_kernel, at.xs, at.bs, slots, db)
        result.append(call(kernel, [dense] * CORES, [], at.numbers, got, weights, numbers=1))
    return result, sent


def sums_kernel(n_ops, pieces, *refs):
    ops, arrays, (*outs, left, right) = refs[:n_ops], refs[n_ops:-6], refs[-6:]
    size, wide = outs[0].shape[0], ops[0].shape[1]
    for i, op in enumerate(ops):
        left[:, i * wide : (i + 1) * wide] = op[...]
    for i, (k, row) in enumerate(pieces):
        right[i * size : (i + 1) * size, :] = arrays[k][row : row + size, :]
    step = right.shape[1] // 4
    for k in range(4):
        columns = slice(k * step, (k + 1) * step)
        part = dot(left[...], right[:, columns], ((1,), (0,)))
        for i, out in enumerate(outs):
            out[:, columns] = part[i * size : (i + 1) * size].astype(out.dtype)


def sums(at, ops, own, across):
    size, width = own[0, 0].shape
    arrays = [*own.values(), *across]
    pieces = []
    for db in range(at.bs):
        pieces += [(db * at.xs + dx, 0) for dx in range(at.xs)]
        pieces += [(len(own) + 1, (db * at.xs + dx - 1) * size) if db or dx else (len(own), 0) for dx in range(at.xs)]
    rows, depth = LINE * size, len(pieces) * size
    return call(
        functools.partial(sums_kernel, CORES * at.bs, pieces),
        [like(size, width, kind=F32)] * 2 + [like(size, width)] * 2,
        [pltpu.VMEM((rows, depth), LOW), pltpu.VMEM((depth, width), LOW)],
        *[op for pair in ops for op in pair],
        *arrays,
    )


def back_kernel(n_ops, *refs):
    ops, lines, rest = refs[:n_ops], refs[n_ops : n_ops + 3], refs[n_ops + 3 :]
    right = jnp.concatenate([line[...] for line in lines], 0)
    parts = [dot(op[...], right, ((0,), (0,))) for op in ops]
    if len(rest) == 1:
        rows = parts[0].shape[0]
        for i, part in enumerate(parts):
            rest[0][i * rows : (i + 1) * rows, :] = part.astype(LOW)
        return
    got, outs = rest[0], rest[1:]
    size = outs[0].shape[0]
    per = parts[0].shape[0] // size
    for i, out in enumerate(outs):
        k = i % per * size
        total = parts[i // per][k : k + size] + got[i * size : (i + 1) * size, :].astype(F32)
        out[...] = total.astype(out.dtype)


def add_up_kernel(n_keeps, *refs):
    *parts, out = refs
    per = len(parts) // n_keeps
    for k, (start, end) in enumerate(bounds(out.shape[1])):
        total = parts[k * per][...]
        for part in parts[k * per + 1 : (k + 1) * per]:
            total = total + part[...].astype(F32)
        out[:, start:end] = total


def along_x(at, value):
    return [value] + [at.send(value, dx=-dx) for dx in range(1, at.xs)]


def along_b(at, value):
    return [value] + [at.send(value, db=-db) for db in range(1, at.bs)]


def gathered_halves(at, halves, gate):
    rows = halves[0].shape[0]
    left, right = along_x(at, halves[0]), along_b(at, halves[1])
    steps = [left[1:] + right[1:]]
    arrays, held = [join(after(left[0], gate), *left[1:]), join(after(right[0], gate), *right[1:])], {}
    for dx in range(at.xs):
        held[dx, 0, 0] = (0, dx * rows)
    for db in range(at.bs):
        held[0, db, 1] = (1, db * rows)
    left, right = arrays
    for db in range(1, at.bs):
        arrays.append(at.send(left, db=-db))
        for dx in range(at.xs):
            held[dx, db, 0] = (len(arrays) - 1, dx * rows)
    for dx in range(1, at.xs):
        arrays.append(at.send(right, dx=-dx))
        for db in range(at.bs):
            held[dx, db, 1] = (len(arrays) - 1, db * rows)
    return arrays, held, steps + [arrays[2:]]


def both_cores(at, arrays, held, gates):
    count = len(arrays)
    across = [at.send(after(value, *gate), dcore=1) for value, gate in zip(arrays, gates)]
    places = {(0, *place): at for place, at in held.items()}
    places.update({(1, *place): (k + count, i) for place, (k, i) in held.items()})
    return arrays + across, places


def line_kernel(place, weight, far, near, last, left, right):
    count, half = weight.shape[0], left.shape[1]
    for flip, source in zip(ORDER, (weight, far, near, last)):
        rows = pl.ds(pl.multiple_of((place[0] ^ flip) * count, count), count)
        left[rows, :] = source[:, :half]
        right[rows, :] = source[:, half:]


def line_weight(at, weight):
    count, width = weight.shape
    far = at.send(weight, flip=2)
    near = at.send(after(weight, far), flip=1)
    last = at.send(far, flip=1)
    halves = [like(LINE * count, width // 2)] * 2
    return call(line_kernel, halves, [], at.numbers, weight, far, near, last, numbers=1)


def dense_kernel(held, xs, bs, lanes, n_held, place, *refs):
    (bias_in, grad_in), arrays, refs = refs[:2], refs[2 : 2 + n_held], refs[2 + n_held :]
    total, near, far, act_ref, left_ref, right_ref, rows_ref = refs[:7]
    messages, refs = refs[7 : 6 + xs], refs[6 + xs :]
    backs, refs = refs[:CHUNKS], refs[CHUNKS:]
    agg_ref, turned, acc, back, blocks, bias, out_grad, sems = refs
    b, x, core = place[1], place[2], place[3]
    width = bias.shape[1]
    half = width // 2
    group = bs * lanes
    places = [(dcore, dx, db) for dcore in range(CORES) for db in range(bs) for dx in range(xs)]
    number = {(at, h): n for n, (at, h) in enumerate((at, h) for at in places for h in range(2))}

    copies = [pltpu.make_async_copy(bias_in, bias, sems.at[0])]
    for (at, h), n in number.items():
        k, row = held[*at, h]
        block = blocks.at[pl.ds(n * lanes, lanes), :]
        copies.append(pltpu.make_async_copy(arrays[k].at[pl.ds(row, lanes), :], block, sems.at[n + 1]))
    copies.append(pltpu.make_async_copy(grad_in, out_grad, sems.at[len(number) + 1]))
    for copy in copies:
        copy.start()

    def weight(at, h):
        n = number[at, h]
        return blocks[n * lanes : (n + 1) * lanes, :]

    agg_ref[...] = (total[...] + near[...].astype(F32) + far[...].astype(F32)).astype(LOW)
    count = lanes // LINE
    at_in = lax.broadcasted_iota(jnp.int32, (group, group), 0)
    at_out = lax.broadcasted_iota(jnp.int32, (group, group), 1)
    db, inner = at_out // lanes, at_out % lanes
    source = (inner // count) * (bs * count) + lax.rem(b + db, bs) * count + inner % count
    turn = (at_in == source).astype(F32).astype(LOW)
    for r in range(width // group):
        at_r = slice(r * group, (r + 1) * group)
        turned[:, at_r] = dot(agg_ref[:, at_r], turn, ((1,), (0,))).astype(LOW)

    def columns(dcore, dx, db):
        row = lax.rem(x + dx, xs) * CORES + lax.rem(core + dcore, CORES)
        return pl.ds(pl.multiple_of(row * group + db * lanes, lanes), lanes)

    copies[0].wait()
    acc[...] = jnp.broadcast_to(bias[...], acc.shape)
    for at in places:
        left = turned[:, columns(*at)]
        for h in range(2):
            copies[1 + number[at, h]].wait()
            acc[:, h * half : (h + 1) * half] += dot(left, weight(at, h), ((1,), (0,)))
    copies[-1].wait()
    for dx, out in enumerate([rows_ref, *messages]):
        start = half if dx else 0
        for db in range(bs):
            for dcore in range(CORES):
                out[:, start : start + lanes] = turned[:, columns(dcore, dx, db)]
                start += lanes
    pre = acc[...]
    phi = 0.5 * (1.0 + lax.erf(pre * (0.5**0.5)))
    act_ref[...] = (pre * phi).astype(LOW)
    slope = phi + pre * (jnp.exp(-0.5 * pre * pre) * 0.3989422804014327)
    pre_low = (out_grad[...].astype(F32) * slope).astype(LOW)
    for out in (left_ref, *messages):
        out[:, :half] = pre_low[:, :half]
    right_ref[...] = pre_low[:, half:]
    for at in places:
        total = 0.0
        for h, ref in enumerate((left_ref, right_ref)):
            total = total + dot(ref[...], weight(at, h), ((1,), (1,)))
        back[:, columns(*at)] = total.astype(LOW)
    for r in range(width // group):
        part = dot(back[:, r * group : (r + 1) * group], turn, ((1,), (1,))).astype(LOW)
        for k, (start, end) in enumerate(bounds(width)):
            left, right = max(start, r * group), min(end, (r + 1) * group)
            if left < right:
                backs[k][:, left - start : right - start] = part[:, left - r * group : right - r * group]


def pick_kernel(db, *refs):
    left, rows, messages, out = refs[0], refs[1], refs[2:-1], refs[-1]
    size, half = left.shape
    wide = out.shape[1] - half
    out[:size, :half] = left[...]
    out[:size, half:] = rows[:, db * wide : (db + 1) * wide]
    for i, message in enumerate(messages, 1):
        at = slice(i * size, (i + 1) * size)
        out[at, :half] = message[:, :half]
        out[at, half:] = message[:, half + db * wide : half + (db + 1) * wide]


def spread(at, lanes, left, right, rows, messages, gate):
    size, half = left.shape
    arrived = [at.send(message, dx=dx) for dx, message in enumerate(messages, 1)]
    rights = [right] + [at.send(right, db=db) for db in range(1, at.bs)]
    steps = [arrived + rights[1:]]

    def pick(db):
        outs = [like(at.xs * size, half + CORES * lanes)]
        return call(functools.partial(pick_kernel, db), outs, [], after(left, gate), rows, *arrived)[0]

    held = {}

    def keep(k, place, row):
        held[place] = (k, row)

    arrays = [pick(0), join(after(right, gate), *rights[1:])]
    for dx in range(at.xs):
        keep(0, (-dx % at.xs, 0, 0), dx * size)
    for db in range(at.bs):
        keep(1, (0, -db % at.bs, 1), db * size)
    for db in range(1, at.bs):
        arrays.append(at.send(pick(db), db=db))
        for dx in range(at.xs):
            keep(len(arrays) - 1, (-dx % at.xs, -db % at.bs, 0), dx * size)
    for dx in range(1, at.xs):
        arrays.append(at.send(arrays[1], dx=dx))
        for db in range(at.bs):
            keep(len(arrays) - 1, (-dx % at.xs, -db % at.bs, 1), db * size)
    return arrays, held, steps + [arrays[2:]]


def grad_kernel(held, xs, bs, lanes, dcore, n_arrays, place, *refs):
    arrays, (*outs, left, right, product, sums_ref) = refs[:n_arrays], refs[n_arrays:]
    a, b, x, core = (place[i] for i in range(4))
    size, width = left.shape[0] // (xs * bs), right.shape[1]
    half, count, group = width // 2, lanes // LINE, bs * lanes
    for n, (dx, db) in enumerate((dx, db) for db in range(bs) for dx in range(xs)):
        rows = slice(n * size, (n + 1) * size)
        k, row = held[dx, db, 0]
        right[rows, :half] = arrays[k][row : row + size, :half]
        start = half + dcore * lanes
        left[rows, :] = arrays[k][row : row + size, start : start + lanes]
        k, row = held[dx, db, 1]
        right[rows, half:] = arrays[k][row : row + size, :]
    product[:, :width] = dot(left[...], right[...], ((0,), (0,)))
    total = jnp.sum(right[...].astype(F32), 0, keepdims=True)
    sums_ref[...] = jnp.broadcast_to(total, sums_ref.shape)
    row = x * CORES + lax.rem(core + dcore, CORES)
    own = sums_ref[0:1, pl.ds(pl.multiple_of(row * group, group), group)]
    at_row = lax.broadcasted_iota(jnp.int32, (lanes, group), 0)
    at_lane = lax.broadcasted_iota(jnp.int32, (lanes, group), 1)
    source = (at_row // count) * (bs * count) + b * count + at_row % count
    column = jnp.sum(jnp.where(at_lane == source, own, 0.0), 1, keepdims=True)
    product[:, width:] = jnp.broadcast_to(column, (lanes, 128))
    if dcore:
        [out] = outs
        out[:, :width] = product[:, :width].astype(LOW)
        out[:, width:] = two_parts(product[:, width:])
        return
    got, outs = outs[0], outs[1:]
    for out, flip in zip(outs, ORDER):
        rows = pl.ds(pl.multiple_of((a ^ flip) * count, count), count)
        tail = got[rows, width:].astype(F32)
        tail = product[rows, width:] + (tail[:, 0:1] + tail[:, 1:2])
        out[:, :width] = (product[rows, :width] + got[rows, :width].astype(F32)).astype(out.dtype)
        out[:, width : width + 128] = two_parts(tail) if out.dtype == LOW else tail


def two_parts(value):
    high = value.astype(LOW)
    rest = (value - high.astype(F32)).astype(LOW)
    lane = lax.broadcasted_iota(jnp.int32, value.shape, 1)
    return jnp.where(lane == 0, high.astype(F32), jnp.where(lane == 1, rest.astype(F32), 0.0)).astype(LOW)


def fold_kernel(kept, got, far):
    width = got.shape[1] - 128
    tail = got[:, width:].astype(F32)
    far[:, :width] = (kept[:, :width] + got[:, :width].astype(F32)).astype(LOW)
    far[:, width : width + 128] = two_parts(kept[:, width : width + 128] + (tail[:, 0:1] + tail[:, 1:2]))


def last_fold_kernel(kept, *refs):
    *arrived, weight_out, bias_out = refs
    width = weight_out.shape[1]
    total, tail = kept[:, :width], kept[:, width : width + 128]
    for got in arrived:
        total = total + got[:, :width].astype(F32)
        rest = got[:, width : width + 128].astype(F32)
        tail = tail + (rest[:, 0:1] + rest[:, 1:2])
    weight_out[...] = total
    bias_out[...] = tail


def far_kernel(kept, got, far):
    far[...] = (kept[...] + got[...].astype(F32)).astype(LOW)


def shards(node_feats, block_vals, block_cols, block_counts, self_weight, weight, bias, out_grad):
    at = Place()
    size, width = node_feats.shape
    own_rows = weight.shape[0]
    lanes = LINE * own_rows
    aligned = lanes % 128 == 0
    halves = line_weight(at, weight) if aligned else []
    ops, gate = operator(at, block_vals, block_cols, block_counts, self_weight, size)
    node_feats = after(node_feats, *gate)
    own = {(dx, db): at.send(node_feats, dx=-dx, db=-db) if dx or db else node_feats for dx, db in at.chips}
    first, *chips = at.chips
    across = [at.send(own[first], dcore=1), at.send(join(after(own[chips[0]], *ops[-1], *halves), *[own[chip] for chip in chips[1:]]), dcore=1)]
    total, kept, to_near, to_last = sums(at, ops, own, across)
    got = at.send(to_last, flip=1)
    near = at.send(to_near, flip=1)
    [far] = call(far_kernel, [like(size, width)], [], kept, got)
    far = at.send(far, flip=2)

    if not aligned:
        return plain_rest(at, ops, total + near.astype(F32) + far.astype(F32), weight, bias, out_grad)
    halves = [after(half, *own.values(), *ops[-1]) for half in halves]
    arrays, held, steps = gathered_halves(at, halves, to_last)
    early = len(arrays) - len(steps[1])
    arrays, held = both_cores(at, arrays, held, [[]] * early + [[near, far]] * len(steps[1]))
    widths = [end - start for start, end in bounds(width)]
    n_blocks = len(held)
    activations, left, right, rows, *rest = call(
        functools.partial(dense_kernel, held, at.xs, at.bs, lanes, len(arrays)),
        [like(size, width)]
        + [like(size, width // 2)] * 2
        + [like(size, at.bs * CORES * lanes)]
        + [like(size, width // 2 + at.bs * CORES * lanes)] * (at.xs - 1)
        + [like(size, wide) for wide in widths],
        [pltpu.VMEM((size, width), kind) for kind in (LOW, LOW, F32, LOW)]
        + [
            pltpu.VMEM((n_blocks * lanes, width // 2), LOW),
            pltpu.VMEM((1, width), F32),
            pltpu.VMEM((size, width), LOW),
            pltpu.SemaphoreType.DMA((n_blocks + 2,)),
        ],
        at.numbers,
        bias[None, :],
        out_grad,
        *arrays,
        total,
        near,
        far,
        numbers=1,
        outside=2 + len(arrays),
    )
    messages, backs = rest[: at.xs - 1], rest[at.xs - 1 :]

    fars = [at.send(backs[0], flip=2)]
    arrays, held, steps = spread(at, lanes, left, right, rows, messages, fars[0])
    nears = [at.send(join(backs[0], fars[0]), flip=1)]
    for k in range(1, CHUNKS):
        fars.append(at.send(after(backs[k], *fars, *steps[0]), flip=2))
        nears.append(at.send(join(backs[k], fars[k]), flip=1))
    feat, parts = feat_sums(at, ops, backs[0], fars[0], after(nears[0], *fars, *steps[1]))
    gates = feat[1:]
    wide, long = width + 128, width + 256
    scratch = [
        pltpu.VMEM((size * len(at.chips), lanes), LOW),
        pltpu.VMEM((size * len(at.chips), width), LOW),
        pltpu.VMEM((lanes, wide), F32),
        pltpu.VMEM((8, width), F32),
    ]
    kernel = functools.partial(grad_kernel, held, at.xs, at.bs, lanes)
    [across] = call(
        functools.partial(kernel, 1, len(arrays)), [like(lanes, wide)], scratch, at.numbers, *arrays, numbers=1
    )
    got = at.send(across, dcore=1)
    outs = [like(own_rows, wide, kind=F32)] * 2 + [like(own_rows, long), like(own_rows, wide)]
    total, kept, to_near, to_last = call(
        functools.partial(kernel, 0, len(arrays)), outs, scratch, at.numbers, *arrays, got, numbers=1
    )
    got = at.send(to_last, flip=1)
    [sent] = call(fold_kernel, [like(own_rows, long)], [], kept, got)
    for k in range(1, CHUNKS):
        more, parts = feat_sums(at, ops, backs[k], fars[k], after(nears[k], sent, *parts, *gates))
        feat = feat + more
    near = at.send(to_near, flip=1)
    far = at.send(sent, flip=2)
    [feat_grad] = call(functools.partial(add_up_kernel, CHUNKS), [like(size, width, kind=F32)], [], *feat)
    outs = [like(own_rows, width, kind=F32), like(own_rows, 128, kind=F32)]
    weight_grad, bias_grad = call(last_fold_kernel, outs, [], after(total, feat_grad), near, far)
    return activations, feat_grad, weight_grad, bias_grad[:, 0]


def feat_sums(at, ops, *lines):
    size, chunk = lines[0].shape
    rows = len(at.chips) * size
    kernel = functools.partial(back_kernel, len(ops))
    [across] = call(kernel, [like(rows, chunk)], [], *[pair[1] for pair in ops], *lines)
    got = at.send(across, dcore=1)
    outs = [like(size, chunk, kind=F32)] + [like(size, chunk)] * (len(at.chips) - 1)
    parts = call(kernel, outs, [], *[pair[0] for pair in ops], *lines, got)
    sent = [at.send(part, dx=dx, db=db) for part, (dx, db) in zip(parts[1:], at.chips[1:])]
    return [parts[0]] + sent, parts


def plain_rest(at, ops, agg, weight, bias, out_grad):
    size, width = out_grad.shape
    own_rows = weight.shape[0]
    lanes = LINE * own_rows
    agg = agg.astype(LOW)
    whole_weight = lax.all_gather(weight, AXES, axis=0, tiled=True)
    pre = dot(agg, whole_weight, ((1,), (0,))) + bias[None, :]
    phi = 0.5 * (1.0 + lax.erf(pre * (0.5**0.5)))
    activations = (pre * phi).astype(LOW)
    slope = phi + pre * (jnp.exp(-0.5 * pre * pre) * 0.3989422804014327)
    pre_low = (out_grad.astype(F32) * slope).astype(LOW)
    feat = []
    for start, end in bounds(width):
        back = dot(pre_low, whole_weight[start:end], ((1,), (1,))).astype(LOW)
        far = at.send(back, flip=2)
        feat = feat + feat_sums(at, ops, back, far, at.send(join(back, far), flip=1))[0]
    [feat_grad] = call(functools.partial(add_up_kernel, CHUNKS), [like(size, width, kind=F32)], [], *feat)

    groups = agg.reshape(size, at.rows, LINE, at.bs, own_rows)
    groups = jnp.concatenate([lax.dynamic_slice_in_dim(groups, at.a ^ flip, 1, 2) for flip in ORDER], 2)
    messages = []
    for dx, db in at.chips:
        dest_x = (at.x + dx) % at.xs
        wide = one_of(groups, (at.b + db) % at.bs, 3)
        picked = [
            one_of(wide, dest_x * CORES + (at.core + dcore) % CORES, 1).reshape(size, lanes) for dcore in range(CORES)
        ]
        message = jnp.concatenate([pre_low] + picked, 1)
        messages.append(at.send(message, dx=dx, db=db) if dx or db else message)
    own = jnp.concatenate(messages)
    other = at.send(own, dcore=1)
    weight_part = dot(own[:, width : width + lanes], own[:, :width], ((0,), (0,)))
    weight_part = weight_part + dot(other[:, width + lanes :], other[:, :width], ((0,), (0,)))
    bias_part = jnp.sum(own[:, :width].astype(F32), 0) + jnp.sum(other[:, :width].astype(F32), 0)
    bias_part = one_of(one_of(bias_part.reshape(at.rows, LINE, at.bs, own_rows), at.row, 0), at.b, 1)
    bias_part = jnp.concatenate([one_of(bias_part, at.a ^ flip, 0) for flip in ORDER])
    near = at.send(weight_part[2 * own_rows :].astype(LOW), flip=1).astype(F32)
    kept = weight_part[: 2 * own_rows] + near
    far = at.send(kept[own_rows:].astype(LOW), flip=2).astype(F32)
    near_bias = at.send(bias_part[2 * own_rows :], flip=1)
    kept_bias = bias_part[: 2 * own_rows] + near_bias
    bias_grad = kept_bias[:own_rows] + at.send(kept_bias[own_rows:], flip=2)
    return activations, feat_grad, kept[:own_rows] + far, bias_grad


def solution(mesh):
    placed = (
        P(("col", "row"), None),
        P("row", "col"),
        P("col", "row"),
        P("col", "row"),
        P("row"),
        P(("row", "col"), None),
        P(),
        P(("row", "col"), None),
    )
    return jax.shard_map(
        shards,
        mesh=mesh,
        in_specs=placed,
        out_specs=(
            P(("row", "col"), None),
            P(("col", "row"), None),
            P(("row", "col"), None),
            P(("row", "col")),
        ),
        check_vma=False,
    )
```

```python
import functools
import math

import jax
import jax.numpy as jnp
from jax import lax
from jax.experimental import pallas as pl
from jax.experimental.pallas import tpu as pltpu
from jax.sharding import PartitionSpec as P

boost = 2.0
AXES = ("row", "col")
CORES = 2
LINE = 4
ORDER = (0, 2, 1, 3)
CUTS = (0, 9, 16)
CHUNKS = len(CUTS) - 1
LOW = jnp.bfloat16
F32 = jnp.float32


def dot(left, right, dims):
    return lax.dot_general(left, right, ((dims[0], dims[1]), ((), ())), preferred_element_type=F32)


def after(value, *others):
    return lax.optimization_barrier((value, *others))[0]


def one_of(value, index, axis):
    return lax.dynamic_index_in_dim(value, index, axis, keepdims=False)


def lookup(table, index):
    found = 0
    for k, entry in enumerate(table):
        found = found + entry * (index == k).astype(jnp.int32)
    return found


def call(kernel, outs, scratch, *operands, numbers=0, outside=0, alone=False):
    whole = pl.BlockSpec(memory_space=pltpu.VMEM)
    specs = [pl.BlockSpec(memory_space=pltpu.SMEM)] * numbers + [pl.BlockSpec(memory_space=pltpu.HBM)] * outside
    specs += [whole] * (len(operands) - len(specs))
    arrays = [v for v in [*operands[numbers:], *outs, *scratch] if hasattr(v.dtype, "itemsize")]
    need = sum(math.prod(v.shape) * v.dtype.itemsize for v in arrays)
    need = 60 * 2**20 if alone else min(need + 6 * 2**20, 60 * 2**20)
    return pl.pallas_call(
        kernel,
        out_shape=outs,
        in_specs=specs,
        out_specs=[whole] * len(outs),
        scratch_shapes=scratch,
        compiler_params=pltpu.CompilerParams(vmem_limit_bytes=need),
        cost_estimate=pl.CostEstimate(flops=1, bytes_accessed=1, transcendentals=0),
    )(*operands)


def like(*shape, kind=LOW):
    return jax.ShapeDtypeStruct(shape, kind)


def bounds(width):
    return [(low * width // CUTS[-1], high * width // CUTS[-1]) for low, high in zip(CUTS, CUTS[1:])]


def join_kernel(pieces, *refs):
    out, row = refs[-1], 0
    for k, start, rows in pieces:
        out[row : row + rows, :] = refs[k][start : start + rows, :]
        row += rows


def join(*pieces):
    pieces = [piece if isinstance(piece, tuple) else (piece, 0, piece.shape[0]) for piece in pieces]
    arrays = list({id(piece[0]): piece[0] for piece in pieces}.values())
    order = {id(array): k for k, array in enumerate(arrays)}
    rows = sum(piece[2] for piece in pieces)
    places = [(order[id(array)], start, count) for array, start, count in pieces]
    return call(functools.partial(join_kernel, places), [like(rows, arrays[0].shape[1])], [], *arrays)[0]


def bounds(width):
    return [(low * width // CUTS[-1], high * width // CUTS[-1]) for low, high in zip(CUTS, CUTS[1:])]


def like(*shape, kind=LOW):
    return jax.ShapeDtypeStruct(shape, kind)


class Place:
    def __init__(self):
        self.rows = lax.axis_size("row")
        self.cols = lax.axis_size("col")
        self.xs = self.rows // CORES
        self.bs = self.cols // LINE
        self.row = lax.axis_index("row")
        self.col = lax.axis_index("col")
        self.x = self.row // CORES
        self.core = self.row % CORES
        self.a = self.col // self.bs
        self.b = self.col % self.bs
        self.chips = [(dx, db) for db in range(self.bs) for dx in range(self.xs)]
        self.numbers = jnp.stack([self.a, self.b, self.x, self.core]).astype(jnp.int32)

    def index(self, x, core, a, b):
        return ((x % self.xs) * CORES + core % CORES) * self.cols + (a % LINE) * self.bs + b % self.bs

    def send(self, value, dx=0, dcore=0, db=0, flip=0):
        pairs = [
            (self.index(x, core, a, b), self.index(x + dx, core + dcore, a ^ flip, b + db))
            for x in range(self.xs)
            for core in range(CORES)
            for a in range(LINE)
            for b in range(self.bs)
        ]
        return lax.ppermute(value, AXES, pairs)


def put_blocks(xs, bs, place, weights, part, mask, db, outs):
    a, b, x, core = (place[i] for i in range(4))
    size = weights.shape[1]
    rows = xs * CORES
    eye = (
        lax.broadcasted_iota(jnp.int32, (size, size), 0) == lax.broadcasted_iota(jnp.int32, (size, size), 1)
    ).astype(F32)
    tile = lax.rem(b + db, bs)
    for k, flip in enumerate(ORDER):
        line = (a ^ flip) * bs + b
        row_block = (x * CORES + core) * (LINE * bs) + line
        diagonal = eye * (boost * weights[pl.ds(line, 1), :])
        values = part(k)
        for dcore in range(CORES):
            for dx in range(xs):
                block = lax.rem(x + dx, xs) * CORES + lax.rem(core + dcore, CORES)
                node_block = a * (bs * rows) + tile * rows + block
                total = diagonal * (row_block == node_block).astype(F32)
                for slot in range(values.shape[1] // size):
                    total = total + values[:, slot * size : (slot + 1) * size] * mask(k, slot, block)
                outs[dcore][k * size : (k + 1) * size, dx * size : (dx + 1) * size] = total.astype(LOW)


def own_blocks_kernel(xs, bs, slots, place, *refs):
    held, outs, scratch, sems = refs[:4], refs[4:-5], refs[-5:-1], refs[-1]
    copies = [pltpu.make_async_copy(held[i], scratch[i], sems.at[i]) for i in range(4)]
    for copy in copies:
        copy.start()
    for copy in copies:
        copy.wait()
    cols, counts, block_vals, weights = scratch
    a, b = place[0], place[1]
    size = weights.shape[1]

    def line(k, dest):
        return (a ^ ORDER[k]) * bs + dest

    def rows(k, dest):
        return block_vals[pl.ds(pl.multiple_of(line(k, dest) * size, size), size), :]

    def column(k, slot, dest):
        at = line(k, dest)
        return jnp.where(slot < counts[0, at], cols[slot, at], -1)

    for db in range(1, bs):
        out = outs[CORES + db - 1]
        dest = lax.rem(b - db + bs, bs)
        for k in range(LINE):
            out[k * size : (k + 1) * size, :] = rows(k, dest)
        at_row = lax.broadcasted_iota(jnp.int32, (16, slots * size), 0)
        head = jnp.zeros((16, slots * size), jnp.int32)
        for k in range(LINE):
            for slot in range(slots):
                head = jnp.where(at_row == k * slots + slot, column(k, slot, dest), head)
        out[LINE * size :, :] = head.astype(F32).astype(LOW)
    put_blocks(
        xs,
        bs,
        place,
        weights,
        lambda k: rows(k, b).astype(F32),
        lambda k, slot, block: (column(k, slot, b) == block).astype(F32),
        0,
        outs[:CORES],
    )


def sent_blocks_kernel(xs, bs, slots, db, place, got, weights, *outs):
    size = weights.shape[1]
    head = got[LINE * size :, :].astype(F32)

    def mask(k, slot, block):
        at = k * slots + slot
        return (head[at : at + 1, :size] == block.astype(F32)).astype(F32)

    put_blocks(
        xs, bs, place, weights, lambda k: got[k * size : (k + 1) * size, :].astype(F32), mask, db, outs
    )


def operator(at, block_vals, block_cols, block_counts, self_weight, size):
    slots = block_cols.shape[0]
    weights = self_weight.reshape(-1, size)
    dense = like(LINE * size, at.xs * size)
    own, other, *sent = call(
        functools.partial(own_blocks_kernel, at.xs, at.bs, slots),
        [dense] * CORES + [like(LINE * size + 16, slots * size)] * (at.bs - 1),
        [
            pltpu.SMEM(block_cols.shape, jnp.int32),
            pltpu.SMEM(block_counts.shape, jnp.int32),
            pltpu.VMEM(block_vals.shape, block_vals.dtype),
            pltpu.VMEM(weights.shape, weights.dtype),
            pltpu.SemaphoreType.DMA((4,)),
        ],
        at.numbers,
        block_cols,
        block_counts,
        block_vals,
        weights,
        numbers=1,
        outside=4,
        alone=True,
    )
    result = [[own, other]]
    arrived = [at.send(value, db=-db) for db, value in enumerate(sent, 1)]
    for db, got in enumerate(arrived, 1):
        kernel = functools.partial(sent_blocks_kernel, at.xs, at.bs, slots, db)
        result.append(call(kernel, [dense] * CORES, [], at.numbers, got, weights, numbers=1))
    return result, sent, arrived


def sums_kernel(n_ops, pieces, *refs):
    ops, arrays, (*outs, left, right) = refs[:n_ops], refs[n_ops:-6], refs[-6:]
    size, wide = outs[0].shape[0], ops[0].shape[1]
    for i, op in enumerate(ops):
        left[:, i * wide : (i + 1) * wide] = op[...]
    for i, (k, row) in enumerate(pieces):
        right[i * size : (i + 1) * size, :] = arrays[k][row : row + size, :]
    step = right.shape[1] // 4
    for k in range(4):
        columns = slice(k * step, (k + 1) * step)
        part = dot(left[...], right[:, columns], ((1,), (0,)))
        for i, out in enumerate(outs):
            out[:, columns] = part[i * size : (i + 1) * size].astype(out.dtype)


def sums(at, ops, own, across):
    size, width = own[0, 0].shape
    arrays = [*own.values(), *across]
    pieces = []
    for db in range(at.bs):
        pieces += [(db * at.xs + dx, 0) for dx in range(at.xs)]
        pieces += [(len(own) + 1, (db * at.xs + dx - 1) * size) if db or dx else (len(own), 0) for dx in range(at.xs)]
    rows, depth = LINE * size, len(pieces) * size
    return call(
        functools.partial(sums_kernel, CORES * at.bs, pieces),
        [like(size, width, kind=F32)] * 2 + [like(size, width)] * 2,
        [pltpu.VMEM((rows, depth), LOW), pltpu.VMEM((depth, width), LOW)],
        *[op for pair in ops for op in pair],
        *arrays,
    )


def back_kernel(n_ops, *refs):
    ops, lines, rest = refs[:n_ops], refs[n_ops : n_ops + 3], refs[n_ops + 3 :]
    right = jnp.concatenate([line[...] for line in lines], 0)
    parts = [dot(op[...], right, ((0,), (0,))) for op in ops]
    if len(rest) == 1:
        rows = parts[0].shape[0]
        for i, part in enumerate(parts):
            rest[0][i * rows : (i + 1) * rows, :] = part.astype(LOW)
        return
    got, outs = rest[0], rest[1:]
    size = outs[0].shape[0]
    per = parts[0].shape[0] // size
    for i, out in enumerate(outs):
        k = i % per * size
        total = parts[i // per][k : k + size] + got[i * size : (i + 1) * size, :].astype(F32)
        out[...] = total.astype(out.dtype)


def add_up_kernel(n_keeps, *refs):
    *parts, out = refs
    per = len(parts) // n_keeps
    for k, (start, end) in enumerate(bounds(out.shape[1])):
        total = parts[k * per][...]
        for part in parts[k * per + 1 : (k + 1) * per]:
            total = total + part[...].astype(F32)
        out[:, start:end] = total


def along_x(at, value):
    return [value] + [at.send(value, dx=-dx) for dx in range(1, at.xs)]


def along_b(at, value):
    return [value] + [at.send(value, db=-db) for db in range(1, at.bs)]


def gathered_halves(at, halves, gate):
    rows = halves[0].shape[0]
    left, right = along_x(at, halves[0]), along_b(at, halves[1])
    steps = [left[1:] + right[1:]]
    arrays, held = [join(after(left[0], gate), *left[1:]), join(after(right[0], gate), *right[1:])], {}
    for dx in range(at.xs):
        held[dx, 0, 0] = (0, dx * rows)
    for db in range(at.bs):
        held[0, db, 1] = (1, db * rows)
    left, right = arrays
    for db in range(1, at.bs):
        arrays.append(at.send(left, db=-db))
        for dx in range(at.xs):
            held[dx, db, 0] = (len(arrays) - 1, dx * rows)
    for dx in range(1, at.xs):
        arrays.append(at.send(right, dx=-dx))
        for db in range(at.bs):
            held[dx, db, 1] = (len(arrays) - 1, db * rows)
    return arrays, held, steps + [arrays[2:]]


def both_cores(at, arrays, held, gates):
    count = len(arrays)
    across = [at.send(after(value, *gate), dcore=1) for value, gate in zip(arrays, gates)]
    places = {(0, *place): at for place, at in held.items()}
    places.update({(1, *place): (k + count, i) for place, (k, i) in held.items()})
    return arrays + across, places


def line_kernel(place, weight, far, near, last, left, right):
    count, half = weight.shape[0], left.shape[1]
    for flip, source in zip(ORDER, (weight, far, near, last)):
        rows = pl.ds(pl.multiple_of((place[0] ^ flip) * count, count), count)
        left[rows, :] = source[:, :half]
        right[rows, :] = source[:, half:]


def line_weight(at, weight, *gates):
    count, width = weight.shape
    far = at.send(weight, flip=2)
    near = at.send(weight, flip=1)
    last = at.send(far, flip=1)
    halves = [like(LINE * count, width // 2)] * 2
    return call(line_kernel, halves, [], at.numbers, weight, far, near, after(last, *gates), numbers=1)


def turned_halves(value, swap):
    parts = [value[:, i : i + 128] for i in range(0, value.shape[1], 128)]
    return [jnp.where(swap, pltpu.roll(part, 64, 1), part) for part in parts]


def apart(value, b):
    parts = turned_halves(value, b == 1)
    left = lax.broadcasted_iota(jnp.int32, parts[0].shape, 1) < 64
    own, other = [], []
    for one, two in zip(parts[::2], parts[1::2]):
        own.append(jnp.where(left, one, pltpu.roll(two, 64, 1)))
        other.append(jnp.where(left, pltpu.roll(one, 64, 1), two))
    return jnp.concatenate(own, 1), jnp.concatenate(other, 1)


def together(own, other, b):
    parts = []
    left = lax.broadcasted_iota(jnp.int32, (own.shape[0], 128), 1) < 64
    for i in range(0, own.shape[1], 128):
        one, two = own[:, i : i + 128], other[:, i : i + 128]
        parts.append(jnp.where(left, one, pltpu.roll(two, 64, 1)))
        parts.append(jnp.where(left, pltpu.roll(one, 64, 1), two))
    return jnp.concatenate(turned_halves(jnp.concatenate(parts, 1), b == 1), 1)


def pieces_of(held):
    pieces = {}
    for (*at, h), (k, row) in sorted(held.items(), key=lambda item: item[1]):
        pieces.setdefault((h, k), []).append(tuple(at))
    return pieces


def first_dense_kernel(held, xs, bs, lanes, n_held, place, *refs):
    arrays, (total, near, far, bias, turned, pre, agg) = refs[:n_held], refs[n_held:]
    b, x, core = place[1], place[2], place[3]
    half, group = bias.shape[1] // 2, bs * lanes
    agg[...] = total[...] + near[...].astype(F32) + far[...].astype(F32)
    n = 0
    for dcore in range(CORES):
        for dx in range(xs):
            row = lax.rem(x + dx, xs) * CORES + lax.rem(core + dcore, CORES)
            for part in apart(agg[:, pl.ds(pl.multiple_of(row * group, group), group)], b):
                turned[:, n * lanes : (n + 1) * lanes] = part.astype(LOW)
                n += 1
    for h in range(2):
        part = slice(h * half, (h + 1) * half)
        pre[:, part] = products(held, arrays, turned, h, xs, bs, lanes) + bias[:, part]


def products(held, arrays, turned, h, xs, bs, lanes):
    total = 0.0
    for (side, k), ats in pieces_of(held).items():
        if side == h and k < len(arrays):
            rows = [((dcore * xs + dx) * bs + db) * lanes for dcore, dx, db in ats]
            left = jnp.concatenate([turned[:, row : row + lanes] for row in rows], 1)
            total = total + dot(left, arrays[k][...], ((1,), (0,)))
    return total


def dense_kernel(held, xs, bs, lanes, n_held, place, *refs):
    arrays, refs = refs[:n_held], refs[n_held:]
    turned, first, out_grad, act, left_ref, right_ref = refs[:6]
    backs, [back] = refs[6 : 6 + CHUNKS], refs[6 + CHUNKS :]
    b, x, core = place[1], place[2], place[3]
    half, group = out_grad.shape[1] // 2, bs * lanes
    others = {at: (k - n_held // 2, row) for at, (k, row) in held.items() if at[0]}
    for h, out in enumerate((left_ref, right_ref)):
        part = slice(h * half, (h + 1) * half)
        pre = first[:, part] + products(others, arrays[n_held // 2 :], turned, h, xs, bs, lanes)
        phi = 0.5 * (1.0 + lax.erf(pre * (0.5**0.5)))
        act[:, part] = (pre * phi).astype(LOW)
        slope = phi + pre * (jnp.exp(-0.5 * pre * pre) * 0.3989422804014327)
        out[...] = (out_grad[:, part].astype(F32) * slope).astype(LOW)
    found = {}
    for (h, k), ats in pieces_of(held).items():
        more = dot((left_ref, right_ref)[h][...], arrays[k][...], ((1,), (1,)))
        for i, at in enumerate(ats):
            part = more[:, i * lanes : (i + 1) * lanes]
            found[at] = found[at] + part if at in found else part
    for dcore in range(CORES):
        for dx in range(xs):
            row = lax.rem(x + dx, xs) * CORES + lax.rem(core + dcore, CORES)
            part = together(found[dcore, dx, 0], found[dcore, dx, 1], b)
            back[:, pl.ds(pl.multiple_of(row * group, group), group)] = part.astype(LOW)
    for k, (start, end) in enumerate(bounds(out_grad.shape[1])):
        backs[k][...] = back[:, start:end]


def rows_kernel(xs, bs, lanes, turned, *outs):
    for dx, out in enumerate(outs):
        for dcore in range(CORES):
            for db in range(bs):
                row = ((dcore * xs + dx) * bs + db) * lanes
                to = (db * CORES + dcore) * lanes
                out[:, to : to + lanes] = turned[:, row : row + lanes]


def pick_kernel(db, *refs):
    *refs, out = refs
    lefts, rows = refs[: len(refs) // 2], refs[len(refs) // 2 :]
    size, half = lefts[0].shape
    wide = out.shape[1] - half
    for i, (left, row) in enumerate(zip(lefts, rows)):
        at = slice(i * size, (i + 1) * size)
        out[at, :half] = left[...]
        out[at, half:] = row[:, db * wide : (db + 1) * wide]


def spread(at, lanes, left, right, rows, gate):
    size, half = left.shape
    lefts = [left] + [at.send(left, dx=dx) for dx in range(1, at.xs)]
    rows = rows[:1] + [at.send(row, dx=dx) for dx, row in enumerate(rows[1:], 1)]
    rights = [right] + [at.send(right, db=db) for db in range(1, at.bs)]
    steps = [lefts[1:] + rights[1:] + rows[1:]]

    def pick(db):
        outs = [like(at.xs * size, half + CORES * lanes)]
        return call(functools.partial(pick_kernel, db), outs, [], after(left, gate), *lefts[1:], *rows)[0]

    held = {}

    def keep(k, place, row):
        held[place] = (k, row)

    arrays = [pick(0), join(after(right, gate), *rights[1:])]
    for dx in range(at.xs):
        keep(0, (-dx % at.xs, 0, 0), dx * size)
    for db in range(at.bs):
        keep(1, (0, -db % at.bs, 1), db * size)
    for db in range(1, at.bs):
        arrays.append(at.send(pick(db), db=db))
        for dx in range(at.xs):
            keep(len(arrays) - 1, (-dx % at.xs, -db % at.bs, 0), dx * size)
    for dx in range(1, at.xs):
        arrays.append(at.send(arrays[1], dx=dx))
        for db in range(at.bs):
            keep(len(arrays) - 1, (-dx % at.xs, -db % at.bs, 1), db * size)
    return arrays, held, steps + [arrays[2:]]


def grad_kernel(held, xs, bs, lanes, dcore, n_arrays, place, *refs):
    arrays, (*outs, left, right, product, sums_ref) = refs[:n_arrays], refs[n_arrays:]
    a, b, x, core = (place[i] for i in range(4))
    size, width = left.shape[0] // (xs * bs), right.shape[1]
    half, count, group = width // 2, lanes // LINE, bs * lanes
    for n, (dx, db) in enumerate((dx, db) for db in range(bs) for dx in range(xs)):
        rows = slice(n * size, (n + 1) * size)
        k, row = held[dx, db, 0]
        right[rows, :half] = arrays[k][row : row + size, :half]
        start = half + dcore * lanes
        left[rows, :] = arrays[k][row : row + size, start : start + lanes]
        k, row = held[dx, db, 1]
        right[rows, half:] = arrays[k][row : row + size, :]
    product[:, :width] = dot(left[...], right[...], ((0,), (0,)))
    total = jnp.sum(right[...].astype(F32), 0, keepdims=True)
    sums_ref[...] = jnp.broadcast_to(total, sums_ref.shape)
    row = x * CORES + lax.rem(core + dcore, CORES)
    own = sums_ref[0:1, pl.ds(pl.multiple_of(row * group, group), group)]
    at_row = lax.broadcasted_iota(jnp.int32, (lanes, group), 0)
    at_lane = lax.broadcasted_iota(jnp.int32, (lanes, group), 1)
    source = (at_row // count) * (bs * count) + b * count + at_row % count
    column = jnp.sum(jnp.where(at_lane == source, own, 0.0), 1, keepdims=True)
    product[:, width:] = jnp.broadcast_to(column, (lanes, 128))
    if dcore:
        [out] = outs
        out[:, :width] = product[:, :width].astype(LOW)
        out[:, width:] = two_parts(product[:, width:])
        return
    got, outs = outs[0], outs[1:]
    for out, flip in zip(outs, ORDER):
        rows = pl.ds(pl.multiple_of((a ^ flip) * count, count), count)
        tail = got[rows, width:].astype(F32)
        tail = product[rows, width:] + (tail[:, 0:1] + tail[:, 1:2])
        out[:, :width] = (product[rows, :width] + got[rows, :width].astype(F32)).astype(out.dtype)
        out[:, width : width + 128] = two_parts(tail) if out.dtype == LOW else tail


def two_parts(value):
    high = value.astype(LOW)
    rest = (value - high.astype(F32)).astype(LOW)
    lane = lax.broadcasted_iota(jnp.int32, value.shape, 1)
    return jnp.where(lane == 0, high.astype(F32), jnp.where(lane == 1, rest.astype(F32), 0.0)).astype(LOW)


def fold_kernel(kept, got, far):
    width = got.shape[1] - 128
    tail = got[:, width:].astype(F32)
    far[:, :width] = (kept[:, :width] + got[:, :width].astype(F32)).astype(LOW)
    far[:, width : width + 128] = two_parts(kept[:, width : width + 128] + (tail[:, 0:1] + tail[:, 1:2]))


def last_fold_kernel(kept, *refs):
    *arrived, weight_out, bias_out = refs
    width = weight_out.shape[1]
    total, tail = kept[:, :width], kept[:, width : width + 128]
    for got in arrived:
        total = total + got[:, :width].astype(F32)
        rest = got[:, width : width + 128].astype(F32)
        tail = tail + (rest[:, 0:1] + rest[:, 1:2])
    weight_out[...] = total
    bias_out[...] = jnp.transpose(tail)[0:1, :]


def far_kernel(kept, got, far):
    far[...] = (kept[...] + got[...].astype(F32)).astype(LOW)


def shards(node_feats, block_vals, block_cols, block_counts, self_weight, weight, bias, out_grad):
    at = Place()
    size, width = node_feats.shape
    own_rows = weight.shape[0]
    lanes = LINE * own_rows
    aligned = own_rows * at.bs == 128
    ops, gate, arrived = operator(at, block_vals, block_cols, block_counts, self_weight, size)
    own = {(dx, db): at.send(node_feats, dx=-dx, db=-db) if dx or db else node_feats for dx, db in at.chips}
    halves = line_weight(at, weight, *arrived) if aligned else []
    first, *chips = at.chips
    across = [at.send(own[first], dcore=1), at.send(join(after(own[chips[0]], *halves), *[own[chip] for chip in chips[1:]]), dcore=1)]
    total, kept, to_near, to_last = sums(at, ops, own, across)
    got = at.send(to_last, flip=1)
    near = at.send(to_near, flip=1)
    [far] = call(far_kernel, [like(size, width)], [], kept, got)
    far = at.send(far, flip=2)

    if not aligned:
        return plain_rest(at, ops, total + near.astype(F32) + far.astype(F32), weight, bias, out_grad)
    halves = [after(half, *own.values(), *ops[-1]) for half in halves]
    arrays, held, steps = gathered_halves(at, halves, to_last)
    early = len(arrays) - len(steps[1])
    arrays, held = both_cores(at, arrays, held, [[]] * early + [[near, far]] * len(steps[1]))
    widths = [end - start for start, end in bounds(width)]
    own_held = {at: where for at, where in held.items() if not at[0]}
    count = len(arrays) // 2
    turned, pre = call(
        functools.partial(first_dense_kernel, own_held, at.xs, at.bs, lanes, count),
        [like(size, width), like(size, width, kind=F32)],
        [pltpu.VMEM((size, width), F32)],
        at.numbers,
        *arrays[:count],
        total,
        near,
        far,
        bias[None, :],
        numbers=1,
    )
    activations, left, right, *backs = call(
        functools.partial(dense_kernel, held, at.xs, at.bs, lanes, len(arrays)),
        [like(size, width)] + [like(size, width // 2)] * 2 + [like(size, wide) for wide in widths],
        [pltpu.VMEM((size, width), LOW)],
        at.numbers,
        *arrays,
        turned,
        pre,
        out_grad,
        numbers=1,
    )
    kernel = functools.partial(rows_kernel, at.xs, at.bs, lanes)
    rows = list(call(kernel, [like(size, at.bs * CORES * lanes)] * at.xs, [], turned))

    fars = [at.send(backs[0], flip=2)]
    arrays, held, steps = spread(at, lanes, left, right, rows, fars[0])
    nears = [at.send(join(backs[0], fars[0]), flip=1)]
    for k in range(1, CHUNKS):
        fars.append(at.send(after(backs[k], *fars, *steps[0]), flip=2))
        nears.append(at.send(join(backs[k], fars[k]), flip=1))
    feat, parts = feat_sums(at, ops, backs[0], fars[0], after(nears[0], *fars, *steps[1]))
    gates = feat[1:]
    wide, long = width + 128, width + 256
    scratch = [
        pltpu.VMEM((size * len(at.chips), lanes), LOW),
        pltpu.VMEM((size * len(at.chips), width), LOW),
        pltpu.VMEM((lanes, wide), F32),
        pltpu.VMEM((8, width), F32),
    ]
    kernel = functools.partial(grad_kernel, held, at.xs, at.bs, lanes)
    [across] = call(
        functools.partial(kernel, 1, len(arrays)), [like(lanes, wide)], scratch, at.numbers, *arrays, numbers=1
    )
    got = at.send(across, dcore=1)
    outs = [like(own_rows, wide, kind=F32)] * 2 + [like(own_rows, long), like(own_rows, wide)]
    total, kept, to_near, to_last = call(
        functools.partial(kernel, 0, len(arrays)), outs, scratch, at.numbers, *arrays, got, numbers=1
    )
    got = at.send(to_last, flip=1)
    [sent] = call(fold_kernel, [like(own_rows, long)], [], kept, got)
    for k in range(1, CHUNKS):
        more, parts = feat_sums(at, ops, backs[k], fars[k], after(nears[k], sent, *parts, *gates))
        feat = feat + more
    near = at.send(to_near, flip=1)
    far = at.send(sent, flip=2)
    [feat_grad] = call(functools.partial(add_up_kernel, CHUNKS), [like(size, width, kind=F32)], [], *feat)
    outs = [like(own_rows, width, kind=F32), like(1, own_rows, kind=F32)]
    weight_grad, bias_grad = call(last_fold_kernel, outs, [], after(total, feat_grad), near, far)
    return activations, feat_grad, weight_grad, bias_grad[0]


def feat_sums(at, ops, *lines):
    size, chunk = lines[0].shape
    rows = len(at.chips) * size
    kernel = functools.partial(back_kernel, len(ops))
    [across] = call(kernel, [like(rows, chunk)], [], *[pair[1] for pair in ops], *lines)
    got = at.send(across, dcore=1)
    outs = [like(size, chunk, kind=F32)] + [like(size, chunk)] * (len(at.chips) - 1)
    parts = call(kernel, outs, [], *[pair[0] for pair in ops], *lines, got)
    sent = [at.send(part, dx=dx, db=db) for part, (dx, db) in zip(parts[1:], at.chips[1:])]
    return [parts[0]] + sent, parts


def plain_rest(at, ops, agg, weight, bias, out_grad):
    size, width = out_grad.shape
    own_rows = weight.shape[0]
    lanes = LINE * own_rows
    agg = agg.astype(LOW)
    whole_weight = lax.all_gather(weight, AXES, axis=0, tiled=True)
    pre = dot(agg, whole_weight, ((1,), (0,))) + bias[None, :]
    phi = 0.5 * (1.0 + lax.erf(pre * (0.5**0.5)))
    activations = (pre * phi).astype(LOW)
    slope = phi + pre * (jnp.exp(-0.5 * pre * pre) * 0.3989422804014327)
    pre_low = (out_grad.astype(F32) * slope).astype(LOW)
    feat = []
    for start, end in bounds(width):
        back = dot(pre_low, whole_weight[start:end], ((1,), (1,))).astype(LOW)
        far = at.send(back, flip=2)
        feat = feat + feat_sums(at, ops, back, far, at.send(join(back, far), flip=1))[0]
    [feat_grad] = call(functools.partial(add_up_kernel, CHUNKS), [like(size, width, kind=F32)], [], *feat)

    groups = agg.reshape(size, at.rows, LINE, at.bs, own_rows)
    groups = jnp.concatenate([lax.dynamic_slice_in_dim(groups, at.a ^ flip, 1, 2) for flip in ORDER], 2)
    messages = []
    for dx, db in at.chips:
        dest_x = (at.x + dx) % at.xs
        wide = one_of(groups, (at.b + db) % at.bs, 3)
        picked = [
            one_of(wide, dest_x * CORES + (at.core + dcore) % CORES, 1).reshape(size, lanes) for dcore in range(CORES)
        ]
        message = jnp.concatenate([pre_low] + picked, 1)
        messages.append(at.send(message, dx=dx, db=db) if dx or db else message)
    own = jnp.concatenate(messages)
    other = at.send(own, dcore=1)
    weight_part = dot(own[:, width : width + lanes], own[:, :width], ((0,), (0,)))
    weight_part = weight_part + dot(other[:, width + lanes :], other[:, :width], ((0,), (0,)))
    bias_part = jnp.sum(own[:, :width].astype(F32), 0) + jnp.sum(other[:, :width].astype(F32), 0)
    bias_part = one_of(one_of(bias_part.reshape(at.rows, LINE, at.bs, own_rows), at.row, 0), at.b, 1)
    bias_part = jnp.concatenate([one_of(bias_part, at.a ^ flip, 0) for flip in ORDER])
    near = at.send(weight_part[2 * own_rows :].astype(LOW), flip=1).astype(F32)
    kept = weight_part[: 2 * own_rows] + near
    far = at.send(kept[own_rows:].astype(LOW), flip=2).astype(F32)
    near_bias = at.send(bias_part[2 * own_rows :], flip=1)
    kept_bias = bias_part[: 2 * own_rows] + near_bias
    bias_grad = kept_bias[:own_rows] + at.send(kept_bias[own_rows:], flip=2)
    return activations, feat_grad, kept[:own_rows] + far, bias_grad


def solution(mesh):
    placed = (
        P(("col", "row"), None),
        P("row", "col"),
        P("col", "row"),
        P("col", "row"),
        P("row"),
        P(("row", "col"), None),
        P(),
        P(("row", "col"), None),
    )
    return jax.shard_map(
        shards,
        mesh=mesh,
        in_specs=placed,
        out_specs=(
            P(("row", "col"), None),
            P(("col", "row"), None),
            P(("row", "col"), None),
            P(("row", "col")),
        ),
        check_vma=False,
    )
```

```python
import functools
import math

import jax
import jax.numpy as jnp
from jax import lax
from jax.experimental import pallas as pl
from jax.experimental.pallas import tpu as pltpu
from jax.sharding import PartitionSpec as P

boost = 2.0
AXES = ("row", "col")
CORES = 2
LINE = 4
ORDER = (0, 2, 1, 3)
CUTS = (0, 9, 16)
CHUNKS = len(CUTS) - 1
PINS = {
    "weight_core1": ("operator",),
    "features_join": ("operator", "weight_near", "weight_last"),
    "weight_halves": ("features", "operator", "weight_near"),
    "weight_join1": ("sums",),
    "weight_join2": ("sums",),
    "weight_core2": ("sum_near", "sum_far", "sum_last"),
    "pick": ("far0",),
    "join_right": ("far0",),
    "far1": ("far0", "left", "rows", "right"),
    "across0": ("far1", "left2", "right2"),
    "grad_far": ("left2",),
    "across1": ("grad_fold", "feat0"),
    "add": ("grad",),
}
NEAR_PAD, FAR_PAD, LAST_PAD = 256, 256, 128
LOW = jnp.bfloat16
F32 = jnp.float32


def dot(left, right, dims):
    return lax.dot_general(left, right, ((dims[0], dims[1]), ((), ())), preferred_element_type=F32)


def after(value, *others):
    return lax.optimization_barrier((value, *others))[0]


def one_of(value, index, axis):
    return lax.dynamic_index_in_dim(value, index, axis, keepdims=False)


def call(kernel, outs, scratch, *operands, numbers=0, outside=0, alone=False):
    whole = pl.BlockSpec(memory_space=pltpu.VMEM)
    specs = [pl.BlockSpec(memory_space=pltpu.SMEM)] * numbers + [pl.BlockSpec(memory_space=pltpu.HBM)] * outside
    specs += [whole] * (len(operands) - len(specs))
    arrays = [v for v in [*operands[numbers:], *outs, *scratch] if hasattr(v.dtype, "itemsize")]
    need = sum(math.prod(v.shape) * v.dtype.itemsize for v in arrays)
    need = 60 * 2**20 if alone else min(need + 6 * 2**20, 60 * 2**20)
    return pl.pallas_call(
        kernel,
        out_shape=outs,
        in_specs=specs,
        out_specs=[whole] * len(outs),
        scratch_shapes=scratch,
        compiler_params=pltpu.CompilerParams(vmem_limit_bytes=need),
        cost_estimate=pl.CostEstimate(flops=1, bytes_accessed=1, transcendentals=0),
    )(*operands)


def like(*shape, kind=LOW):
    return jax.ShapeDtypeStruct(shape, kind)


def bounds(width):
    return [(low * width // CUTS[-1], high * width // CUTS[-1]) for low, high in zip(CUTS, CUTS[1:])]


def join_kernel(pieces, *refs):
    out, row = refs[-1], 0
    for k, start, rows in pieces:
        out[row : row + rows, :] = refs[k][start : start + rows, :]
        row += rows


def join(*pieces):
    pieces = [piece if isinstance(piece, tuple) else (piece, 0, piece.shape[0]) for piece in pieces]
    arrays = list({id(piece[0]): piece[0] for piece in pieces}.values())
    order = {id(array): k for k, array in enumerate(arrays)}
    rows = sum(piece[2] for piece in pieces)
    places = [(order[id(array)], start, count) for array, start, count in pieces]
    return call(functools.partial(join_kernel, places), [like(rows, arrays[0].shape[1])], [], *arrays)[0]


def bounds(width):
    return [(low * width // CUTS[-1], high * width // CUTS[-1]) for low, high in zip(CUTS, CUTS[1:])]


def like(*shape, kind=LOW):
    return jax.ShapeDtypeStruct(shape, kind)


class Place:
    def __init__(self):
        self.rows = lax.axis_size("row")
        self.cols = lax.axis_size("col")
        self.xs = self.rows // CORES
        self.bs = self.cols // LINE
        self.row = lax.axis_index("row")
        self.col = lax.axis_index("col")
        self.x = self.row // CORES
        self.core = self.row % CORES
        self.a = self.col // self.bs
        self.b = self.col % self.bs
        self.chips = [(dx, db) for db in range(self.bs) for dx in range(self.xs)]
        self.numbers = jnp.stack([self.a, self.b, self.x, self.core]).astype(jnp.int32)
        self.tokens = {}

    def token(self, name, value):
        self.tokens[name] = value if isinstance(value, (list, tuple)) else [value]
        return value

    def gate(self, name, value):
        others = [array for step in PINS.get(name, ()) for array in self.tokens.get(step, ())]
        return after(value, *others) if others else value

    def index(self, x, core, a, b):
        return ((x % self.xs) * CORES + core % CORES) * self.cols + (a % LINE) * self.bs + b % self.bs

    def send(self, value, dx=0, dcore=0, db=0, flip=0):
        pairs = [
            (self.index(x, core, a, b), self.index(x + dx, core + dcore, a ^ flip, b + db))
            for x in range(self.xs)
            for core in range(CORES)
            for a in range(LINE)
            for b in range(self.bs)
        ]
        return lax.ppermute(value, AXES, pairs)


def put_blocks(xs, bs, place, weights, part, mask, db, outs):
    a, b, x, core = (place[i] for i in range(4))
    size = weights.shape[1]
    rows = xs * CORES
    eye = (
        lax.broadcasted_iota(jnp.int32, (size, size), 0) == lax.broadcasted_iota(jnp.int32, (size, size), 1)
    ).astype(F32)
    tile = lax.rem(b + db, bs)
    for k, flip in enumerate(ORDER):
        line = (a ^ flip) * bs + b
        row_block = (x * CORES + core) * (LINE * bs) + line
        diagonal = eye * (boost * weights[pl.ds(line, 1), :])
        values = part(k)
        for dcore in range(CORES):
            for dx in range(xs):
                block = lax.rem(x + dx, xs) * CORES + lax.rem(core + dcore, CORES)
                node_block = a * (bs * rows) + tile * rows + block
                total = diagonal * (row_block == node_block).astype(F32)
                for slot in range(values.shape[1] // size):
                    total = total + values[:, slot * size : (slot + 1) * size] * mask(k, slot, block)
                outs[dcore][k * size : (k + 1) * size, dx * size : (dx + 1) * size] = total.astype(LOW)


def own_blocks_kernel(xs, bs, slots, place, *refs):
    held, outs, scratch, sems = refs[:4], refs[4:-5], refs[-5:-1], refs[-1]
    copies = [pltpu.make_async_copy(held[i], scratch[i], sems.at[i]) for i in range(4)]
    for copy in copies:
        copy.start()
    for copy in copies:
        copy.wait()
    cols, counts, block_vals, weights = scratch
    a, b = place[0], place[1]
    size = weights.shape[1]

    def line(k, dest):
        return (a ^ ORDER[k]) * bs + dest

    def rows(k, dest):
        return block_vals[pl.ds(pl.multiple_of(line(k, dest) * size, size), size), :]

    def column(k, slot, dest):
        at = line(k, dest)
        return jnp.where(slot < counts[0, at], cols[slot, at], -1)

    for db in range(1, bs):
        out = outs[CORES + db - 1]
        dest = lax.rem(b - db + bs, bs)
        for k in range(LINE):
            out[k * size : (k + 1) * size, :] = rows(k, dest)
        at_row = lax.broadcasted_iota(jnp.int32, (16, slots * size), 0)
        head = jnp.zeros((16, slots * size), jnp.int32)
        for k in range(LINE):
            for slot in range(slots):
                head = jnp.where(at_row == k * slots + slot, column(k, slot, dest), head)
        out[LINE * size :, :] = head.astype(F32).astype(LOW)
    put_blocks(
        xs,
        bs,
        place,
        weights,
        lambda k: rows(k, b).astype(F32),
        lambda k, slot, block: (column(k, slot, b) == block).astype(F32),
        0,
        outs[:CORES],
    )


def sent_blocks_kernel(xs, bs, slots, db, place, got, weights, *outs):
    size = weights.shape[1]
    head = got[LINE * size :, :].astype(F32)

    def mask(k, slot, block):
        at = k * slots + slot
        return (head[at : at + 1, :size] == block.astype(F32)).astype(F32)

    put_blocks(
        xs, bs, place, weights, lambda k: got[k * size : (k + 1) * size, :].astype(F32), mask, db, outs
    )


def operator(at, block_vals, block_cols, block_counts, self_weight, size):
    slots = block_cols.shape[0]
    weights = self_weight.reshape(-1, size)
    dense = like(LINE * size, at.xs * size)
    own, other, *sent = call(
        functools.partial(own_blocks_kernel, at.xs, at.bs, slots),
        [dense] * CORES + [like(LINE * size + 16, slots * size)] * (at.bs - 1),
        [
            pltpu.SMEM(block_cols.shape, jnp.int32),
            pltpu.SMEM(block_counts.shape, jnp.int32),
            pltpu.VMEM(block_vals.shape, block_vals.dtype),
            pltpu.VMEM(weights.shape, weights.dtype),
            pltpu.SemaphoreType.DMA((4,)),
        ],
        at.numbers,
        block_cols,
        block_counts,
        at.gate("blocks", block_vals),
        weights,
        numbers=1,
        outside=4,
        alone=True,
    )
    result = [[own, other]]
    arrived = at.token("blocks", [at.send(value, db=-db) for db, value in enumerate(sent, 1)])
    for db, got in enumerate(arrived, 1):
        kernel = functools.partial(sent_blocks_kernel, at.xs, at.bs, slots, db)
        got = at.gate("operator", got)
        result.append(call(kernel, [dense] * CORES, [], at.numbers, got, weights, numbers=1))
    at.token("operator", result[-1])
    return result


def sums_kernel(n_ops, pieces, *refs):
    ops, arrays, (*outs, left, right) = refs[:n_ops], refs[n_ops:-6], refs[-6:]
    size, wide = outs[0].shape[0], ops[0].shape[1]
    for i, op in enumerate(ops):
        left[:, i * wide : (i + 1) * wide] = op[...]
    for i, (k, row) in enumerate(pieces):
        right[i * size : (i + 1) * size, :] = arrays[k][row : row + size, :]
    step = right.shape[1] // 4
    for k in range(4):
        columns = slice(k * step, (k + 1) * step)
        part = dot(left[...], right[:, columns], ((1,), (0,)))
        for i, out in enumerate(outs):
            out[:, columns] = part[i * size : (i + 1) * size].astype(out.dtype)


def sums(at, ops, own, across):
    size, width = own[0, 0].shape
    arrays = [*own.values(), *across]
    pieces = []
    for db in range(at.bs):
        pieces += [(db * at.xs + dx, 0) for dx in range(at.xs)]
        pieces += [(len(own) + 1, (db * at.xs + dx - 1) * size) if db or dx else (len(own), 0) for dx in range(at.xs)]
    rows, depth = LINE * size, len(pieces) * size
    return call(
        functools.partial(sums_kernel, CORES * at.bs, pieces),
        [like(size, width, kind=F32)] * 2 + [like(size, width)] * 2,
        [pltpu.VMEM((rows, depth), LOW), pltpu.VMEM((depth, width), LOW)],
        *[op for pair in ops for op in pair],
        *arrays,
    )


def back_kernel(n_ops, *refs):
    ops, lines, rest = refs[:n_ops], refs[n_ops : n_ops + 3], refs[n_ops + 3 :]
    right = jnp.concatenate([line[...] for line in lines], 0)
    parts = [dot(op[...], right, ((0,), (0,))) for op in ops]
    if len(rest) == 1:
        rows = parts[0].shape[0]
        for i, part in enumerate(parts):
            rest[0][i * rows : (i + 1) * rows, :] = part.astype(LOW)
        return
    got, outs = rest[0], rest[1:]
    size = outs[0].shape[0]
    per = parts[0].shape[0] // size
    for i, out in enumerate(outs):
        k = i % per * size
        total = parts[i // per][k : k + size] + got[i * size : (i + 1) * size, :].astype(F32)
        out[...] = total.astype(out.dtype)


def add_up_kernel(n_keeps, *refs):
    *parts, out = refs
    per = len(parts) // n_keeps
    for k, (start, end) in enumerate(bounds(out.shape[1])):
        total = parts[k * per][...]
        for part in parts[k * per + 1 : (k + 1) * per]:
            total = total + part[...].astype(F32)
        out[:, start:end] = total


def along_x(at, value):
    return [value] + [at.send(value, dx=-dx) for dx in range(1, at.xs)]


def along_b(at, value):
    return [value] + [at.send(value, db=-db) for db in range(1, at.bs)]


def gathered_halves(at, halves):
    rows = halves[0].shape[0]
    left, right = along_x(at, halves[0]), along_b(at, halves[1])
    at.token("weight_step1", left[1:] + right[1:])
    lefts = [at.gate("weight_join1", left[0]), *left[1:]]
    rights = [at.gate("weight_join2", right[0]), *right[1:]]
    arrays, held = [at.token("weight_join1", join(*lefts)), at.token("weight_join2", join(*rights))], {}
    for dx in range(at.xs):
        held[dx, 0, 0] = (0, dx * rows)
    for db in range(at.bs):
        held[0, db, 1] = (1, db * rows)
    left, right = arrays
    for db in range(1, at.bs):
        arrays.append(at.send(left, db=-db))
        for dx in range(at.xs):
            held[dx, db, 0] = (len(arrays) - 1, dx * rows)
    for dx in range(1, at.xs):
        arrays.append(at.send(right, dx=-dx))
        for db in range(at.bs):
            held[dx, db, 1] = (len(arrays) - 1, db * rows)
    at.token("weight_step2", arrays[2:])
    return arrays, held


def both_cores(at, arrays, held):
    count = len(arrays)
    across = [at.send(at.gate("weight_core1", value), dcore=1) for value in arrays[:2]]
    at.token("weight_core1", across)
    across += [at.send(at.gate("weight_core2", value), dcore=1) for value in arrays[2:]]
    places = {(0, *place): at for place, at in held.items()}
    places.update({(1, *place): (k + count, i) for place, (k, i) in held.items()})
    return arrays + across, places


def line_kernel(place, weight, far, near, last, left, right):
    count, half = weight.shape[0], left.shape[1]
    for flip, source in zip(ORDER, (weight, far, near, last)):
        rows = pl.ds(pl.multiple_of((place[0] ^ flip) * count, count), count)
        left[rows, :] = source[:, :half]
        right[rows, :] = source[:, half:]


def line_weight(at, weight):
    count, width = weight.shape
    far = at.token("weight_far", at.send(at.gate("weight_far", weight), flip=2))
    near = at.token("weight_near", at.send(at.gate("weight_near", weight), flip=1))
    last = at.token("weight_last", at.send(at.gate("weight_last", far), flip=1))
    halves = [like(LINE * count, width // 2)] * 2
    last = at.gate("weight_line", last)
    return at.token("weight_line", call(line_kernel, halves, [], at.numbers, weight, far, near, last, numbers=1))


def turned_halves(value, swap):
    parts = [value[:, i : i + 128] for i in range(0, value.shape[1], 128)]
    return [jnp.where(swap, pltpu.roll(part, 64, 1), part) for part in parts]


def apart(value, b):
    parts = turned_halves(value, b == 1)
    left = lax.broadcasted_iota(jnp.int32, parts[0].shape, 1) < 64
    own, other = [], []
    for one, two in zip(parts[::2], parts[1::2]):
        own.append(jnp.where(left, one, pltpu.roll(two, 64, 1)))
        other.append(jnp.where(left, pltpu.roll(one, 64, 1), two))
    return jnp.concatenate(own, 1), jnp.concatenate(other, 1)


def together(own, other, b):
    parts = []
    left = lax.broadcasted_iota(jnp.int32, (own.shape[0], 128), 1) < 64
    for i in range(0, own.shape[1], 128):
        one, two = own[:, i : i + 128], other[:, i : i + 128]
        parts.append(jnp.where(left, one, pltpu.roll(two, 64, 1)))
        parts.append(jnp.where(left, pltpu.roll(one, 64, 1), two))
    return jnp.concatenate(turned_halves(jnp.concatenate(parts, 1), b == 1), 1)


def pieces_of(held):
    pieces = {}
    for (*at, h), (k, row) in sorted(held.items(), key=lambda item: item[1]):
        pieces.setdefault((h, k), []).append(tuple(at))
    return pieces


def first_dense_kernel(held, xs, bs, lanes, n_held, place, *refs):
    arrays, (total, near, far, bias, turned, pre, agg) = refs[:n_held], refs[n_held:]
    b, x, core = place[1], place[2], place[3]
    half, group = bias.shape[1] // 2, bs * lanes
    agg[...] = total[...] + near[...].astype(F32) + far[...].astype(F32)
    n = 0
    for dcore in range(CORES):
        for dx in range(xs):
            row = lax.rem(x + dx, xs) * CORES + lax.rem(core + dcore, CORES)
            for part in apart(agg[:, pl.ds(pl.multiple_of(row * group, group), group)], b):
                turned[:, n * lanes : (n + 1) * lanes] = part.astype(LOW)
                n += 1
    for h in range(2):
        part = slice(h * half, (h + 1) * half)
        pre[:, part] = products(held, arrays, turned, h, xs, bs, lanes) + bias[:, part]


def products(held, arrays, turned, h, xs, bs, lanes):
    total = 0.0
    for (side, k), ats in pieces_of(held).items():
        if side == h and k < len(arrays):
            rows = [((dcore * xs + dx) * bs + db) * lanes for dcore, dx, db in ats]
            left = jnp.concatenate([turned[:, row : row + lanes] for row in rows], 1)
            total = total + dot(left, arrays[k][...], ((1,), (0,)))
    return total


def dense_kernel(held, xs, bs, lanes, n_held, place, *refs):
    arrays, refs = refs[:n_held], refs[n_held:]
    turned, first, out_grad, act, left_ref, right_ref = refs[:6]
    backs, [back] = refs[6 : 6 + CHUNKS], refs[6 + CHUNKS :]
    b, x, core = place[1], place[2], place[3]
    half, group = out_grad.shape[1] // 2, bs * lanes
    others = {at: (k - n_held // 2, row) for at, (k, row) in held.items() if at[0]}
    for h, out in enumerate((left_ref, right_ref)):
        part = slice(h * half, (h + 1) * half)
        pre = first[:, part] + products(others, arrays[n_held // 2 :], turned, h, xs, bs, lanes)
        phi = 0.5 * (1.0 + lax.erf(pre * (0.5**0.5)))
        act[:, part] = (pre * phi).astype(LOW)
        slope = phi + pre * (jnp.exp(-0.5 * pre * pre) * 0.3989422804014327)
        out[...] = (out_grad[:, part].astype(F32) * slope).astype(LOW)
    found = {}
    for (h, k), ats in pieces_of(held).items():
        more = dot((left_ref, right_ref)[h][...], arrays[k][...], ((1,), (1,)))
        for i, at in enumerate(ats):
            part = more[:, i * lanes : (i + 1) * lanes]
            found[at] = found[at] + part if at in found else part
    for dcore in range(CORES):
        for dx in range(xs):
            row = lax.rem(x + dx, xs) * CORES + lax.rem(core + dcore, CORES)
            part = together(found[dcore, dx, 0], found[dcore, dx, 1], b)
            back[:, pl.ds(pl.multiple_of(row * group, group), group)] = part.astype(LOW)
    for k, (start, end) in enumerate(bounds(out_grad.shape[1])):
        backs[k][...] = back[:, start:end]


def rows_kernel(xs, bs, lanes, turned, *outs):
    for dx, out in enumerate(outs):
        for dcore in range(CORES):
            for db in range(bs):
                row = ((dcore * xs + dx) * bs + db) * lanes
                to = (db * CORES + dcore) * lanes
                out[:, to : to + lanes] = turned[:, row : row + lanes]


def pick_kernel(db, *refs):
    *refs, out = refs
    lefts, rows = refs[: len(refs) // 2], refs[len(refs) // 2 :]
    size, half = lefts[0].shape
    wide = out.shape[1] - half
    for i, (left, row) in enumerate(zip(lefts, rows)):
        at = slice(i * size, (i + 1) * size)
        out[at, :half] = left[...]
        out[at, half:] = row[:, db * wide : (db + 1) * wide]


def spread(at, lanes, left, right, rows):
    size, half = left.shape
    lefts = [left] + [at.send(at.gate("left", left), dx=dx) for dx in range(1, at.xs)]
    rows = rows[:1] + [at.send(at.gate("rows", row), dx=dx) for dx, row in enumerate(rows[1:], 1)]
    rights = [right] + [at.send(at.gate("right", right), db=db) for db in range(1, at.bs)]
    at.token("left", lefts[1:])
    at.token("rows", rows[1:])
    at.token("right", rights[1:])

    def pick(db):
        outs = [like(at.xs * size, half + CORES * lanes)]
        refs = [at.gate("pick", left), *lefts[1:], *rows]
        return call(functools.partial(pick_kernel, db), outs, [], *refs)[0]

    held = {}

    def keep(k, place, row):
        held[place] = (k, row)

    arrays = [pick(0), join(at.gate("join_right", right), *rights[1:])]
    for dx in range(at.xs):
        keep(0, (-dx % at.xs, 0, 0), dx * size)
    for db in range(at.bs):
        keep(1, (0, -db % at.bs, 1), db * size)
    for db in range(1, at.bs):
        arrays.append(at.send(pick(db), db=db))
        for dx in range(at.xs):
            keep(len(arrays) - 1, (-dx % at.xs, -db % at.bs, 0), dx * size)
    for dx in range(1, at.xs):
        arrays.append(at.send(arrays[1], dx=dx))
        for db in range(at.bs):
            keep(len(arrays) - 1, (-dx % at.xs, -db % at.bs, 1), db * size)
    at.token("left2", arrays[2 : 1 + at.bs])
    at.token("right2", arrays[1 + at.bs :])
    return arrays, held


def grad_kernel(held, xs, bs, lanes, dcore, n_arrays, place, *refs):
    arrays, (*outs, left, right, product, sums_ref) = refs[:n_arrays], refs[n_arrays:]
    a, b, x, core = (place[i] for i in range(4))
    size, width = left.shape[0] // (xs * bs), right.shape[1]
    half, count, group = width // 2, lanes // LINE, bs * lanes
    for n, (dx, db) in enumerate((dx, db) for db in range(bs) for dx in range(xs)):
        rows = slice(n * size, (n + 1) * size)
        k, row = held[dx, db, 0]
        right[rows, :half] = arrays[k][row : row + size, :half]
        start = half + dcore * lanes
        left[rows, :] = arrays[k][row : row + size, start : start + lanes]
        k, row = held[dx, db, 1]
        right[rows, half:] = arrays[k][row : row + size, :]
    product[:, :width] = dot(left[...], right[...], ((0,), (0,)))
    total = jnp.sum(right[...].astype(F32), 0, keepdims=True)
    sums_ref[...] = jnp.broadcast_to(total, sums_ref.shape)
    row = x * CORES + lax.rem(core + dcore, CORES)
    own = sums_ref[0:1, pl.ds(pl.multiple_of(row * group, group), group)]
    at_row = lax.broadcasted_iota(jnp.int32, (lanes, group), 0)
    at_lane = lax.broadcasted_iota(jnp.int32, (lanes, group), 1)
    source = (at_row // count) * (bs * count) + b * count + at_row % count
    column = jnp.sum(jnp.where(at_lane == source, own, 0.0), 1, keepdims=True)
    product[:, width:] = jnp.broadcast_to(column, (lanes, 128))
    if dcore:
        [out] = outs
        out[:, :width] = product[:, :width].astype(LOW)
        out[:, width:] = two_parts(product[:, width:])
        return
    got, outs = outs[0], outs[1:]
    for out, flip in zip(outs, ORDER):
        rows = pl.ds(pl.multiple_of((a ^ flip) * count, count), count)
        tail = got[rows, width:].astype(F32)
        tail = product[rows, width:] + (tail[:, 0:1] + tail[:, 1:2])
        out[:, :width] = (product[rows, :width] + got[rows, :width].astype(F32)).astype(out.dtype)
        out[:, width : width + 128] = two_parts(tail) if out.dtype == LOW else tail


def two_parts(value):
    high = value.astype(LOW)
    rest = (value - high.astype(F32)).astype(LOW)
    lane = lax.broadcasted_iota(jnp.int32, value.shape, 1)
    return jnp.where(lane == 0, high.astype(F32), jnp.where(lane == 1, rest.astype(F32), 0.0)).astype(LOW)


def fold_kernel(kept, got, far):
    width = kept.shape[1] - 128
    tail = got[:, width : width + 128].astype(F32)
    far[:, :width] = (kept[:, :width] + got[:, :width].astype(F32)).astype(LOW)
    far[:, width : width + 128] = two_parts(kept[:, width : width + 128] + (tail[:, 0:1] + tail[:, 1:2]))


def last_fold_kernel(kept, *refs):
    *arrived, weight_out, bias_out = refs
    width = weight_out.shape[1]
    total, tail = kept[:, :width], kept[:, width : width + 128]
    for got in arrived:
        total = total + got[:, :width].astype(F32)
        rest = got[:, width : width + 128].astype(F32)
        tail = tail + (rest[:, 0:1] + rest[:, 1:2])
    weight_out[...] = total
    bias_out[...] = jnp.transpose(tail)[0:1, :]


def far_kernel(kept, got, far):
    far[...] = (kept[...] + got[...].astype(F32)).astype(LOW)


def shards(node_feats, block_vals, block_cols, block_counts, self_weight, weight, bias, out_grad):
    at = Place()
    size, width = node_feats.shape
    own_rows = weight.shape[0]
    lanes = LINE * own_rows
    aligned = own_rows * at.bs == 128
    halves = line_weight(at, weight) if aligned else []
    first, *chips = at.chips
    own = {first: node_feats}
    for dx, db in chips:
        own[dx, db] = at.send(at.gate("features", node_feats), dx=-dx, db=-db)
    at.token("features", [own[chip] for chip in chips])
    ops = operator(at, block_vals, block_cols, block_counts, self_weight, size)
    others = at.token("features_join", join(at.gate("features_join", own[chips[0]]), *[own[chip] for chip in chips[1:]]))
    across = [at.send(node_feats, dcore=1), at.send(others, dcore=1)]
    across[0] = at.gate("sums", across[0])
    total, kept, to_near, to_last = at.token("sums", sums(at, ops, own, across))
    got = at.token("sum_last", at.send(to_last, flip=1))
    [far] = at.token("sum_fold", call(far_kernel, [like(size, width)], [], kept, at.gate("sum_fold", got)))
    near = at.token("sum_near", at.send(at.gate("sum_near", to_near), flip=1))
    far = at.token("sum_far", at.send(far, flip=2))

    if not aligned:
        return plain_rest(at, ops, total + near.astype(F32) + far.astype(F32), weight, bias, out_grad)
    halves = [at.gate("weight_halves", half) for half in halves]
    arrays, held = gathered_halves(at, halves)
    arrays, held = both_cores(at, arrays, held)
    widths = [end - start for start, end in bounds(width)]
    own_held = {at: where for at, where in held.items() if not at[0]}
    count = len(arrays) // 2
    turned, pre = call(
        functools.partial(first_dense_kernel, own_held, at.xs, at.bs, lanes, count),
        [like(size, width), like(size, width, kind=F32)],
        [pltpu.VMEM((size, width), F32)],
        at.numbers,
        *arrays[:count],
        total,
        near,
        far,
        bias[None, :],
        numbers=1,
    )
    activations, left, right, *backs = call(
        functools.partial(dense_kernel, held, at.xs, at.bs, lanes, len(arrays)),
        [like(size, width)] + [like(size, width // 2)] * 2 + [like(size, wide) for wide in widths],
        [pltpu.VMEM((size, width), LOW)],
        at.numbers,
        *arrays,
        turned,
        pre,
        out_grad,
        numbers=1,
    )

    fars = [at.token("far0", at.send(backs[0], flip=2))]
    kernel = functools.partial(rows_kernel, at.xs, at.bs, lanes)
    rows = list(call(kernel, [like(size, at.bs * CORES * lanes)] * at.xs, [], at.gate("rows_kernel", turned)))
    arrays, held = spread(at, lanes, left, right, rows)
    nears = [at.token("near0", at.send(join(at.gate("near0", backs[0]), fars[0]), flip=1))]
    for k in range(1, CHUNKS):
        fars.append(at.token("far1", at.send(at.gate("far1", backs[k]), flip=2)))
        nears.append(at.token("near1", at.send(join(at.gate("near1", backs[k]), fars[k]), flip=1)))

    across0 = feat_across(at, ops, "0", backs[0], fars[0], nears[0])
    wide = width + 128
    scratch = [
        pltpu.VMEM((size * len(at.chips), lanes), LOW),
        pltpu.VMEM((size * len(at.chips), width), LOW),
        pltpu.VMEM((lanes, wide), F32),
        pltpu.VMEM((8, width), F32),
    ]
    kernel = functools.partial(grad_kernel, held, at.xs, at.bs, lanes)
    first = at.gate("grad_across", arrays[0])
    [across] = call(
        functools.partial(kernel, 1, len(arrays)), [like(lanes, wide)], scratch, at.numbers, first, *arrays[1:], numbers=1
    )
    at.token("grad_across", across)
    got = at.token("grad_core", at.send(across, dcore=1))
    feat = feat_own(at, ops, "0", across0, backs[0], fars[0], nears[0])
    outs = [like(own_rows, wide, kind=F32)] * 2 + [like(own_rows, width + NEAR_PAD), like(own_rows, width + LAST_PAD)]
    total, kept, to_near, to_last = call(
        functools.partial(kernel, 0, len(arrays)),
        outs,
        scratch,
        at.numbers,
        *arrays,
        at.gate("grad", got),
        numbers=1,
    )
    at.token("grad", to_last)
    got = at.token("grad_last", at.send(to_last, flip=1))
    [sent] = call(fold_kernel, [like(own_rows, width + FAR_PAD)], [], kept, at.gate("grad_fold", got))
    at.token("grad_fold", sent)
    far = at.token("grad_far", at.send(at.gate("grad_far", sent), flip=2))
    for k in range(1, CHUNKS):
        across1 = feat_across(at, ops, "1", backs[k], fars[k], nears[k])
        feat = feat + feat_own(at, ops, "1", across1, backs[k], fars[k], nears[k])
    near = at.token("grad_near", at.send(at.gate("grad_near", to_near), flip=1))
    feat[0] = at.gate("add", feat[0])
    [feat_grad] = call(functools.partial(add_up_kernel, CHUNKS), [like(size, width, kind=F32)], [], *feat)
    at.token("add", feat_grad)
    outs = [like(own_rows, width, kind=F32), like(1, own_rows, kind=F32)]
    weight_grad, bias_grad = call(last_fold_kernel, outs, [], at.gate("last", total), near, far)
    return activations, feat_grad, weight_grad, bias_grad[0]


def feat_across(at, ops, name, *lines):
    size, chunk = lines[0].shape
    rows = len(at.chips) * size
    *lines, near = lines
    lines = [*lines, at.gate("across" + name, near)]
    kernel = functools.partial(back_kernel, len(ops))
    [across] = call(kernel, [like(rows, chunk)], [], *[pair[1] for pair in ops], *lines)
    at.token("across" + name, across)
    return at.token("core" + name, at.send(across, dcore=1))


def feat_own(at, ops, name, got, *lines):
    size, chunk = lines[0].shape
    kernel = functools.partial(back_kernel, len(ops))
    outs = [like(size, chunk, kind=F32)] + [like(size, chunk)] * (len(at.chips) - 1)
    parts = call(kernel, outs, [], *[pair[0] for pair in ops], *lines, at.gate("own" + name, got))
    at.token("own" + name, parts)
    sent = [at.send(part, dx=dx, db=db) for part, (dx, db) in zip(parts[1:], at.chips[1:])]
    at.token("feat" + name, sent)
    return [parts[0]] + sent


def plain_rest(at, ops, agg, weight, bias, out_grad):
    size, width = out_grad.shape
    own_rows = weight.shape[0]
    lanes = LINE * own_rows
    agg = agg.astype(LOW)
    whole_weight = lax.all_gather(weight, AXES, axis=0, tiled=True)
    pre = dot(agg, whole_weight, ((1,), (0,))) + bias[None, :]
    phi = 0.5 * (1.0 + lax.erf(pre * (0.5**0.5)))
    activations = (pre * phi).astype(LOW)
    slope = phi + pre * (jnp.exp(-0.5 * pre * pre) * 0.3989422804014327)
    pre_low = (out_grad.astype(F32) * slope).astype(LOW)
    feat = []
    for start, end in bounds(width):
        back = dot(pre_low, whole_weight[start:end], ((1,), (1,))).astype(LOW)
        far = at.send(back, flip=2)
        lines = [back, far, at.send(join(back, far), flip=1)]
        feat = feat + feat_own(at, ops, "", feat_across(at, ops, "", *lines), *lines)
    [feat_grad] = call(functools.partial(add_up_kernel, CHUNKS), [like(size, width, kind=F32)], [], *feat)

    groups = agg.reshape(size, at.rows, LINE, at.bs, own_rows)
    groups = jnp.concatenate([lax.dynamic_slice_in_dim(groups, at.a ^ flip, 1, 2) for flip in ORDER], 2)
    messages = []
    for dx, db in at.chips:
        dest_x = (at.x + dx) % at.xs
        wide = one_of(groups, (at.b + db) % at.bs, 3)
        picked = [
            one_of(wide, dest_x * CORES + (at.core + dcore) % CORES, 1).reshape(size, lanes) for dcore in range(CORES)
        ]
        message = jnp.concatenate([pre_low] + picked, 1)
        messages.append(at.send(message, dx=dx, db=db) if dx or db else message)
    own = jnp.concatenate(messages)
    other = at.send(own, dcore=1)
    weight_part = dot(own[:, width : width + lanes], own[:, :width], ((0,), (0,)))
    weight_part = weight_part + dot(other[:, width + lanes :], other[:, :width], ((0,), (0,)))
    bias_part = jnp.sum(own[:, :width].astype(F32), 0) + jnp.sum(other[:, :width].astype(F32), 0)
    bias_part = one_of(one_of(bias_part.reshape(at.rows, LINE, at.bs, own_rows), at.row, 0), at.b, 1)
    bias_part = jnp.concatenate([one_of(bias_part, at.a ^ flip, 0) for flip in ORDER])
    near = at.send(weight_part[2 * own_rows :].astype(LOW), flip=1).astype(F32)
    kept = weight_part[: 2 * own_rows] + near
    far = at.send(kept[own_rows:].astype(LOW), flip=2).astype(F32)
    near_bias = at.send(bias_part[2 * own_rows :], flip=1)
    kept_bias = bias_part[: 2 * own_rows] + near_bias
    bias_grad = kept_bias[:own_rows] + at.send(kept_bias[own_rows:], flip=2)
    return activations, feat_grad, kept[:own_rows] + far, bias_grad


def solution(mesh):
    placed = (
        P(("col", "row"), None),
        P("row", "col"),
        P("col", "row"),
        P("col", "row"),
        P("row"),
        P(("row", "col"), None),
        P(),
        P(("row", "col"), None),
    )
    return jax.shard_map(
        shards,
        mesh=mesh,
        in_specs=placed,
        out_specs=(
            P(("row", "col"), None),
            P(("col", "row"), None),
            P(("row", "col"), None),
            P(("row", "col")),
        ),
        check_vma=False,
    )
```

```python
import functools
import math

import jax
import jax.numpy as jnp
from jax import lax
from jax.experimental import pallas as pl
from jax.experimental.pallas import tpu as pltpu
from jax.sharding import PartitionSpec as P

boost = 2.0
AXES = ("row", "col")
CORES = 2
LINE = 4
ORDER = (0, 2, 1, 3)
CUTS = (0, 9, 16)
CHUNKS = len(CUTS) - 1
PINS = {
    "features_join": ("operator", "weight_near", "weight_last"),
    "weight_halves": ("features", "operator", "weight_near"),
    "weight_join1": ("sums",),
    "weight_join2": ("sums",),
    "weight_core2": ("sum_near", "sum_far", "sum_last"),
    "pick": ("far0", "right"),
    "far1": ("far0", "left", "rows", "right"),
    "across0": ("far1", "left2", "right2"),
    "across1": ("grad_fold", "feat0"),
    "grad_far": ("left2", "grad_fold"),
    "add": ("grad",),
    "weight_core1": ("operator",),
    "operator": ("weight_far",),
}
NEAR_PAD, FAR_PAD, LAST_PAD = 256, 128, 128
LOW = jnp.bfloat16
F32 = jnp.float32


def dot(left, right, dims):
    return lax.dot_general(left, right, ((dims[0], dims[1]), ((), ())), preferred_element_type=F32)


def after(value, *others):
    return lax.optimization_barrier((value, *others))[0]


def one_of(value, index, axis):
    return lax.dynamic_index_in_dim(value, index, axis, keepdims=False)


def call(kernel, outs, scratch, *operands, numbers=0, outside=0, alone=False):
    whole = pl.BlockSpec(memory_space=pltpu.VMEM)
    specs = [pl.BlockSpec(memory_space=pltpu.SMEM)] * numbers + [pl.BlockSpec(memory_space=pltpu.HBM)] * outside
    specs += [whole] * (len(operands) - len(specs))
    arrays = [v for v in [*operands[numbers:], *outs, *scratch] if hasattr(v.dtype, "itemsize")]
    need = sum(math.prod(v.shape) * v.dtype.itemsize for v in arrays)
    need = 60 * 2**20 if alone else min(need + 6 * 2**20, 60 * 2**20)
    return pl.pallas_call(
        kernel,
        out_shape=outs,
        in_specs=specs,
        out_specs=[whole] * len(outs),
        scratch_shapes=scratch,
        compiler_params=pltpu.CompilerParams(vmem_limit_bytes=need),
        cost_estimate=pl.CostEstimate(flops=1, bytes_accessed=1, transcendentals=0),
    )(*operands)


def like(*shape, kind=LOW):
    return jax.ShapeDtypeStruct(shape, kind)


def bounds(width):
    return [(low * width // CUTS[-1], high * width // CUTS[-1]) for low, high in zip(CUTS, CUTS[1:])]


def join_kernel(pieces, *refs):
    out, row = refs[-1], 0
    for k, start, rows in pieces:
        out[row : row + rows, :] = refs[k][start : start + rows, :]
        row += rows


def join(*pieces):
    pieces = [piece if isinstance(piece, tuple) else (piece, 0, piece.shape[0]) for piece in pieces]
    arrays = list({id(piece[0]): piece[0] for piece in pieces}.values())
    order = {id(array): k for k, array in enumerate(arrays)}
    rows = sum(piece[2] for piece in pieces)
    places = [(order[id(array)], start, count) for array, start, count in pieces]
    return call(functools.partial(join_kernel, places), [like(rows, arrays[0].shape[1])], [], *arrays)[0]


def bounds(width):
    return [(low * width // CUTS[-1], high * width // CUTS[-1]) for low, high in zip(CUTS, CUTS[1:])]


def like(*shape, kind=LOW):
    return jax.ShapeDtypeStruct(shape, kind)


class Place:
    def __init__(self):
        self.rows = lax.axis_size("row")
        self.cols = lax.axis_size("col")
        self.xs = self.rows // CORES
        self.bs = self.cols // LINE
        self.row = lax.axis_index("row")
        self.col = lax.axis_index("col")
        self.x = self.row // CORES
        self.core = self.row % CORES
        self.a = self.col // self.bs
        self.b = self.col % self.bs
        self.chips = [(dx, db) for db in range(self.bs) for dx in range(self.xs)]
        self.numbers = jnp.stack([self.a, self.b, self.x, self.core]).astype(jnp.int32)
        self.tokens = {}

    def token(self, name, value):
        self.tokens[name] = value if isinstance(value, (list, tuple)) else [value]
        return value

    def gate(self, name, value):
        others = [array for step in PINS.get(name, ()) for array in self.tokens.get(step, ())]
        return after(value, *others) if others else value

    def index(self, x, core, a, b):
        return ((x % self.xs) * CORES + core % CORES) * self.cols + (a % LINE) * self.bs + b % self.bs

    def send(self, value, dx=0, dcore=0, db=0, flip=0):
        pairs = [
            (self.index(x, core, a, b), self.index(x + dx, core + dcore, a ^ flip, b + db))
            for x in range(self.xs)
            for core in range(CORES)
            for a in range(LINE)
            for b in range(self.bs)
        ]
        return lax.ppermute(value, AXES, pairs)


def put_blocks(xs, bs, place, weights, part, mask, db, outs):
    a, b, x, core = (place[i] for i in range(4))
    size = weights.shape[1]
    rows = xs * CORES
    eye = (
        lax.broadcasted_iota(jnp.int32, (size, size), 0) == lax.broadcasted_iota(jnp.int32, (size, size), 1)
    ).astype(F32)
    tile = lax.rem(b + db, bs)
    for k, flip in enumerate(ORDER):
        line = (a ^ flip) * bs + b
        row_block = (x * CORES + core) * (LINE * bs) + line
        diagonal = eye * (boost * weights[pl.ds(line, 1), :])
        values = part(k)
        for dcore in range(CORES):
            for dx in range(xs):
                block = lax.rem(x + dx, xs) * CORES + lax.rem(core + dcore, CORES)
                node_block = a * (bs * rows) + tile * rows + block
                total = diagonal * (row_block == node_block).astype(F32)
                for slot in range(values.shape[1] // size):
                    total = total + values[:, slot * size : (slot + 1) * size] * mask(k, slot, block)
                outs[dcore][k * size : (k + 1) * size, dx * size : (dx + 1) * size] = total.astype(LOW)


def own_blocks_kernel(xs, bs, slots, place, *refs):
    held, outs, scratch, sems = refs[:4], refs[4:-5], refs[-5:-1], refs[-1]
    copies = [pltpu.make_async_copy(held[i], scratch[i], sems.at[i]) for i in range(4)]
    for copy in copies:
        copy.start()
    for copy in copies:
        copy.wait()
    cols, counts, block_vals, weights = scratch
    a, b = place[0], place[1]
    size = weights.shape[1]

    def line(k, dest):
        return (a ^ ORDER[k]) * bs + dest

    def rows(k, dest):
        return block_vals[pl.ds(pl.multiple_of(line(k, dest) * size, size), size), :]

    def column(k, slot, dest):
        at = line(k, dest)
        return jnp.where(slot < counts[0, at], cols[slot, at], -1)

    for db in range(1, bs):
        out = outs[CORES + db - 1]
        dest = lax.rem(b - db + bs, bs)
        for k in range(LINE):
            out[k * size : (k + 1) * size, :] = rows(k, dest)
        at_row = lax.broadcasted_iota(jnp.int32, (16, slots * size), 0)
        head = jnp.zeros((16, slots * size), jnp.int32)
        for k in range(LINE):
            for slot in range(slots):
                head = jnp.where(at_row == k * slots + slot, column(k, slot, dest), head)
        out[LINE * size :, :] = head.astype(F32).astype(LOW)
    put_blocks(
        xs,
        bs,
        place,
        weights,
        lambda k: rows(k, b).astype(F32),
        lambda k, slot, block: (column(k, slot, b) == block).astype(F32),
        0,
        outs[:CORES],
    )


def sent_blocks_kernel(xs, bs, slots, db, place, got, weights, *outs):
    size = weights.shape[1]
    head = got[LINE * size :, :].astype(F32)

    def mask(k, slot, block):
        at = k * slots + slot
        return (head[at : at + 1, :size] == block.astype(F32)).astype(F32)

    put_blocks(
        xs, bs, place, weights, lambda k: got[k * size : (k + 1) * size, :].astype(F32), mask, db, outs
    )


def operator(at, block_vals, block_cols, block_counts, self_weight, size):
    slots = block_cols.shape[0]
    weights = self_weight.reshape(-1, size)
    dense = like(LINE * size, at.xs * size)
    own, other, *sent = call(
        functools.partial(own_blocks_kernel, at.xs, at.bs, slots),
        [dense] * CORES + [like(LINE * size + 16, slots * size)] * (at.bs - 1),
        [
            pltpu.SMEM(block_cols.shape, jnp.int32),
            pltpu.SMEM(block_counts.shape, jnp.int32),
            pltpu.VMEM(block_vals.shape, block_vals.dtype),
            pltpu.VMEM(weights.shape, weights.dtype),
            pltpu.SemaphoreType.DMA((4,)),
        ],
        at.numbers,
        block_cols,
        block_counts,
        at.gate("blocks", block_vals),
        weights,
        numbers=1,
        outside=4,
        alone=True,
    )
    result = [[own, other]]
    arrived = at.token("blocks", [at.send(value, db=-db) for db, value in enumerate(sent, 1)])
    for db, got in enumerate(arrived, 1):
        kernel = functools.partial(sent_blocks_kernel, at.xs, at.bs, slots, db)
        got = at.gate("operator", got)
        result.append(call(kernel, [dense] * CORES, [], at.numbers, got, weights, numbers=1))
    at.token("operator", result[-1])
    return result


def sums_kernel(n_ops, pieces, *refs):
    ops, arrays, (*outs, left, right) = refs[:n_ops], refs[n_ops:-6], refs[-6:]
    size, wide = outs[0].shape[0], ops[0].shape[1]
    for i, op in enumerate(ops):
        left[:, i * wide : (i + 1) * wide] = op[...]
    for i, (k, row) in enumerate(pieces):
        right[i * size : (i + 1) * size, :] = arrays[k][row : row + size, :]
    step = right.shape[1] // 4
    for k in range(4):
        columns = slice(k * step, (k + 1) * step)
        part = dot(left[...], right[:, columns], ((1,), (0,)))
        for i, out in enumerate(outs):
            out[:, columns] = part[i * size : (i + 1) * size].astype(out.dtype)


def sums(at, ops, own, across):
    size, width = own[0, 0].shape
    arrays = [*own.values(), *across]
    pieces = []
    for db in range(at.bs):
        pieces += [(db * at.xs + dx, 0) for dx in range(at.xs)]
        pieces += [(len(own) + 1, (db * at.xs + dx - 1) * size) if db or dx else (len(own), 0) for dx in range(at.xs)]
    rows, depth = LINE * size, len(pieces) * size
    return call(
        functools.partial(sums_kernel, CORES * at.bs, pieces),
        [like(size, width, kind=F32)] * 2 + [like(size, width)] * 2,
        [pltpu.VMEM((rows, depth), LOW), pltpu.VMEM((depth, width), LOW)],
        *[op for pair in ops for op in pair],
        *arrays,
    )


def back_kernel(n_ops, *refs):
    ops, lines, rest = refs[:n_ops], refs[n_ops : n_ops + 3], refs[n_ops + 3 :]
    right = jnp.concatenate([line[...] for line in lines], 0)
    parts = [dot(op[...], right, ((0,), (0,))) for op in ops]
    if len(rest) == 1:
        rows = parts[0].shape[0]
        for i, part in enumerate(parts):
            rest[0][i * rows : (i + 1) * rows, :] = part.astype(LOW)
        return
    got, outs = rest[0], rest[1:]
    size = outs[0].shape[0]
    per = parts[0].shape[0] // size
    for i, out in enumerate(outs):
        k = i % per * size
        total = parts[i // per][k : k + size] + got[i * size : (i + 1) * size, :].astype(F32)
        out[...] = total.astype(out.dtype)


def add_up_kernel(n_keeps, *refs):
    *parts, out = refs
    per = len(parts) // n_keeps
    for k, (start, end) in enumerate(bounds(out.shape[1])):
        total = parts[k * per][...]
        for part in parts[k * per + 1 : (k + 1) * per]:
            total = total + part[...].astype(F32)
        out[:, start:end] = total


def along_x(at, value):
    return [value] + [at.send(value, dx=-dx) for dx in range(1, at.xs)]


def along_b(at, value):
    return [value] + [at.send(value, db=-db) for db in range(1, at.bs)]


def gathered_halves(at, halves):
    rows = halves[0].shape[0]
    left, right = along_x(at, halves[0]), along_b(at, halves[1])
    at.token("weight_step1", left[1:] + right[1:])
    lefts = [at.gate("weight_join1", left[0]), *left[1:]]
    rights = [at.gate("weight_join2", right[0]), *right[1:]]
    arrays, held = [at.token("weight_join1", join(*lefts)), at.token("weight_join2", join(*rights))], {}
    for dx in range(at.xs):
        held[dx, 0, 0] = (0, dx * rows)
    for db in range(at.bs):
        held[0, db, 1] = (1, db * rows)
    left, right = arrays
    for db in range(1, at.bs):
        arrays.append(at.send(left, db=-db))
        for dx in range(at.xs):
            held[dx, db, 0] = (len(arrays) - 1, dx * rows)
    for dx in range(1, at.xs):
        arrays.append(at.send(right, dx=-dx))
        for db in range(at.bs):
            held[dx, db, 1] = (len(arrays) - 1, db * rows)
    at.token("weight_step2", arrays[2:])
    return arrays, held


def both_cores(at, arrays, held):
    count = len(arrays)
    across = [at.send(at.gate("weight_core1", value), dcore=1) for value in arrays[:2]]
    at.token("weight_core1", across)
    across += [at.send(at.gate("weight_core2", value), dcore=1) for value in arrays[2:]]
    places = {(0, *place): at for place, at in held.items()}
    places.update({(1, *place): (k + count, i) for place, (k, i) in held.items()})
    return arrays + across, places


def line_kernel(place, weight, far, near, last, left, right):
    count, half = weight.shape[0], left.shape[1]
    for flip, source in zip(ORDER, (weight, far, near, last)):
        rows = pl.ds(pl.multiple_of((place[0] ^ flip) * count, count), count)
        left[rows, :] = source[:, :half]
        right[rows, :] = source[:, half:]


def line_weight(at, weight):
    count, width = weight.shape
    far = at.token("weight_far", at.send(at.gate("weight_far", weight), flip=2))
    near = at.token("weight_near", at.send(at.gate("weight_near", weight), flip=1))
    last = at.token("weight_last", at.send(at.gate("weight_last", far), flip=1))
    halves = [like(LINE * count, width // 2)] * 2
    last = at.gate("weight_line", last)
    return at.token("weight_line", call(line_kernel, halves, [], at.numbers, weight, far, near, last, numbers=1))


def turned_halves(value, swap):
    parts = [value[:, i : i + 128] for i in range(0, value.shape[1], 128)]
    return [jnp.where(swap, pltpu.roll(part, 64, 1), part) for part in parts]


def apart(value, b):
    parts = turned_halves(value, b == 1)
    left = lax.broadcasted_iota(jnp.int32, parts[0].shape, 1) < 64
    own, other = [], []
    for one, two in zip(parts[::2], parts[1::2]):
        own.append(jnp.where(left, one, pltpu.roll(two, 64, 1)))
        other.append(jnp.where(left, pltpu.roll(one, 64, 1), two))
    return jnp.concatenate(own, 1), jnp.concatenate(other, 1)


def together(own, other, b):
    parts = []
    left = lax.broadcasted_iota(jnp.int32, (own.shape[0], 128), 1) < 64
    for i in range(0, own.shape[1], 128):
        one, two = own[:, i : i + 128], other[:, i : i + 128]
        parts.append(jnp.where(left, one, pltpu.roll(two, 64, 1)))
        parts.append(jnp.where(left, pltpu.roll(one, 64, 1), two))
    return jnp.concatenate(turned_halves(jnp.concatenate(parts, 1), b == 1), 1)


def pieces_of(held):
    pieces = {}
    for (*at, h), (k, row) in sorted(held.items(), key=lambda item: item[1]):
        pieces.setdefault((h, k), []).append(tuple(at))
    return pieces


def first_dense_kernel(held, xs, bs, lanes, n_held, place, *refs):
    arrays, (total, near, far, bias, turned, pre, agg) = refs[:n_held], refs[n_held:]
    b, x, core = place[1], place[2], place[3]
    half, group = bias.shape[1] // 2, bs * lanes
    agg[...] = total[...] + near[...].astype(F32) + far[...].astype(F32)
    n = 0
    for dcore in range(CORES):
        for dx in range(xs):
            row = lax.rem(x + dx, xs) * CORES + lax.rem(core + dcore, CORES)
            for part in apart(agg[:, pl.ds(pl.multiple_of(row * group, group), group)], b):
                turned[:, n * lanes : (n + 1) * lanes] = part.astype(LOW)
                n += 1
    for h in range(2):
        part = slice(h * half, (h + 1) * half)
        pre[:, part] = products(held, arrays, turned, h, xs, bs, lanes) + bias[:, part]


def products(held, arrays, turned, h, xs, bs, lanes):
    total = 0.0
    for (side, k), ats in pieces_of(held).items():
        if side == h and k < len(arrays):
            rows = [((dcore * xs + dx) * bs + db) * lanes for dcore, dx, db in ats]
            left = jnp.concatenate([turned[:, row : row + lanes] for row in rows], 1)
            total = total + dot(left, arrays[k][...], ((1,), (0,)))
    return total


def dense_kernel(held, xs, bs, lanes, n_held, place, *refs):
    arrays, refs = refs[:n_held], refs[n_held:]
    turned, first, out_grad, act, left_ref, right_ref = refs[:6]
    backs, [back] = refs[6 : 6 + CHUNKS], refs[6 + CHUNKS :]
    b, x, core = place[1], place[2], place[3]
    half, group = out_grad.shape[1] // 2, bs * lanes
    others = {at: (k - n_held // 2, row) for at, (k, row) in held.items() if at[0]}
    for h, out in enumerate((left_ref, right_ref)):
        part = slice(h * half, (h + 1) * half)
        pre = first[:, part] + products(others, arrays[n_held // 2 :], turned, h, xs, bs, lanes)
        phi = 0.5 * (1.0 + lax.erf(pre * (0.5**0.5)))
        act[:, part] = (pre * phi).astype(LOW)
        slope = phi + pre * (jnp.exp(-0.5 * pre * pre) * 0.3989422804014327)
        out[...] = (out_grad[:, part].astype(F32) * slope).astype(LOW)
    found = {}
    for (h, k), ats in pieces_of(held).items():
        more = dot((left_ref, right_ref)[h][...], arrays[k][...], ((1,), (1,)))
        for i, at in enumerate(ats):
            part = more[:, i * lanes : (i + 1) * lanes]
            found[at] = found[at] + part if at in found else part
    for dcore in range(CORES):
        for dx in range(xs):
            row = lax.rem(x + dx, xs) * CORES + lax.rem(core + dcore, CORES)
            part = together(found[dcore, dx, 0], found[dcore, dx, 1], b)
            back[:, pl.ds(pl.multiple_of(row * group, group), group)] = part.astype(LOW)
    for k, (start, end) in enumerate(bounds(out_grad.shape[1])):
        backs[k][...] = back[:, start:end]


def rows_kernel(xs, bs, lanes, turned, *outs):
    for dx, out in enumerate(outs):
        for dcore in range(CORES):
            for db in range(bs):
                row = ((dcore * xs + dx) * bs + db) * lanes
                to = (db * CORES + dcore) * lanes
                out[:, to : to + lanes] = turned[:, row : row + lanes]


def pick_kernel(db, *refs):
    *refs, out = refs
    lefts, rows = refs[: len(refs) // 2], refs[len(refs) // 2 :]
    size, half = lefts[0].shape
    wide = out.shape[1] - half
    for i, (left, row) in enumerate(zip(lefts, rows)):
        at = slice(i * size, (i + 1) * size)
        out[at, :half] = left[...]
        out[at, half:] = row[:, db * wide : (db + 1) * wide]


def spread(at, lanes, left, right, rows):
    size, half = left.shape
    lefts = [left] + [at.send(at.gate("left", left), dx=dx) for dx in range(1, at.xs)]
    rows = rows[:1] + [at.send(at.gate("rows", row), dx=dx) for dx, row in enumerate(rows[1:], 1)]
    rights = [right] + [at.send(at.gate("right", right), db=db) for db in range(1, at.bs)]
    at.token("left", lefts[1:])
    at.token("rows", rows[1:])
    at.token("right", rights[1:])

    def pick(db):
        outs = [like(at.xs * size, half + CORES * lanes)]
        refs = [at.gate("pick", left), *lefts[1:], *rows]
        return call(functools.partial(pick_kernel, db), outs, [], *refs)[0]

    held = {}

    def keep(k, place, row):
        held[place] = (k, row)

    arrays = [pick(0), join(at.gate("join_right", right), *rights[1:])]
    for dx in range(at.xs):
        keep(0, (-dx % at.xs, 0, 0), dx * size)
    for db in range(at.bs):
        keep(1, (0, -db % at.bs, 1), db * size)
    for db in range(1, at.bs):
        arrays.append(at.send(pick(db), db=db))
        for dx in range(at.xs):
            keep(len(arrays) - 1, (-dx % at.xs, -db % at.bs, 0), dx * size)
    for dx in range(1, at.xs):
        arrays.append(at.send(arrays[1], dx=dx))
        for db in range(at.bs):
            keep(len(arrays) - 1, (-dx % at.xs, -db % at.bs, 1), db * size)
    at.token("left2", arrays[2 : 1 + at.bs])
    at.token("right2", arrays[1 + at.bs :])
    return arrays, held


def grad_kernel(held, xs, bs, lanes, dcore, n_arrays, place, *refs):
    arrays, (*outs, left, right, product, sums_ref) = refs[:n_arrays], refs[n_arrays:]
    a, b, x, core = (place[i] for i in range(4))
    size, width = left.shape[0] // (xs * bs), right.shape[1]
    half, count, group = width // 2, lanes // LINE, bs * lanes
    for n, (dx, db) in enumerate((dx, db) for db in range(bs) for dx in range(xs)):
        rows = slice(n * size, (n + 1) * size)
        k, row = held[dx, db, 0]
        right[rows, :half] = arrays[k][row : row + size, :half]
        start = half + dcore * lanes
        left[rows, :] = arrays[k][row : row + size, start : start + lanes]
        k, row = held[dx, db, 1]
        right[rows, half:] = arrays[k][row : row + size, :]
    product[:, :width] = dot(left[...], right[...], ((0,), (0,)))
    total = jnp.sum(right[...].astype(F32), 0, keepdims=True)
    sums_ref[...] = jnp.broadcast_to(total, sums_ref.shape)
    row = x * CORES + lax.rem(core + dcore, CORES)
    own = sums_ref[0:1, pl.ds(pl.multiple_of(row * group, group), group)]
    at_row = lax.broadcasted_iota(jnp.int32, (lanes, group), 0)
    at_lane = lax.broadcasted_iota(jnp.int32, (lanes, group), 1)
    source = (at_row // count) * (bs * count) + b * count + at_row % count
    column = jnp.sum(jnp.where(at_lane == source, own, 0.0), 1, keepdims=True)
    product[:, width:] = jnp.broadcast_to(column, (lanes, 128))
    if dcore:
        [out] = outs
        out[:, :width] = product[:, :width].astype(LOW)
        out[:, width:] = two_parts(product[:, width:])
        return
    got, outs = outs[0], outs[1:]
    for out, flip in zip(outs, ORDER):
        rows = pl.ds(pl.multiple_of((a ^ flip) * count, count), count)
        tail = got[rows, width:].astype(F32)
        tail = product[rows, width:] + (tail[:, 0:1] + tail[:, 1:2])
        out[:, :width] = (product[rows, :width] + got[rows, :width].astype(F32)).astype(out.dtype)
        out[:, width : width + 128] = two_parts(tail) if out.dtype == LOW else tail


def two_parts(value):
    high = value.astype(LOW)
    rest = (value - high.astype(F32)).astype(LOW)
    lane = lax.broadcasted_iota(jnp.int32, value.shape, 1)
    return jnp.where(lane == 0, high.astype(F32), jnp.where(lane == 1, rest.astype(F32), 0.0)).astype(LOW)


def fold_kernel(kept, got, far):
    width = kept.shape[1] - 128
    tail = got[:, width : width + 128].astype(F32)
    far[:, :width] = (kept[:, :width] + got[:, :width].astype(F32)).astype(LOW)
    far[:, width : width + 128] = two_parts(kept[:, width : width + 128] + (tail[:, 0:1] + tail[:, 1:2]))


def last_fold_kernel(kept, *refs):
    *arrived, weight_out, bias_out = refs
    width = weight_out.shape[1]
    total, tail = kept[:, :width], kept[:, width : width + 128]
    for got in arrived:
        total = total + got[:, :width].astype(F32)
        rest = got[:, width : width + 128].astype(F32)
        tail = tail + (rest[:, 0:1] + rest[:, 1:2])
    weight_out[...] = total
    bias_out[...] = jnp.transpose(tail)[0:1, :]


def far_kernel(kept, got, far):
    far[...] = (kept[...] + got[...].astype(F32)).astype(LOW)


def shards(node_feats, block_vals, block_cols, block_counts, self_weight, weight, bias, out_grad):
    at = Place()
    size, width = node_feats.shape
    own_rows = weight.shape[0]
    lanes = LINE * own_rows
    aligned = own_rows * at.bs == 128
    halves = line_weight(at, weight) if aligned else []
    first, *chips = at.chips
    own = {first: node_feats}
    for dx, db in chips:
        own[dx, db] = at.send(at.gate("features", node_feats), dx=-dx, db=-db)
    at.token("features", [own[chip] for chip in chips])
    ops = operator(at, block_vals, block_cols, block_counts, self_weight, size)
    others = at.token("features_join", join(at.gate("features_join", own[chips[0]]), *[own[chip] for chip in chips[1:]]))
    across = [at.send(node_feats, dcore=1), at.send(others, dcore=1)]
    across[0] = at.gate("sums", across[0])
    total, kept, to_near, to_last = at.token("sums", sums(at, ops, own, across))
    got = at.token("sum_last", at.send(to_last, flip=1))
    [far] = at.token("sum_fold", call(far_kernel, [like(size, width)], [], kept, at.gate("sum_fold", got)))
    near = at.token("sum_near", at.send(at.gate("sum_near", to_near), flip=1))
    far = at.token("sum_far", at.send(far, flip=2))

    if not aligned:
        return plain_rest(at, ops, total + near.astype(F32) + far.astype(F32), weight, bias, out_grad)
    halves = [at.gate("weight_halves", half) for half in halves]
    arrays, held = gathered_halves(at, halves)
    arrays, held = both_cores(at, arrays, held)
    widths = [end - start for start, end in bounds(width)]
    own_held = {at: where for at, where in held.items() if not at[0]}
    count = len(arrays) // 2
    turned, pre = call(
        functools.partial(first_dense_kernel, own_held, at.xs, at.bs, lanes, count),
        [like(size, width), like(size, width, kind=F32)],
        [pltpu.VMEM((size, width), F32)],
        at.numbers,
        *arrays[:count],
        total,
        near,
        far,
        bias[None, :],
        numbers=1,
    )
    activations, left, right, *backs = call(
        functools.partial(dense_kernel, held, at.xs, at.bs, lanes, len(arrays)),
        [like(size, width)] + [like(size, width // 2)] * 2 + [like(size, wide) for wide in widths],
        [pltpu.VMEM((size, width), LOW)],
        at.numbers,
        *arrays,
        turned,
        pre,
        out_grad,
        numbers=1,
    )

    fars = [at.token("far0", at.send(backs[0], flip=2))]
    kernel = functools.partial(rows_kernel, at.xs, at.bs, lanes)
    rows = list(call(kernel, [like(size, at.bs * CORES * lanes)] * at.xs, [], at.gate("rows_kernel", turned)))
    arrays, held = spread(at, lanes, left, right, rows)
    nears = [at.token("near0", at.send(join(at.gate("near0", backs[0]), fars[0]), flip=1))]
    for k in range(1, CHUNKS):
        fars.append(at.token("far1", at.send(at.gate("far1", backs[k]), flip=2)))
        nears.append(at.token("near1", at.send(join(at.gate("near1", backs[k]), fars[k]), flip=1)))

    across0 = feat_across(at, ops, "0", backs[0], fars[0], nears[0])
    wide = width + 128
    scratch = [
        pltpu.VMEM((size * len(at.chips), lanes), LOW),
        pltpu.VMEM((size * len(at.chips), width), LOW),
        pltpu.VMEM((lanes, wide), F32),
        pltpu.VMEM((8, width), F32),
    ]
    kernel = functools.partial(grad_kernel, held, at.xs, at.bs, lanes)
    first = at.gate("grad_across", arrays[0])
    [across] = call(
        functools.partial(kernel, 1, len(arrays)), [like(lanes, wide)], scratch, at.numbers, first, *arrays[1:], numbers=1
    )
    at.token("grad_across", across)
    got = at.token("grad_core", at.send(across, dcore=1))
    feat = feat_own(at, ops, "0", across0, backs[0], fars[0], nears[0])
    outs = [like(own_rows, wide, kind=F32)] * 2 + [like(own_rows, width + NEAR_PAD), like(own_rows, width + LAST_PAD)]
    total, kept, to_near, to_last = call(
        functools.partial(kernel, 0, len(arrays)),
        outs,
        scratch,
        at.numbers,
        *arrays,
        at.gate("grad", got),
        numbers=1,
    )
    at.token("grad", to_last)
    got = at.token("grad_last", at.send(to_last, flip=1))
    [sent] = call(fold_kernel, [like(own_rows, width + FAR_PAD)], [], kept, at.gate("grad_fold", got))
    at.token("grad_fold", sent)
    far = at.token("grad_far", at.send(at.gate("grad_far", sent), flip=2))
    for k in range(1, CHUNKS):
        across1 = feat_across(at, ops, "1", backs[k], fars[k], nears[k])
        feat = feat + feat_own(at, ops, "1", across1, backs[k], fars[k], nears[k])
    near = at.token("grad_near", at.send(at.gate("grad_near", to_near), flip=1))
    feat[0] = at.gate("add", feat[0])
    [feat_grad] = call(functools.partial(add_up_kernel, CHUNKS), [like(size, width, kind=F32)], [], *feat)
    at.token("add", feat_grad)
    outs = [like(own_rows, width, kind=F32), like(1, own_rows, kind=F32)]
    weight_grad, bias_grad = call(last_fold_kernel, outs, [], at.gate("last", total), near, far)
    return activations, feat_grad, weight_grad, bias_grad[0]


def feat_across(at, ops, name, *lines):
    size, chunk = lines[0].shape
    rows = len(at.chips) * size
    *lines, near = lines
    lines = [*lines, at.gate("across" + name, near)]
    kernel = functools.partial(back_kernel, len(ops))
    [across] = call(kernel, [like(rows, chunk)], [], *[pair[1] for pair in ops], *lines)
    at.token("across" + name, across)
    return at.token("core" + name, at.send(across, dcore=1))


def feat_own(at, ops, name, got, *lines):
    size, chunk = lines[0].shape
    kernel = functools.partial(back_kernel, len(ops))
    outs = [like(size, chunk, kind=F32)] + [like(size, chunk)] * (len(at.chips) - 1)
    parts = call(kernel, outs, [], *[pair[0] for pair in ops], *lines, at.gate("own" + name, got))
    at.token("own" + name, parts)
    sent = [at.send(part, dx=dx, db=db) for part, (dx, db) in zip(parts[1:], at.chips[1:])]
    at.token("feat" + name, sent)
    return [parts[0]] + sent


def plain_rest(at, ops, agg, weight, bias, out_grad):
    size, width = out_grad.shape
    own_rows = weight.shape[0]
    lanes = LINE * own_rows
    agg = agg.astype(LOW)
    whole_weight = lax.all_gather(weight, AXES, axis=0, tiled=True)
    pre = dot(agg, whole_weight, ((1,), (0,))) + bias[None, :]
    phi = 0.5 * (1.0 + lax.erf(pre * (0.5**0.5)))
    activations = (pre * phi).astype(LOW)
    slope = phi + pre * (jnp.exp(-0.5 * pre * pre) * 0.3989422804014327)
    pre_low = (out_grad.astype(F32) * slope).astype(LOW)
    feat = []
    for start, end in bounds(width):
        back = dot(pre_low, whole_weight[start:end], ((1,), (1,))).astype(LOW)
        far = at.send(back, flip=2)
        lines = [back, far, at.send(join(back, far), flip=1)]
        feat = feat + feat_own(at, ops, "", feat_across(at, ops, "", *lines), *lines)
    [feat_grad] = call(functools.partial(add_up_kernel, CHUNKS), [like(size, width, kind=F32)], [], *feat)

    groups = agg.reshape(size, at.rows, LINE, at.bs, own_rows)
    groups = jnp.concatenate([lax.dynamic_slice_in_dim(groups, at.a ^ flip, 1, 2) for flip in ORDER], 2)
    messages = []
    for dx, db in at.chips:
        dest_x = (at.x + dx) % at.xs
        wide = one_of(groups, (at.b + db) % at.bs, 3)
        picked = [
            one_of(wide, dest_x * CORES + (at.core + dcore) % CORES, 1).reshape(size, lanes) for dcore in range(CORES)
        ]
        message = jnp.concatenate([pre_low] + picked, 1)
        messages.append(at.send(message, dx=dx, db=db) if dx or db else message)
    own = jnp.concatenate(messages)
    other = at.send(own, dcore=1)
    weight_part = dot(own[:, width : width + lanes], own[:, :width], ((0,), (0,)))
    weight_part = weight_part + dot(other[:, width + lanes :], other[:, :width], ((0,), (0,)))
    bias_part = jnp.sum(own[:, :width].astype(F32), 0) + jnp.sum(other[:, :width].astype(F32), 0)
    bias_part = one_of(one_of(bias_part.reshape(at.rows, LINE, at.bs, own_rows), at.row, 0), at.b, 1)
    bias_part = jnp.concatenate([one_of(bias_part, at.a ^ flip, 0) for flip in ORDER])
    near = at.send(weight_part[2 * own_rows :].astype(LOW), flip=1).astype(F32)
    kept = weight_part[: 2 * own_rows] + near
    far = at.send(kept[own_rows:].astype(LOW), flip=2).astype(F32)
    near_bias = at.send(bias_part[2 * own_rows :], flip=1)
    kept_bias = bias_part[: 2 * own_rows] + near_bias
    bias_grad = kept_bias[:own_rows] + at.send(kept_bias[own_rows:], flip=2)
    return activations, feat_grad, kept[:own_rows] + far, bias_grad


def solution(mesh):
    placed = (
        P(("col", "row"), None),
        P("row", "col"),
        P("col", "row"),
        P("col", "row"),
        P("row"),
        P(("row", "col"), None),
        P(),
        P(("row", "col"), None),
    )
    return jax.shard_map(
        shards,
        mesh=mesh,
        in_specs=placed,
        out_specs=(
            P(("row", "col"), None),
            P(("col", "row"), None),
            P(("row", "col"), None),
            P(("row", "col")),
        ),
        check_vma=False,
    )
```

```python
import functools
import math

import jax
import jax.numpy as jnp
from jax import lax
from jax.experimental import pallas as pl
from jax.experimental.pallas import tpu as pltpu
from jax.sharding import PartitionSpec as P

boost = 2.0
AXES = ("row", "col")
CORES = 2
LINE = 4
ORDER = (0, 2, 1, 3)
CUTS = (0, 9, 16)
CHUNKS = len(CUTS) - 1
PINS = {
    "weight_core1": ("operator",),
    "features_join": ("operator", "weight_near", "weight_last"),
    "weight_halves": ("features", "operator", "weight_near"),
    "weight_join1": ("sums",),
    "weight_join2": ("sums",),
    "weight_core2": ("sum_near", "sum_far", "sum_last"),
    "pick": ("far0",),
    "join_right": ("far0",),
    "far1": ("far0", "left", "rows", "right"),
    "across0": ("far1", "left2", "right2"),
    "grad_far": ("left2",),
    "across1": ("grad_fold", "feat0"),
    "add": ("grad",),
}
NEAR_PAD, FAR_PAD, LAST_PAD = 256, 256, 128
LOW = jnp.bfloat16
F32 = jnp.float32


def dot(left, right, dims):
    return lax.dot_general(left, right, ((dims[0], dims[1]), ((), ())), preferred_element_type=F32)


def after(value, *others):
    return lax.optimization_barrier((value, *others))[0]


def one_of(value, index, axis):
    return lax.dynamic_index_in_dim(value, index, axis, keepdims=False)


def call(kernel, outs, scratch, *operands, numbers=0, outside=0, alone=False):
    whole = pl.BlockSpec(memory_space=pltpu.VMEM)
    specs = [pl.BlockSpec(memory_space=pltpu.SMEM)] * numbers + [pl.BlockSpec(memory_space=pltpu.HBM)] * outside
    specs += [whole] * (len(operands) - len(specs))
    arrays = [v for v in [*operands[numbers:], *outs, *scratch] if hasattr(v.dtype, "itemsize")]
    need = sum(math.prod(v.shape) * v.dtype.itemsize for v in arrays)
    need = 60 * 2**20 if alone else min(need + 6 * 2**20, 60 * 2**20)
    return pl.pallas_call(
        kernel,
        out_shape=outs,
        in_specs=specs,
        out_specs=[whole] * len(outs),
        scratch_shapes=scratch,
        compiler_params=pltpu.CompilerParams(vmem_limit_bytes=need),
        cost_estimate=pl.CostEstimate(flops=1, bytes_accessed=1, transcendentals=0),
    )(*operands)


def like(*shape, kind=LOW):
    return jax.ShapeDtypeStruct(shape, kind)


def bounds(width):
    return [(low * width // CUTS[-1], high * width // CUTS[-1]) for low, high in zip(CUTS, CUTS[1:])]


def join_kernel(pieces, *refs):
    out, row = refs[-1], 0
    for k, start, rows in pieces:
        out[row : row + rows, :] = refs[k][start : start + rows, :]
        row += rows


def join(*pieces):
    pieces = [piece if isinstance(piece, tuple) else (piece, 0, piece.shape[0]) for piece in pieces]
    arrays = list({id(piece[0]): piece[0] for piece in pieces}.values())
    order = {id(array): k for k, array in enumerate(arrays)}
    rows = sum(piece[2] for piece in pieces)
    places = [(order[id(array)], start, count) for array, start, count in pieces]
    return call(functools.partial(join_kernel, places), [like(rows, arrays[0].shape[1])], [], *arrays)[0]


def bounds(width):
    return [(low * width // CUTS[-1], high * width // CUTS[-1]) for low, high in zip(CUTS, CUTS[1:])]


def like(*shape, kind=LOW):
    return jax.ShapeDtypeStruct(shape, kind)


class Place:
    def __init__(self):
        self.rows = lax.axis_size("row")
        self.cols = lax.axis_size("col")
        self.xs = self.rows // CORES
        self.bs = self.cols // LINE
        self.row = lax.axis_index("row")
        self.col = lax.axis_index("col")
        self.x = self.row // CORES
        self.core = self.row % CORES
        self.a = self.col // self.bs
        self.b = self.col % self.bs
        self.chips = [(dx, db) for db in range(self.bs) for dx in range(self.xs)]
        self.numbers = jnp.stack([self.a, self.b, self.x, self.core]).astype(jnp.int32)
        self.tokens = {}

    def token(self, name, value):
        self.tokens[name] = value if isinstance(value, (list, tuple)) else [value]
        return value

    def gate(self, name, value):
        others = [array for step in PINS.get(name, ()) for array in self.tokens.get(step, ())]
        return after(value, *others) if others else value

    def index(self, x, core, a, b):
        return ((x % self.xs) * CORES + core % CORES) * self.cols + (a % LINE) * self.bs + b % self.bs

    def send(self, value, dx=0, dcore=0, db=0, flip=0):
        pairs = [
            (self.index(x, core, a, b), self.index(x + dx, core + dcore, a ^ flip, b + db))
            for x in range(self.xs)
            for core in range(CORES)
            for a in range(LINE)
            for b in range(self.bs)
        ]
        return lax.ppermute(value, AXES, pairs)


def put_blocks(xs, bs, place, weights, part, mask, db, outs):
    a, b, x, core = (place[i] for i in range(4))
    size = weights.shape[1]
    rows = xs * CORES
    eye = (
        lax.broadcasted_iota(jnp.int32, (size, size), 0) == lax.broadcasted_iota(jnp.int32, (size, size), 1)
    ).astype(F32)
    tile = lax.rem(b + db, bs)
    for k, flip in enumerate(ORDER):
        line = (a ^ flip) * bs + b
        row_block = (x * CORES + core) * (LINE * bs) + line
        diagonal = eye * (boost * weights[pl.ds(line, 1), :])
        values = part(k)
        for dcore in range(CORES):
            for dx in range(xs):
                block = lax.rem(x + dx, xs) * CORES + lax.rem(core + dcore, CORES)
                node_block = a * (bs * rows) + tile * rows + block
                total = diagonal * (row_block == node_block).astype(F32)
                for slot in range(values.shape[1] // size):
                    total = total + values[:, slot * size : (slot + 1) * size] * mask(k, slot, block)
                outs[dcore][k * size : (k + 1) * size, dx * size : (dx + 1) * size] = total.astype(LOW)


def own_blocks_kernel(xs, bs, slots, place, *refs):
    held, outs, scratch, sems = refs[:4], refs[4:-5], refs[-5:-1], refs[-1]
    copies = [pltpu.make_async_copy(held[i], scratch[i], sems.at[i]) for i in range(4)]
    for copy in copies:
        copy.start()
    for copy in copies:
        copy.wait()
    cols, counts, block_vals, weights = scratch
    a, b = place[0], place[1]
    size = weights.shape[1]

    def line(k, dest):
        return (a ^ ORDER[k]) * bs + dest

    def rows(k, dest):
        return block_vals[pl.ds(pl.multiple_of(line(k, dest) * size, size), size), :]

    def column(k, slot, dest):
        at = line(k, dest)
        return jnp.where(slot < counts[0, at], cols[slot, at], -1)

    for db in range(1, bs):
        out = outs[CORES + db - 1]
        dest = lax.rem(b - db + bs, bs)
        for k in range(LINE):
            out[k * size : (k + 1) * size, :] = rows(k, dest)
        at_row = lax.broadcasted_iota(jnp.int32, (16, slots * size), 0)
        head = jnp.zeros((16, slots * size), jnp.int32)
        for k in range(LINE):
            for slot in range(slots):
                head = jnp.where(at_row == k * slots + slot, column(k, slot, dest), head)
        out[LINE * size :, :] = head.astype(F32).astype(LOW)
    put_blocks(
        xs,
        bs,
        place,
        weights,
        lambda k: rows(k, b).astype(F32),
        lambda k, slot, block: (column(k, slot, b) == block).astype(F32),
        0,
        outs[:CORES],
    )


def sent_blocks_kernel(xs, bs, slots, db, place, got, weights, *outs):
    size = weights.shape[1]
    head = got[LINE * size :, :].astype(F32)

    def mask(k, slot, block):
        at = k * slots + slot
        return (head[at : at + 1, :size] == block.astype(F32)).astype(F32)

    put_blocks(
        xs, bs, place, weights, lambda k: got[k * size : (k + 1) * size, :].astype(F32), mask, db, outs
    )


def operator(at, block_vals, block_cols, block_counts, self_weight, size):
    slots = block_cols.shape[0]
    weights = self_weight.reshape(-1, size)
    dense = like(LINE * size, at.xs * size)
    own, other, *sent = call(
        functools.partial(own_blocks_kernel, at.xs, at.bs, slots),
        [dense] * CORES + [like(LINE * size + 16, slots * size)] * (at.bs - 1),
        [
            pltpu.SMEM(block_cols.shape, jnp.int32),
            pltpu.SMEM(block_counts.shape, jnp.int32),
            pltpu.VMEM(block_vals.shape, block_vals.dtype),
            pltpu.VMEM(weights.shape, weights.dtype),
            pltpu.SemaphoreType.DMA((4,)),
        ],
        at.numbers,
        block_cols,
        block_counts,
        at.gate("blocks", block_vals),
        weights,
        numbers=1,
        outside=4,
        alone=True,
    )
    result = [[own, other]]
    arrived = at.token("blocks", [at.send(value, db=-db) for db, value in enumerate(sent, 1)])
    for db, got in enumerate(arrived, 1):
        kernel = functools.partial(sent_blocks_kernel, at.xs, at.bs, slots, db)
        got = at.gate("operator", got)
        result.append(call(kernel, [dense] * CORES, [], at.numbers, got, weights, numbers=1))
    at.token("operator", result[-1])
    return result


def sums_kernel(n_ops, pieces, *refs):
    ops, arrays, (*outs, left, right) = refs[:n_ops], refs[n_ops:-6], refs[-6:]
    size, wide = outs[0].shape[0], ops[0].shape[1]
    for i, op in enumerate(ops):
        left[:, i * wide : (i + 1) * wide] = op[...]
    for i, (k, row) in enumerate(pieces):
        right[i * size : (i + 1) * size, :] = arrays[k][row : row + size, :]
    step = right.shape[1] // 4
    for k in range(4):
        columns = slice(k * step, (k + 1) * step)
        part = dot(left[...], right[:, columns], ((1,), (0,)))
        for i, out in enumerate(outs):
            out[:, columns] = part[i * size : (i + 1) * size].astype(out.dtype)


def sums(at, ops, own, across):
    size, width = own[0, 0].shape
    arrays = [*own.values(), *across]
    pieces = []
    for db in range(at.bs):
        pieces += [(db * at.xs + dx, 0) for dx in range(at.xs)]
        pieces += [(len(own) + 1, (db * at.xs + dx - 1) * size) if db or dx else (len(own), 0) for dx in range(at.xs)]
    rows, depth = LINE * size, len(pieces) * size
    return call(
        functools.partial(sums_kernel, CORES * at.bs, pieces),
        [like(size, width, kind=F32)] * 2 + [like(size, width)] * 2,
        [pltpu.VMEM((rows, depth), LOW), pltpu.VMEM((depth, width), LOW)],
        *[op for pair in ops for op in pair],
        *arrays,
    )


def back_kernel(n_ops, *refs):
    ops, lines, rest = refs[:n_ops], refs[n_ops : n_ops + 3], refs[n_ops + 3 :]
    right = jnp.concatenate([line[...] for line in lines], 0)
    parts = [dot(op[...], right, ((0,), (0,))) for op in ops]
    if len(rest) == 1:
        rows = parts[0].shape[0]
        for i, part in enumerate(parts):
            rest[0][i * rows : (i + 1) * rows, :] = part.astype(LOW)
        return
    got, outs = rest[0], rest[1:]
    size = outs[0].shape[0]
    per = parts[0].shape[0] // size
    for i, out in enumerate(outs):
        k = i % per * size
        total = parts[i // per][k : k + size] + got[i * size : (i + 1) * size, :].astype(F32)
        out[...] = total.astype(out.dtype)


def sum_kernel(first, *refs):
    *parts, out = refs
    total = first[...]
    for part in parts:
        total = total + part[...].astype(F32)
    out[...] = total


def last_sum_kernel(first, *refs):
    *parts, out = refs
    done = first.shape[1]
    out[:, :done] = first[...]
    total = parts[0][...]
    for part in parts[1:]:
        total = total + part[...].astype(F32)
    out[:, done:] = total


def add_up_kernel(n_keeps, *refs):
    *parts, out = refs
    per = len(parts) // n_keeps
    for k, (start, end) in enumerate(bounds(out.shape[1])):
        total = parts[k * per][...]
        for part in parts[k * per + 1 : (k + 1) * per]:
            total = total + part[...].astype(F32)
        out[:, start:end] = total


def along_x(at, value):
    return [value] + [at.send(value, dx=-dx) for dx in range(1, at.xs)]


def along_b(at, value):
    return [value] + [at.send(value, db=-db) for db in range(1, at.bs)]


def gathered_halves(at, halves):
    rows = halves[0].shape[0]
    left, right = along_x(at, halves[0]), along_b(at, halves[1])
    at.token("weight_step1", left[1:] + right[1:])
    lefts = [at.gate("weight_join1", left[0]), *left[1:]]
    rights = [at.gate("weight_join2", right[0]), *right[1:]]
    arrays, held = [at.token("weight_join1", join(*lefts)), at.token("weight_join2", join(*rights))], {}
    for dx in range(at.xs):
        held[dx, 0, 0] = (0, dx * rows)
    for db in range(at.bs):
        held[0, db, 1] = (1, db * rows)
    left, right = arrays
    for db in range(1, at.bs):
        arrays.append(at.send(left, db=-db))
        for dx in range(at.xs):
            held[dx, db, 0] = (len(arrays) - 1, dx * rows)
    for dx in range(1, at.xs):
        arrays.append(at.send(right, dx=-dx))
        for db in range(at.bs):
            held[dx, db, 1] = (len(arrays) - 1, db * rows)
    at.token("weight_step2", arrays[2:])
    return arrays, held


def both_cores(at, arrays, held):
    count = len(arrays)
    across = [at.send(at.gate("weight_core1", value), dcore=1) for value in arrays[:2]]
    at.token("weight_core1", across)
    across += [at.send(at.gate("weight_core2", value), dcore=1) for value in arrays[2:]]
    places = {(0, *place): at for place, at in held.items()}
    places.update({(1, *place): (k + count, i) for place, (k, i) in held.items()})
    return arrays + across, places


def line_kernel(place, weight, far, near, last, left, right):
    count, half = weight.shape[0], left.shape[1]
    for flip, source in zip(ORDER, (weight, far, near, last)):
        rows = pl.ds(pl.multiple_of((place[0] ^ flip) * count, count), count)
        left[rows, :] = source[:, :half]
        right[rows, :] = source[:, half:]


def line_weight(at, weight):
    count, width = weight.shape
    far = at.token("weight_far", at.send(at.gate("weight_far", weight), flip=2))
    near = at.token("weight_near", at.send(at.gate("weight_near", weight), flip=1))
    last = at.token("weight_last", at.send(at.gate("weight_last", far), flip=1))
    halves = [like(LINE * count, width // 2)] * 2
    last = at.gate("weight_line", last)
    return at.token("weight_line", call(line_kernel, halves, [], at.numbers, weight, far, near, last, numbers=1))


def turned_halves(value, swap):
    parts = [value[:, i : i + 128] for i in range(0, value.shape[1], 128)]
    return [jnp.where(swap, pltpu.roll(part, 64, 1), part) for part in parts]


def apart(value, b):
    parts = turned_halves(value, b == 1)
    left = lax.broadcasted_iota(jnp.int32, parts[0].shape, 1) < 64
    own, other = [], []
    for one, two in zip(parts[::2], parts[1::2]):
        own.append(jnp.where(left, one, pltpu.roll(two, 64, 1)))
        other.append(jnp.where(left, pltpu.roll(one, 64, 1), two))
    return jnp.concatenate(own, 1), jnp.concatenate(other, 1)


def together(own, other, b):
    parts = []
    left = lax.broadcasted_iota(jnp.int32, (own.shape[0], 128), 1) < 64
    for i in range(0, own.shape[1], 128):
        one, two = own[:, i : i + 128], other[:, i : i + 128]
        parts.append(jnp.where(left, one, pltpu.roll(two, 64, 1)))
        parts.append(jnp.where(left, pltpu.roll(one, 64, 1), two))
    return jnp.concatenate(turned_halves(jnp.concatenate(parts, 1), b == 1), 1)


def pieces_of(held):
    pieces = {}
    for (*at, h), (k, row) in sorted(held.items(), key=lambda item: item[1]):
        pieces.setdefault((h, k), []).append(tuple(at))
    return pieces


def first_dense_kernel(held, xs, bs, lanes, n_held, place, *refs):
    arrays, (total, near, far, bias, turned, pre, agg) = refs[:n_held], refs[n_held:]
    b, x, core = place[1], place[2], place[3]
    half, group = bias.shape[1] // 2, bs * lanes
    agg[...] = total[...] + near[...].astype(F32) + far[...].astype(F32)
    n = 0
    for dcore in range(CORES):
        for dx in range(xs):
            row = lax.rem(x + dx, xs) * CORES + lax.rem(core + dcore, CORES)
            for part in apart(agg[:, pl.ds(pl.multiple_of(row * group, group), group)], b):
                turned[:, n * lanes : (n + 1) * lanes] = part.astype(LOW)
                n += 1
    for h in range(2):
        part = slice(h * half, (h + 1) * half)
        pre[:, part] = products(held, arrays, turned, h, xs, bs, lanes) + bias[:, part]


def products(held, arrays, turned, h, xs, bs, lanes):
    total = 0.0
    for (side, k), ats in pieces_of(held).items():
        if side == h and k < len(arrays):
            rows = [((dcore * xs + dx) * bs + db) * lanes for dcore, dx, db in ats]
            left = jnp.concatenate([turned[:, row : row + lanes] for row in rows], 1)
            total = total + dot(left, arrays[k][...], ((1,), (0,)))
    return total


def dense_kernel(held, xs, bs, lanes, n_held, place, *refs):
    arrays, refs = refs[:n_held], refs[n_held:]
    turned, first, out_grad, act, left_ref, right_ref = refs[:6]
    backs, [back] = refs[6 : 6 + CHUNKS], refs[6 + CHUNKS :]
    b, x, core = place[1], place[2], place[3]
    half, group = out_grad.shape[1] // 2, bs * lanes
    others = {at: (k - n_held // 2, row) for at, (k, row) in held.items() if at[0]}
    for h, out in enumerate((left_ref, right_ref)):
        part = slice(h * half, (h + 1) * half)
        pre = first[:, part] + products(others, arrays[n_held // 2 :], turned, h, xs, bs, lanes)
        phi = 0.5 * (1.0 + lax.erf(pre * (0.5**0.5)))
        act[:, part] = (pre * phi).astype(LOW)
        slope = phi + pre * (jnp.exp(-0.5 * pre * pre) * 0.3989422804014327)
        out[...] = (out_grad[:, part].astype(F32) * slope).astype(LOW)
    found = {}
    for (h, k), ats in pieces_of(held).items():
        more = dot((left_ref, right_ref)[h][...], arrays[k][...], ((1,), (1,)))
        for i, at in enumerate(ats):
            part = more[:, i * lanes : (i + 1) * lanes]
            found[at] = found[at] + part if at in found else part
    for dcore in range(CORES):
        for dx in range(xs):
            row = lax.rem(x + dx, xs) * CORES + lax.rem(core + dcore, CORES)
            part = together(found[dcore, dx, 0], found[dcore, dx, 1], b)
            back[:, pl.ds(pl.multiple_of(row * group, group), group)] = part.astype(LOW)
    for k, (start, end) in enumerate(bounds(out_grad.shape[1])):
        backs[k][...] = back[:, start:end]


def rows_kernel(xs, bs, lanes, turned, *outs):
    for dx, out in enumerate(outs):
        for dcore in range(CORES):
            for db in range(bs):
                row = ((dcore * xs + dx) * bs + db) * lanes
                to = (db * CORES + dcore) * lanes
                out[:, to : to + lanes] = turned[:, row : row + lanes]


def pick_kernel(db, *refs):
    *refs, out = refs
    lefts, rows = refs[: len(refs) // 2], refs[len(refs) // 2 :]
    size, half = lefts[0].shape
    wide = out.shape[1] - half
    for i, (left, row) in enumerate(zip(lefts, rows)):
        at = slice(i * size, (i + 1) * size)
        out[at, :half] = left[...]
        out[at, half:] = row[:, db * wide : (db + 1) * wide]


def spread(at, lanes, left, right, rows):
    size, half = left.shape
    lefts = [left] + [at.send(at.gate("left", left), dx=dx) for dx in range(1, at.xs)]
    rows = rows[:1] + [at.send(at.gate("rows", row), dx=dx) for dx, row in enumerate(rows[1:], 1)]
    rights = [right] + [at.send(at.gate("right", right), db=db) for db in range(1, at.bs)]
    at.token("left", lefts[1:])
    at.token("rows", rows[1:])
    at.token("right", rights[1:])

    def pick(db):
        outs = [like(at.xs * size, half + CORES * lanes)]
        refs = [at.gate("pick", left), *lefts[1:], *rows]
        return call(functools.partial(pick_kernel, db), outs, [], *refs)[0]

    held = {}

    def keep(k, place, row):
        held[place] = (k, row)

    arrays = [pick(0), join(at.gate("join_right", right), *rights[1:])]
    for dx in range(at.xs):
        keep(0, (-dx % at.xs, 0, 0), dx * size)
    for db in range(at.bs):
        keep(1, (0, -db % at.bs, 1), db * size)
    for db in range(1, at.bs):
        arrays.append(at.send(pick(db), db=db))
        for dx in range(at.xs):
            keep(len(arrays) - 1, (-dx % at.xs, -db % at.bs, 0), dx * size)
    for dx in range(1, at.xs):
        arrays.append(at.send(arrays[1], dx=dx))
        for db in range(at.bs):
            keep(len(arrays) - 1, (-dx % at.xs, -db % at.bs, 1), db * size)
    at.token("left2", arrays[2 : 1 + at.bs])
    at.token("right2", arrays[1 + at.bs :])
    return arrays, held


def grad_kernel(held, xs, bs, lanes, dcore, n_arrays, place, *refs):
    arrays, (*outs, left, right, product, sums_ref) = refs[:n_arrays], refs[n_arrays:]
    a, b, x, core = (place[i] for i in range(4))
    size, width = left.shape[0] // (xs * bs), right.shape[1]
    half, count, group = width // 2, lanes // LINE, bs * lanes
    for n, (dx, db) in enumerate((dx, db) for db in range(bs) for dx in range(xs)):
        rows = slice(n * size, (n + 1) * size)
        k, row = held[dx, db, 0]
        right[rows, :half] = arrays[k][row : row + size, :half]
        start = half + dcore * lanes
        left[rows, :] = arrays[k][row : row + size, start : start + lanes]
        k, row = held[dx, db, 1]
        right[rows, half:] = arrays[k][row : row + size, :]
    product[:, :width] = dot(left[...], right[...], ((0,), (0,)))
    total = jnp.sum(right[...].astype(F32), 0, keepdims=True)
    sums_ref[...] = jnp.broadcast_to(total, sums_ref.shape)
    row = x * CORES + lax.rem(core + dcore, CORES)
    own = sums_ref[0:1, pl.ds(pl.multiple_of(row * group, group), group)]
    at_row = lax.broadcasted_iota(jnp.int32, (lanes, group), 0)
    at_lane = lax.broadcasted_iota(jnp.int32, (lanes, group), 1)
    source = (at_row // count) * (bs * count) + b * count + at_row % count
    column = jnp.sum(jnp.where(at_lane == source, own, 0.0), 1, keepdims=True)
    product[:, width:] = jnp.broadcast_to(column, (lanes, 128))
    if dcore:
        [out] = outs
        out[:, :width] = product[:, :width].astype(LOW)
        out[:, width:] = two_parts(product[:, width:])
        return
    got, outs = outs[0], outs[1:]
    for out, flip in zip(outs, ORDER):
        rows = pl.ds(pl.multiple_of((a ^ flip) * count, count), count)
        tail = got[rows, width:].astype(F32)
        tail = product[rows, width:] + (tail[:, 0:1] + tail[:, 1:2])
        out[:, :width] = (product[rows, :width] + got[rows, :width].astype(F32)).astype(out.dtype)
        out[:, width : width + 128] = two_parts(tail) if out.dtype == LOW else tail


def two_parts(value):
    high = value.astype(LOW)
    rest = (value - high.astype(F32)).astype(LOW)
    lane = lax.broadcasted_iota(jnp.int32, value.shape, 1)
    return jnp.where(lane == 0, high.astype(F32), jnp.where(lane == 1, rest.astype(F32), 0.0)).astype(LOW)


def fold_kernel(kept, got, far):
    width = kept.shape[1] - 128
    tail = got[:, width : width + 128].astype(F32)
    far[:, :width] = (kept[:, :width] + got[:, :width].astype(F32)).astype(LOW)
    far[:, width : width + 128] = two_parts(kept[:, width : width + 128] + (tail[:, 0:1] + tail[:, 1:2]))


def last_fold_kernel(kept, *refs):
    *arrived, weight_out, bias_out = refs
    width = weight_out.shape[1]
    total, tail = kept[:, :width], kept[:, width : width + 128]
    for got in arrived:
        total = total + got[:, :width].astype(F32)
        rest = got[:, width : width + 128].astype(F32)
        tail = tail + (rest[:, 0:1] + rest[:, 1:2])
    weight_out[...] = total
    bias_out[...] = jnp.transpose(tail)[0:1, :]


def far_kernel(kept, got, far):
    far[...] = (kept[...] + got[...].astype(F32)).astype(LOW)


def shards(node_feats, block_vals, block_cols, block_counts, self_weight, weight, bias, out_grad):
    at = Place()
    size, width = node_feats.shape
    own_rows = weight.shape[0]
    lanes = LINE * own_rows
    aligned = own_rows * at.bs == 128
    halves = line_weight(at, weight) if aligned else []
    first, *chips = at.chips
    own = {first: node_feats}
    for dx, db in chips:
        own[dx, db] = at.send(at.gate("features", node_feats), dx=-dx, db=-db)
    at.token("features", [own[chip] for chip in chips])
    ops = operator(at, block_vals, block_cols, block_counts, self_weight, size)
    others = at.token("features_join", join(at.gate("features_join", own[chips[0]]), *[own[chip] for chip in chips[1:]]))
    across = [at.send(node_feats, dcore=1), at.send(others, dcore=1)]
    across[0] = at.gate("sums", across[0])
    total, kept, to_near, to_last = at.token("sums", sums(at, ops, own, across))
    got = at.token("sum_last", at.send(to_last, flip=1))
    [far] = at.token("sum_fold", call(far_kernel, [like(size, width)], [], kept, at.gate("sum_fold", got)))
    near = at.token("sum_near", at.send(at.gate("sum_near", to_near), flip=1))
    far = at.token("sum_far", at.send(far, flip=2))

    if not aligned:
        return plain_rest(at, ops, total + near.astype(F32) + far.astype(F32), weight, bias, out_grad)
    halves = [at.gate("weight_halves", half) for half in halves]
    arrays, held = gathered_halves(at, halves)
    arrays, held = both_cores(at, arrays, held)
    widths = [end - start for start, end in bounds(width)]
    own_held = {at: where for at, where in held.items() if not at[0]}
    count = len(arrays) // 2
    turned, pre = call(
        functools.partial(first_dense_kernel, own_held, at.xs, at.bs, lanes, count),
        [like(size, width), like(size, width, kind=F32)],
        [pltpu.VMEM((size, width), F32)],
        at.numbers,
        *arrays[:count],
        total,
        near,
        far,
        bias[None, :],
        numbers=1,
    )
    activations, left, right, *backs = call(
        functools.partial(dense_kernel, held, at.xs, at.bs, lanes, len(arrays)),
        [like(size, width)] + [like(size, width // 2)] * 2 + [like(size, wide) for wide in widths],
        [pltpu.VMEM((size, width), LOW)],
        at.numbers,
        *arrays,
        turned,
        pre,
        out_grad,
        numbers=1,
    )

    fars = [at.token("far0", at.send(backs[0], flip=2))]
    kernel = functools.partial(rows_kernel, at.xs, at.bs, lanes)
    rows = list(call(kernel, [like(size, at.bs * CORES * lanes)] * at.xs, [], at.gate("rows_kernel", turned)))
    arrays, held = spread(at, lanes, left, right, rows)
    nears = [at.token("near0", at.send(join(at.gate("near0", backs[0]), fars[0]), flip=1))]
    for k in range(1, CHUNKS):
        fars.append(at.token("far1", at.send(at.gate("far1", backs[k]), flip=2)))
        nears.append(at.token("near1", at.send(join(at.gate("near1", backs[k]), fars[k]), flip=1)))

    across0 = feat_across(at, ops, "0", backs[0], fars[0], nears[0])
    wide = width + 128
    scratch = [
        pltpu.VMEM((size * len(at.chips), lanes), LOW),
        pltpu.VMEM((size * len(at.chips), width), LOW),
        pltpu.VMEM((lanes, wide), F32),
        pltpu.VMEM((8, width), F32),
    ]
    kernel = functools.partial(grad_kernel, held, at.xs, at.bs, lanes)
    first = at.gate("grad_across", arrays[0])
    [across] = call(
        functools.partial(kernel, 1, len(arrays)), [like(lanes, wide)], scratch, at.numbers, first, *arrays[1:], numbers=1
    )
    at.token("grad_across", across)
    got = at.token("grad_core", at.send(across, dcore=1))
    feat = feat_own(at, ops, "0", across0, backs[0], fars[0], nears[0])
    outs = [like(own_rows, wide, kind=F32)] * 2 + [like(own_rows, width + NEAR_PAD), like(own_rows, width + LAST_PAD)]
    total, kept, to_near, to_last = call(
        functools.partial(kernel, 0, len(arrays)),
        outs,
        scratch,
        at.numbers,
        *arrays,
        at.gate("grad", got),
        numbers=1,
    )
    at.token("grad", to_last)
    got = at.token("grad_last", at.send(to_last, flip=1))
    [sent] = call(fold_kernel, [like(own_rows, width + FAR_PAD)], [], kept, at.gate("grad_fold", got))
    at.token("grad_fold", sent)
    far = at.token("grad_far", at.send(at.gate("grad_far", sent), flip=2))
    for k in range(1, CHUNKS):
        across1 = feat_across(at, ops, "1", backs[k], fars[k], nears[k])
        feat = feat + feat_own(at, ops, "1", across1, backs[k], fars[k], nears[k])
    near = at.token("grad_near", at.send(at.gate("grad_near", to_near), flip=1))
    per = len(at.chips)
    [done] = call(sum_kernel, [like(size, widths[0], kind=F32)], [], at.gate("add", feat[0]), *feat[1:per])
    [feat_grad] = call(last_sum_kernel, [like(size, width, kind=F32)], [], done, *feat[per:])
    at.token("add", feat_grad)
    outs = [like(own_rows, width, kind=F32), like(1, own_rows, kind=F32)]
    weight_grad, bias_grad = call(last_fold_kernel, outs, [], at.gate("last", total), near, far)
    return activations, feat_grad, weight_grad, bias_grad[0]


def feat_across(at, ops, name, *lines):
    size, chunk = lines[0].shape
    rows = len(at.chips) * size
    *lines, near = lines
    lines = [*lines, at.gate("across" + name, near)]
    kernel = functools.partial(back_kernel, len(ops))
    [across] = call(kernel, [like(rows, chunk)], [], *[pair[1] for pair in ops], *lines)
    at.token("across" + name, across)
    return at.token("core" + name, at.send(across, dcore=1))


def feat_own(at, ops, name, got, *lines):
    size, chunk = lines[0].shape
    kernel = functools.partial(back_kernel, len(ops))
    outs = [like(size, chunk, kind=F32)] + [like(size, chunk)] * (len(at.chips) - 1)
    parts = call(kernel, outs, [], *[pair[0] for pair in ops], *lines, at.gate("own" + name, got))
    at.token("own" + name, parts)
    sent = [at.send(part, dx=dx, db=db) for part, (dx, db) in zip(parts[1:], at.chips[1:])]
    at.token("feat" + name, sent)
    return [parts[0]] + sent


def plain_rest(at, ops, agg, weight, bias, out_grad):
    size, width = out_grad.shape
    own_rows = weight.shape[0]
    lanes = LINE * own_rows
    agg = agg.astype(LOW)
    whole_weight = lax.all_gather(weight, AXES, axis=0, tiled=True)
    pre = dot(agg, whole_weight, ((1,), (0,))) + bias[None, :]
    phi = 0.5 * (1.0 + lax.erf(pre * (0.5**0.5)))
    activations = (pre * phi).astype(LOW)
    slope = phi + pre * (jnp.exp(-0.5 * pre * pre) * 0.3989422804014327)
    pre_low = (out_grad.astype(F32) * slope).astype(LOW)
    feat = []
    for start, end in bounds(width):
        back = dot(pre_low, whole_weight[start:end], ((1,), (1,))).astype(LOW)
        far = at.send(back, flip=2)
        lines = [back, far, at.send(join(back, far), flip=1)]
        feat = feat + feat_own(at, ops, "", feat_across(at, ops, "", *lines), *lines)
    [feat_grad] = call(functools.partial(add_up_kernel, CHUNKS), [like(size, width, kind=F32)], [], *feat)

    groups = agg.reshape(size, at.rows, LINE, at.bs, own_rows)
    groups = jnp.concatenate([lax.dynamic_slice_in_dim(groups, at.a ^ flip, 1, 2) for flip in ORDER], 2)
    messages = []
    for dx, db in at.chips:
        dest_x = (at.x + dx) % at.xs
        wide = one_of(groups, (at.b + db) % at.bs, 3)
        picked = [
            one_of(wide, dest_x * CORES + (at.core + dcore) % CORES, 1).reshape(size, lanes) for dcore in range(CORES)
        ]
        message = jnp.concatenate([pre_low] + picked, 1)
        messages.append(at.send(message, dx=dx, db=db) if dx or db else message)
    own = jnp.concatenate(messages)
    other = at.send(own, dcore=1)
    weight_part = dot(own[:, width : width + lanes], own[:, :width], ((0,), (0,)))
    weight_part = weight_part + dot(other[:, width + lanes :], other[:, :width], ((0,), (0,)))
    bias_part = jnp.sum(own[:, :width].astype(F32), 0) + jnp.sum(other[:, :width].astype(F32), 0)
    bias_part = one_of(one_of(bias_part.reshape(at.rows, LINE, at.bs, own_rows), at.row, 0), at.b, 1)
    bias_part = jnp.concatenate([one_of(bias_part, at.a ^ flip, 0) for flip in ORDER])
    near = at.send(weight_part[2 * own_rows :].astype(LOW), flip=1).astype(F32)
    kept = weight_part[: 2 * own_rows] + near
    far = at.send(kept[own_rows:].astype(LOW), flip=2).astype(F32)
    near_bias = at.send(bias_part[2 * own_rows :], flip=1)
    kept_bias = bias_part[: 2 * own_rows] + near_bias
    bias_grad = kept_bias[:own_rows] + at.send(kept_bias[own_rows:], flip=2)
    return activations, feat_grad, kept[:own_rows] + far, bias_grad


def solution(mesh):
    placed = (
        P(("col", "row"), None),
        P("row", "col"),
        P("col", "row"),
        P("col", "row"),
        P("row"),
        P(("row", "col"), None),
        P(),
        P(("row", "col"), None),
    )
    return jax.shard_map(
        shards,
        mesh=mesh,
        in_specs=placed,
        out_specs=(
            P(("row", "col"), None),
            P(("col", "row"), None),
            P(("row", "col"), None),
            P(("row", "col")),
        ),
        check_vma=False,
    )
```
